32 devices in a mesh: section: 2 (over x), batch: 16 (over z, y, core).
Axes of the slice: x: 2, y: 2, z: 4, core: 2. Of those that a mesh axis runs over, the one named last changes fastest.
Arguments:
- tokens: bfloat16 [16384, 768], P('batch'), may hold values from -6 to 6
- cotangent: bfloat16 [16384, 768], P('batch'), may hold values from -6 to 6
- loss_weight: float32 [32], P('batch'), may hold values from 0.25 to 4
- timesteps: int32 [32], P('batch'), may hold values from 0 to 999, as said below
- owners: int32 [2, 432], P('section'), may hold values from 0 to 15, as said below
- master: float32 [2, 496, 32, 768], P('section', 'batch'), as said below
- first_moment: float32 [2, 496, 32, 768], P('section', 'batch'), as said below
- second_moment: float32 [2, 496, 32, 768], P('section', 'batch'), as said below
Outputs:
- block_outputs: bfloat16 [2, 16384, 768], P('section', 'batch')
- input_grads: float32 [2, 16384, 768], P('section', 'batch')
- master_new: float32 [2, 496, 32, 768], P('section', 'batch')
- first_new: float32 [2, 496, 32, 768], P('section', 'batch')
- second_new: float32 [2, 496, 32, 768], P('section', 'batch')
- copies_new: bfloat16 [2, 496, 32, 768], P('section', 'batch')
The draws below stay inside these ranges and needn't reach their ends.
Inputs may be any that keep to these rules, and one draw needn't show every extreme that they name: `timesteps`: larger timestep indices are more common. `owners`: each owner holds at most 31 panels of a block; in every section some owner holds exactly 31. `master`: owner o's k-th panel (in panel order) sits in slot o * 31 + k; slots that hold no panel are zero. `first_moment`: same slots as master; slots that hold no panel are zero. `second_moment`: same slots as master; positive where a panel sits, zero elsewhere.
All inputs are finite; a program needn't handle non-finite values.
Results may differ from the reference program's by a relative error of at most 0.017.
The reference program's roundings to bfloat16 on the way count: a program that leaves them out, or rounds other values in their place, can miss the bound.
Values may be sent and summed in bfloat16 or wider, within the bound.
No kernel may reach another device: no remote copies, remote signals or barrier semaphores. Data moves between devices by JAX's collectives and lax.ppermute only.
A program may use at most 448 MiB of HBM per device.

```python
import math
import jax
import jax.numpy as jnp
from jax import lax

D = 768
HEADS = 12
HEAD_DIM = 64
FF = 3072
CLIP_LEN = 512
STEP = 10
PANEL_ROWS = 32
SHEET_ROWS = 13824
PANELS = 432
SLOTS = 31
SAMPLES = 32
TOKENS = 16384
N_BATCH = 16


def panel_slots_drawn(owner_row, slot_count, owner_count):
    onehot = (owner_row[:, None] == jnp.arange(owner_count, dtype=jnp.int32)[None, :]).astype(jnp.int32)
    earlier = jnp.cumsum(onehot, axis=0) - onehot
    rank_in_owner = jnp.sum(earlier * onehot, axis=1)
    return (owner_row * slot_count + rank_in_owner).astype(jnp.int32)


def owner_layout(key):
    owner_rows = []
    for section_number in range(2):
        section_key = jax.random.fold_in(key, 71 + section_number)
        key_full, key_order, key_assign = jax.random.split(section_key, 3)
        slot_total = N_BATCH * SLOTS
        full_owner = jax.random.randint(key_full, (), 0, N_BATCH)
        slot_order = jax.random.permutation(key_order, slot_total).astype(jnp.int32)
        slot_ids = jnp.arange(slot_total, dtype=jnp.int32)
        priority = jnp.where(slot_ids // SLOTS == full_owner, -1, slot_order)
        chosen = jnp.argsort(priority, stable=True)[:PANELS].astype(jnp.int32)
        assign = jax.random.permutation(key_assign, PANELS)
        owner_rows.append((chosen[assign] // SLOTS).astype(jnp.int32))
    return jnp.stack(owner_rows)


def kind_factors(table):
    starts = jnp.arange(PANELS, dtype=jnp.int32) * PANEL_ROWS
    bounds = (3 * D, 4 * D, 4 * D + FF, 4 * D + 2 * FF)
    result = jnp.full((PANELS,), table[4], jnp.float32)
    for number in (3, 2, 1, 0):
        result = jnp.where(starts < bounds[number], jnp.float32(table[number]), result)
    return result


def slot_values(owner_rows, table):
    section_rows = []
    for section_number in range(2):
        slot_index = panel_slots_drawn(owner_rows[section_number], SLOTS, N_BATCH)
        section_rows.append(jnp.zeros((N_BATCH * SLOTS,), jnp.float32).at[slot_index].set(kind_factors(table)))
    return jnp.stack(section_rows)


def grad_table():
    root_tokens = float(TOKENS) ** 0.5
    return (0.05 * root_tokens, 0.1 * root_tokens, 0.2 * root_tokens, 0.2 * root_tokens, 0.2 * root_tokens)


def draw_timesteps(key, part):
    key_one, key_two = jax.random.split(jax.random.fold_in(key, 3))
    first_draw = jax.random.randint(key_one, (SAMPLES,), 0, 1000)
    second_draw = jax.random.randint(key_two, (SAMPLES,), 0, 1000)
    return jnp.maximum(first_draw, second_draw).astype(jnp.int32)


def draw_owners(key, part):
    return owner_layout(key)


def draw_master(key, part):
    owner_rows = owner_layout(key)
    table = (D ** (-0.5), 0.4 * (CLIP_LEN / D) ** 0.5, D ** (-0.5), FF ** (-0.5), 2.0 * D ** (-0.5))
    scales = slot_values(owner_rows, table)
    noise_key = jax.random.fold_in(key, 13)
    full_shape = (2, N_BATCH * SLOTS, PANEL_ROWS, D)
    noise_draw = jax.random.normal(noise_key, full_shape, jnp.float32)
    return noise_draw * scales[:, :, None, None]


def draw_first_moment(key, part):
    owner_rows = owner_layout(key)
    scales = slot_values(owner_rows, grad_table())
    noise_key = jax.random.fold_in(key, 17)
    full_shape = (2, N_BATCH * SLOTS, PANEL_ROWS, D)
    noise_draw = jax.random.normal(noise_key, full_shape, jnp.float32)
    return noise_draw * scales[:, :, None, None]


def draw_second_moment(key, part):
    owner_rows = owner_layout(key)
    scales = slot_values(owner_rows, grad_table())
    noise_key = jax.random.fold_in(key, 19)
    full_shape = (2, N_BATCH * SLOTS, PANEL_ROWS, D)
    factor = jnp.exp(jax.random.uniform(noise_key, full_shape, jnp.float32, 0.0, math.log(4.0)))
    return factor * (scales * scales)[:, :, None, None]


def block_scale(own_key, shape, cuts, low, largest):
    factor_of = 1.0
    for position, blocks in cuts:
        heights = jax.random.uniform(jax.random.fold_in(jax.random.fold_in(own_key, 6), position), (blocks,), jnp.float32, low / len(cuts), largest / len(cuts))
        factor_of = factor_of * jnp.repeat(jnp.exp(heights), shape[position] // blocks).reshape((-1,) + (1,) * (len(shape) - 1 - position))
    return factor_of


def normal_values(stream_key, extent, scale, limit, shards=(), kind=jnp.bfloat16):
    loudness = block_scale(stream_key, extent, shards, -0.22, 0.18) if shards else 1.0
    drawn = jax.random.normal(stream_key, extent, jnp.float32) * scale * loudness
    return jnp.minimum(jnp.maximum(drawn, -limit), limit).astype(kind)


def setup_inputs(seed: int = 0) -> dict:
    splits = jax.random.split(jax.random.key(seed), 9)
    return {
        "tokens": normal_values(splits[0], (TOKENS, D), 1.0, 6.0, ((0, 16),)),
        "cotangent": normal_values(splits[1], (TOKENS, D), 1.0, 6.0, ((0, 16),)),
        "loss_weight": jnp.clip(jnp.exp(math.log(4.0) - 2.7725887 * jax.random.uniform(splits[2], (SAMPLES,), jnp.float32) ** block_scale(splits[2], (SAMPLES,), ((0, 16),), -0.2, 0.2)), 0.25, 4.0),
        "timesteps": draw_timesteps(jax.random.fold_in(splits[8], 71), 0),
        "owners": draw_owners(jax.random.fold_in(splits[8], 71), 0),
        "master": draw_master(jax.random.fold_in(splits[8], 71), 0),
        "first_moment": draw_first_moment(jax.random.fold_in(splits[8], 71), 0),
        "second_moment": draw_second_moment(jax.random.fold_in(splits[8], 71), 0),
    }


@jax.custom_vjp
def low(v):
    return lax.optimization_barrier(v.astype(jnp.bfloat16)).astype(jnp.float32)

@jax.custom_vjp
def low_back(v):
    return v

def low_keep(v):
    return (low(v), None)

def low_pass(kept, grad):
    return (grad,)

def back_keep(v):
    return (v, None)

def back_low(kept, grad):
    return (low(grad),)
low.defvjp(low_keep, low_pass)
low_back.defvjp(back_keep, back_low)
highest = lax.Precision.HIGHEST
norm_eps = 1e-06
adam_eps = 1e-08
learn_rate = 0.03
decay_rate = 0.1
beta_one = 0.5
beta_two = 0.5

def both_ways(values_in):
    return low(low_back(values_in))

def panel_slots(owner_row, slot_count, owner_count):
    onehot = (owner_row[:, None] == jnp.arange(owner_count, dtype=jnp.int32)[None, :]).astype(jnp.int32)
    earlier = jnp.cumsum(onehot, axis=0) - onehot
    rank_in_owner = lax.optimization_barrier(jnp.sum(earlier * onehot, axis=1))
    return (owner_row * slot_count + rank_in_owner).astype(jnp.int32)

def time_features(steps_in):
    half_width = D // 2
    freqs = jnp.exp(-math.log(10000.0) * jnp.arange(half_width, dtype=jnp.float32) / half_width)
    angles = steps_in.astype(jnp.float32)[:, None] * freqs[None, :]
    return jnp.concatenate([jnp.cos(angles), jnp.sin(angles)], axis=1)

def layer_norm(values_in):
    average = lax.optimization_barrier(jnp.mean(values_in, axis=-1, keepdims=True))
    centred = values_in - average
    variance = lax.optimization_barrier(jnp.mean(centred * centred, axis=-1, keepdims=True))
    return centred * lax.rsqrt(variance + norm_eps)

def split_sheet(sheet):
    return (sheet[:3 * D], sheet[3 * D:4 * D], sheet[4 * D:4 * D + FF], sheet[4 * D + FF:4 * D + 2 * FF], sheet[4 * D + 2 * FF:])

def clip_forward(inputs, cond_row, weights):
    qkv_weight, proj_weight, up_weight, down_weight, mod_weight = weights
    modulation = low_back(jnp.dot(cond_row, mod_weight.T, precision=highest))
    pieces = jnp.split(modulation, 6)
    hidden_one = low(layer_norm(inputs) * (1.0 + pieces[1]) + pieces[0])
    projected = both_ways(jnp.dot(hidden_one, qkv_weight.T, precision=highest))
    query_heads = projected[:, :D].reshape(CLIP_LEN, HEADS, HEAD_DIM)
    key_heads = projected[:, D:2 * D].reshape(CLIP_LEN, HEADS, HEAD_DIM)
    value_heads = projected[:, 2 * D:].reshape(CLIP_LEN, HEADS, HEAD_DIM)
    scores = low_back(jnp.einsum('qhd,khd->hqk', query_heads, key_heads, precision=highest)) * HEAD_DIM ** (-0.5)
    soft_weights = jax.nn.softmax(scores, axis=-1)
    mixed = both_ways(jnp.einsum('hqk,khd->qhd', low(soft_weights), value_heads, precision=highest)).reshape(CLIP_LEN, D)
    branch = low_back(jnp.dot(mixed, proj_weight.T, precision=highest))
    middle = inputs + pieces[2] * branch
    hidden_two = low(layer_norm(middle) * (1.0 + pieces[4]) + pieces[3])
    upward = low_back(jnp.dot(hidden_two, up_weight.T, precision=highest))
    activated = low(jax.nn.gelu(upward))
    branch_two = low_back(jnp.dot(activated, down_weight, precision=highest))
    return middle + pieces[5] * branch_two

def run_block(inputs, sheet, conditions):
    weights = split_sheet(low(sheet))

    def one_clip(clip_pair):
        return clip_forward(clip_pair[0], clip_pair[1], weights)
    return lax.map(jax.checkpoint(one_clip), (inputs, conditions))

def adam_update(master_row, first_row, second_row, grad_sheet, slot_index):
    grad_slots = jnp.zeros_like(master_row).at[slot_index].set(grad_sheet.reshape(PANELS, PANEL_ROWS, D))
    first_next = beta_one * first_row + (1.0 - beta_one) * grad_slots
    second_next = beta_two * second_row + (1.0 - beta_two) * grad_slots * grad_slots
    first_hat = first_next / (1.0 - beta_one ** STEP)
    second_hat = second_next / (1.0 - beta_two ** STEP)
    master_next = master_row - learn_rate * (first_hat / (jnp.sqrt(second_hat) + adam_eps) + decay_rate * master_row)
    return (master_next, first_next, second_next)

def reference(tokens, cotangent, loss_weight, timesteps, owners, master, first_moment, second_moment):
    conditions = low(jax.nn.silu(time_features(timesteps)))
    slot_lists = []
    sheets = []
    for section_number in range(2):
        slot_index = panel_slots(owners[section_number], SLOTS, N_BATCH)
        slot_lists.append(slot_index)
        sheets.append(master[section_number][slot_index].reshape(SHEET_ROWS, D))
    start_rows = tokens.astype(jnp.float32).reshape(SAMPLES, CLIP_LEN, D)
    middle_raw, back_zero = jax.vjp(lambda inputs, sheet: run_block(inputs, sheet, conditions), start_rows, sheets[0])
    middle = low(middle_raw)
    final_rows, back_one = jax.vjp(lambda inputs, sheet: run_block(inputs, sheet, conditions), middle, sheets[1])
    upstream = cotangent.astype(jnp.float32).reshape(SAMPLES, CLIP_LEN, D) * loss_weight[:, None, None]
    grad_middle, grad_sheet_one = back_one(upstream)
    grad_start, grad_sheet_zero = back_zero(low(grad_middle))
    grad_sheets = (grad_sheet_zero, grad_sheet_one)
    results = [adam_update(master[number], first_moment[number], second_moment[number], grad_sheets[number], slot_lists[number]) for number in range(2)]
    master_next = jnp.stack([results[0][0], results[1][0]])
    first_next = jnp.stack([results[0][1], results[1][1]])
    second_next = jnp.stack([results[0][2], results[1][2]])
    block_outputs = jnp.stack([middle.reshape(TOKENS, D), final_rows.reshape(TOKENS, D)]).astype(jnp.bfloat16)
    input_grads = jnp.stack([grad_start.reshape(TOKENS, D), grad_middle.reshape(TOKENS, D)])
    return (block_outputs, input_grads, master_next, first_next, second_next, master_next.astype(jnp.bfloat16))
```

```python
import functools
import math

import jax
import jax.numpy as jnp
from jax import lax
from jax.experimental import pallas as pl
from jax.experimental.pallas import tpu as pltpu
from jax.sharding import PartitionSpec as P

D = 768
HEADS = 12
HEAD_DIM = 64
FF = 3072
STEP = 10
QKV_END = 3 * D
PROJ_END = 4 * D
UP_END = 4 * D + FF
DOWN_END = 4 * D + 2 * FF

norm_eps = 1e-06
adam_eps = 1e-08
learn_rate = 0.03
decay_rate = 0.1
beta_one = 0.5
beta_two = 0.5

bf16 = jnp.bfloat16
f32 = jnp.float32
VMEM_LIMIT = 60 * 1024 * 1024
ROWS = 128
GELU_C = math.sqrt(2.0 / math.pi)


def dot_nn(a, b):
    return lax.dot_general(a, b, (((1,), (0,)), ((), ())), preferred_element_type=f32)


def dot_nt(a, b):
    return lax.dot_general(a, b, (((1,), (1,)), ((), ())), preferred_element_type=f32)


def dot_tn(a, b):
    return lax.dot_general(a, b, (((0,), (0,)), ((), ())), preferred_element_type=f32)


def start(src, dst, sem):
    copy = pltpu.make_async_copy(src, dst, sem)
    copy.start()
    return copy


def norm(values):
    average = jnp.mean(values, axis=-1, keepdims=True)
    centred = values - average
    variance = jnp.mean(centred * centred, axis=-1, keepdims=True)
    inverse = lax.rsqrt(variance + norm_eps)
    return centred * inverse, inverse


def norm_back(grad, values, scale_row):
    normed, inverse = norm(values)
    dn = grad * (1.0 + scale_row)
    mean_one = jnp.mean(dn, axis=-1, keepdims=True)
    mean_two = jnp.mean(dn * normed, axis=-1, keepdims=True)
    dx = inverse * (dn - mean_one - normed * mean_two)
    return dx, jnp.sum(grad, axis=0, keepdims=True), jnp.sum(grad * normed, axis=0, keepdims=True)


def gelu(u):
    return 0.5 * u * (1.0 + jnp.tanh(GELU_C * (u + 0.044715 * (u * u * u))))


def gelu_slope(u):
    square = u * u
    t = jnp.tanh(GELU_C * (u + 0.044715 * (square * u)))
    return 0.5 * (1.0 + t) + 0.5 * u * (1.0 - t * t) * (GELU_C * (1.0 + 3.0 * 0.044715 * square))


def assemble_kernel(panels, first_size, index_ref, *refs):
    sources, sheet, sem = refs[:-2], refs[-2], refs[-1]
    rows = sheet.shape[1]

    @pl.loop(0, panels)
    def _(p):
        where = index_ref[p]
        if len(sources) == 1:
            pltpu.make_async_copy(sources[0].at[where], sheet.at[p], sem).start()
        else:

            @pl.when(where < first_size)
            def _():
                pltpu.make_async_copy(sources[0].at[where], sheet.at[p], sem).start()

            @pl.when(where >= first_size)
            def _():
                pltpu.make_async_copy(sources[1].at[where - first_size], sheet.at[p], sem).start()

    pltpu.make_async_copy(sheet, sheet, sem).wait()


def assemble(index, sources, panels):
    first_size = sources[0].shape[0]
    rows = sources[0].shape[1]
    return pl.pallas_call(
        functools.partial(assemble_kernel, panels, first_size),
        out_shape=jax.ShapeDtypeStruct((panels, rows, D), bf16),
        in_specs=[pl.BlockSpec(memory_space=pltpu.SMEM)]
        + [pl.BlockSpec(memory_space=pl.ANY)] * len(sources),
        out_specs=pl.BlockSpec(memory_space=pl.ANY),
        scratch_shapes=[pltpu.SemaphoreType.DMA],
        cost_estimate=pl.CostEstimate(flops=0, bytes_accessed=4 * panels * rows * D, transcendentals=0),
        name="assemble",
    )(index, *sources)


FORWARD_STATE = ("xin", "h1", "qkv", "lse", "o", "a", "x1", "h2", "u", "z", "b")


def forward_shapes(length):
    return {
        "xin": ((length, D), bf16),
        "h1": ((length, D), bf16),
        "qkv": ((length, 3 * D), bf16),
        "lse": ((16, length), f32),
        "o": ((length, D), bf16),
        "a": ((length, D), bf16),
        "x1": ((length, D), f32),
        "h2": ((length, D), bf16),
        "u": ((length, FF), f32),
        "z": ((length, FF), bf16),
        "b": ((length, D), bf16),
    }


def forward_kernel(want, clip, x_offset, length, chained, *refs):
    n_state = len(FORWARD_STATE)
    sec_ref, mod_ref, x_hbm, w_hbm = refs[:4]
    refs = refs[4 + 1 :]
    refs = refs[(n_state if chained else 0) + (1 if clip or chained else 0) :]
    state = dict(zip(FORWARD_STATE, refs[:n_state]))
    outs_hbm, sent_hbm = refs[n_state : n_state + 2]
    scratch = refs[n_state + 2 :]
    w, keep, out_v, acc, score, soft, lse_cols, w_sem, x_sem, o_sem = (
        scratch[0],
        dict(zip(FORWARD_STATE, scratch[1 : 1 + n_state])),
        *scratch[1 + n_state :],
    )

    @pl.when(sec_ref[0] == want)
    def _():
        get_x = start(x_hbm.at[pl.ds(x_offset, length)], keep["xin"], x_sem)
        bounds = (0, QKV_END, PROJ_END, UP_END, DOWN_END)
        get_w = [
            start(
                w_hbm.at[pl.ds(bounds[i], bounds[i + 1] - bounds[i])],
                w.at[pl.ds(bounds[i], bounds[i + 1] - bounds[i])],
                w_sem.at[i],
            )
            for i in range(4)
        ]
        row = lambda n: mod_ref[clip, n : n + 1, :]
        put = []

        def save(name):
            put.append(start(keep[name], state[name], o_sem.at[len(put)]))

        get_x.wait()
        save("xin")
        for r in range(0, length, ROWS):
            block = pl.ds(r, ROWS)
            normed, _ = norm(keep["xin"][block, :].astype(f32))
            keep["h1"][block, :] = (normed * (1.0 + row(1)) + row(0)).astype(bf16)
        save("h1")
        get_w[0].wait()
        for n in range(3):
            part = dot_nt(keep["h1"][...], w[n * D : (n + 1) * D, :])
            keep["qkv"][:, n * D : (n + 1) * D] = part.astype(bf16)
        save("qkv")
        lse_cols[...] = jnp.zeros_like(lse_cols)
        low_lanes = lax.broadcasted_iota(jnp.int32, (1, 128), 1) < HEAD_DIM

        @pl.loop(0, HEADS // 2)
        def _(pair):
            at = lambda n: pl.ds(pl.multiple_of(n * D + pair * 128, 128), 128)
            q = keep["qkv"][:, at(0)] * jnp.asarray(HEAD_DIM ** (-0.5), bf16)
            k = keep["qkv"][:, at(1)]
            v = keep["qkv"][:, at(2)]
            mixed = []
            for h in range(2):
                qh = jnp.where(low_lanes if h == 0 else ~low_lanes, q, jnp.zeros_like(q))
                score[h, :, :] = dot_nt(qh, k)
                lane = lax.broadcasted_iota(jnp.int32, (1, 128), 1) == pair * 2 + h
                for r in range(0, length, ROWS):
                    block = pl.ds(r, ROWS)
                    s = score[h, block, :]
                    top = jnp.max(s, axis=-1, keepdims=True)
                    e = jnp.exp(s - top)
                    total = jnp.sum(e, axis=-1, keepdims=True)
                    soft[h, block, :] = (e * (1.0 / total)).astype(bf16)
                    lse_cols[block, :] = jnp.where(lane, top + jnp.log(total), lse_cols[block, :])
                mixed.append(dot_nn(soft[h, :, :], v))
            keep["o"][:, at(0)] = jnp.where(low_lanes, mixed[0], mixed[1]).astype(bf16)

        keep["lse"][...] = lse_cols[...].T[:16, :]
        save("lse")
        save("o")
        get_w[1].wait()
        acc[...] = dot_nt(keep["o"][...], w[QKV_END:PROJ_END, :])
        for r in range(0, length, ROWS):
            block = pl.ds(r, ROWS)
            branch = acc[block, :]
            keep["a"][block, :] = branch.astype(bf16)
            middle = keep["xin"][block, :].astype(f32) + row(2) * branch
            keep["x1"][block, :] = middle
            normed, _ = norm(middle)
            keep["h2"][block, :] = (normed * (1.0 + row(4)) + row(3)).astype(bf16)
        save("a")
        save("x1")
        save("h2")
        get_w[2].wait()
        get_w[3].wait()
        tile = D
        for n in range(FF // tile):
            span = slice(n * tile, (n + 1) * tile)
            keep["u"][:, span] = dot_nt(keep["h2"][...], w[PROJ_END + n * tile : PROJ_END + (n + 1) * tile, :])
            for r in range(0, length, ROWS):
                block = pl.ds(r, ROWS)
                keep["z"][block, span] = gelu(keep["u"][block, span]).astype(bf16)
            part = dot_nn(keep["z"][:, span], w[UP_END + n * tile : UP_END + (n + 1) * tile, :])
            if n:
                acc[...] += part
            else:
                acc[...] = part
        save("u")
        save("z")
        for r in range(0, length, ROWS):
            block = pl.ds(r, ROWS)
            branch = acc[block, :]
            keep["b"][block, :] = branch.astype(bf16)
            out_v[block, :] = (keep["x1"][block, :] + row(5) * branch).astype(bf16)
        save("b")
        put.append(start(out_v, outs_hbm.at[pl.ds(clip * length, length)], o_sem.at[len(put)]))
        put.append(start(out_v, sent_hbm, o_sem.at[len(put)]))
        for copy in put:
            copy.wait()


def forward(want, clip, clips, length, section, mod, x, x_offset, sheet, token, state, outs):
    shapes = forward_shapes(length)
    any_spec = pl.BlockSpec(memory_space=pl.ANY)
    chained = state is not None
    operands = [section, mod, x, sheet, token]
    aliases = {}
    if chained:
        for n, name in enumerate(FORWARD_STATE):
            aliases[len(operands)] = n
            operands.append(state[name])
    if outs is not None:
        aliases[len(operands)] = len(FORWARD_STATE)
        operands.append(outs)
    out_shape = [jax.ShapeDtypeStruct(*shapes[name]) for name in FORWARD_STATE]
    out_shape += [
        jax.ShapeDtypeStruct((clips * length, D), bf16),
        jax.ShapeDtypeStruct((length, D), bf16),
    ]
    results = pl.pallas_call(
        functools.partial(forward_kernel, want, clip, x_offset, length, chained),
        out_shape=out_shape,
        in_specs=[
            pl.BlockSpec(memory_space=pltpu.SMEM),
            pl.BlockSpec(memory_space=pltpu.VMEM),
        ]
        + [any_spec] * (len(operands) - 2),
        out_specs=[any_spec] * len(out_shape),
        scratch_shapes=[pltpu.VMEM((DOWN_END, D), bf16)]
        + [pltpu.VMEM(*shapes[name]) for name in FORWARD_STATE]
        + [
            pltpu.VMEM((length, D), bf16),
            pltpu.VMEM((length, D), f32),
            pltpu.VMEM((2, length, length), f32),
            pltpu.VMEM((2, length, length), bf16),
            pltpu.VMEM((length, 128), f32),
            pltpu.SemaphoreType.DMA((4,)),
            pltpu.SemaphoreType.DMA,
            pltpu.SemaphoreType.DMA((len(FORWARD_STATE) + 2,)),
        ],
        input_output_aliases=aliases,
        compiler_params=pltpu.CompilerParams(vmem_limit_bytes=VMEM_LIMIT),
        cost_estimate=pl.CostEstimate(
            flops=2 * length * DOWN_END * D * 2, bytes_accessed=20 << 20, transcendentals=length * length * HEADS
        ),
        name=f"block_forward_{want}_{clip}",
    )(*operands)
    return dict(zip(FORWARD_STATE, results)), results[-2], results[-1]


BACK_NEEDS = ("xin", "qkv", "lse", "a", "x1", "u", "b")
BACK_STATE = ("db", "du", "da", "dqkv", "dmod")


def back_shapes(length):
    return {
        "db": ((length, D), bf16),
        "du": ((length, FF), bf16),
        "da": ((length, D), bf16),
        "dqkv": ((length, 3 * D), bf16),
        "dmod": ((6, D), f32),
    }


def back_kernel(want, clip, g_offset, length, chained, *refs):
    n_need, n_state = len(BACK_NEEDS), len(BACK_STATE)
    sec_ref, loss_ref, mod_ref, g_hbm, w_hbm = refs[:5]
    needs = dict(zip(BACK_NEEDS, refs[5 : 5 + n_need]))
    refs = refs[5 + n_need :]
    refs = refs[(n_state if chained else 0) + (1 if clip or chained else 0) :]
    state = dict(zip(BACK_STATE, refs[:n_state]))
    gin_hbm, sent_hbm, token_hbm = refs[n_state : n_state + 3]
    scratch = refs[n_state + 3 :]
    w = scratch[0]
    have = dict(zip(BACK_NEEDS, scratch[1 : 1 + n_need]))
    keep = dict(zip(BACK_STATE, scratch[1 + n_need : 1 + n_need + n_state]))
    g_low, dx1, acc, do, sent_v, w_sem, g_sem, h_sem, o_sem = scratch[1 + n_need + n_state :]

    @pl.when(sec_ref[0] == want)
    def _():
        get_g = start(g_hbm.at[pl.ds(g_offset, length)], g_low, g_sem)
        get = {}
        bounds = (0, QKV_END, PROJ_END, UP_END, DOWN_END)

        def fetch(name):
            get[name] = start(needs[name], have[name], h_sem.at[BACK_NEEDS.index(name)])

        def fetch_w(i):
            span = pl.ds(bounds[i], bounds[i + 1] - bounds[i])
            get[i] = start(w_hbm.at[span], w.at[span], w_sem.at[i])

        fetch("b")
        fetch_w(3)
        fetch("u")
        fetch_w(2)
        fetch("x1")
        fetch("a")
        fetch_w(1)
        fetch("qkv")
        fetch("lse")
        fetch_w(0)
        fetch("xin")
        row = lambda n: mod_ref[clip, n : n + 1, :]
        put = []

        def save(name):
            put.append(start(keep[name], state[name], o_sem.at[len(put)]))

        get_g.wait()
        get["b"].wait()
        gate_two = jnp.zeros((1, D), f32)
        for r in range(0, length, ROWS):
            block = pl.ds(r, ROWS)
            g = g_low[block, :].astype(f32)
            if want:
                g = g * loss_ref[clip]
            dx1[block, :] = g
            keep["db"][block, :] = (row(5) * g).astype(bf16)
            gate_two += jnp.sum(g * have["b"][block, :].astype(f32), axis=0, keepdims=True)
        keep["dmod"][5:6, :] = gate_two
        save("db")
        get[3].wait()
        get["u"].wait()
        get[2].wait()
        tile = D
        for n in range(FF // tile):
            span = slice(n * tile, (n + 1) * tile)
            dz = dot_nt(keep["db"][...], w[UP_END + n * tile : UP_END + (n + 1) * tile, :])
            keep["du"][:, span] = (dz * gelu_slope(have["u"][:, span])).astype(bf16)
            part = dot_nn(keep["du"][:, span], w[PROJ_END + n * tile : PROJ_END + (n + 1) * tile, :])
            if n:
                acc[...] += part
            else:
                acc[...] = part
        save("du")
        get["x1"].wait()
        get["a"].wait()
        shift_two = jnp.zeros((1, D), f32)
        scale_two = jnp.zeros((1, D), f32)
        gate_one = jnp.zeros((1, D), f32)
        for r in range(0, length, ROWS):
            block = pl.ds(r, ROWS)
            dx, shift_part, scale_part = norm_back(acc[block, :], have["x1"][block, :], row(4))
            total = dx1[block, :] + dx
            dx1[block, :] = total
            shift_two += shift_part
            scale_two += scale_part
            gate_one += jnp.sum(total * have["a"][block, :].astype(f32), axis=0, keepdims=True)
            keep["da"][block, :] = (row(2) * total).astype(bf16)
        keep["dmod"][2:3, :] = gate_one
        keep["dmod"][3:4, :] = shift_two
        keep["dmod"][4:5, :] = scale_two
        save("da")
        get[1].wait()
        do[...] = dot_nn(keep["da"][...], w[QKV_END:PROJ_END, :]).astype(bf16)
        get["qkv"].wait()
        get["lse"].wait()
        low_lanes = lax.broadcasted_iota(jnp.int32, (1, 128), 1) < HEAD_DIM
        scale = HEAD_DIM ** (-0.5)

        @pl.loop(0, HEADS // 2)
        def _(pair):
            at = lambda n: pl.ds(pl.multiple_of(n * D + pair * 128, 128), 128)
            q = have["qkv"][:, at(0)]
            k = have["qkv"][:, at(1)]
            v = have["qkv"][:, at(2)]
            dop = do[:, at(0)]
            zero = jnp.zeros_like(q)
            dq = dk = dv = None
            for h in range(2):
                lanes = low_lanes if h == 0 else ~low_lanes
                qh = jnp.where(lanes, q, zero)
                kh = jnp.where(lanes, k, zero)
                doh = jnp.where(lanes, dop, zero)
                st = dot_nt(k, qh * jnp.asarray(scale, bf16))
                pt = jnp.exp(st - have["lse"][pl.ds(pair * 2 + h, 1), :])
                dpt = dot_nt(v, doh)
                dv_part = dot_nn(pt.astype(bf16), doh)
                inner = jnp.sum(dpt * pt, axis=0, keepdims=True)
                drt = (pt * (dpt - inner) * scale).astype(bf16)
                dk_part = dot_nn(drt, qh)
                dq_part = dot_tn(drt, kh)
                dq = dq_part if h == 0 else dq + dq_part
                dk = dk_part if h == 0 else dk + dk_part
                dv = dv_part if h == 0 else dv + dv_part
            keep["dqkv"][:, at(0)] = dq.astype(bf16)
            keep["dqkv"][:, at(1)] = dk.astype(bf16)
            keep["dqkv"][:, at(2)] = dv.astype(bf16)

        save("dqkv")
        get[0].wait()
        acc[...] = dot_nn(keep["dqkv"][...], w[0:QKV_END, :])
        get["xin"].wait()
        shift_one = jnp.zeros((1, D), f32)
        scale_one = jnp.zeros((1, D), f32)
        for r in range(0, length, ROWS):
            block = pl.ds(r, ROWS)
            dx, shift_part, scale_part = norm_back(acc[block, :], have["xin"][block, :].astype(f32), row(1))
            total = dx1[block, :] + dx
            dx1[block, :] = total
            sent_v[block, :] = total.astype(bf16)
            shift_one += shift_part
            scale_one += scale_part
        keep["dmod"][0:1, :] = shift_one
        keep["dmod"][1:2, :] = scale_one
        save("dmod")
        put.append(start(sent_v, sent_hbm, o_sem.at[len(put)]))
        put.append(start(dx1, gin_hbm.at[pl.ds(clip * length, length)], o_sem.at[len(put)]))
        for copy in put:
            copy.wait()


def back(want, clip, clips, length, section, loss_weight, mod, g, g_offset, sheet, kept, state, gin):
    shapes, kept_shapes = back_shapes(length), forward_shapes(length)
    any_spec = pl.BlockSpec(memory_space=pl.ANY)
    chained = state is not None
    operands = [section, loss_weight, mod, g, sheet] + [kept[name] for name in BACK_NEEDS]
    aliases = {}
    if chained:
        for n, name in enumerate(BACK_STATE):
            aliases[len(operands)] = n
            operands.append(state[name])
    if gin is not None:
        aliases[len(operands)] = len(BACK_STATE)
        operands.append(gin)
    out_shape = [jax.ShapeDtypeStruct(*shapes[name]) for name in BACK_STATE]
    out_shape += [
        jax.ShapeDtypeStruct((clips * length, D), f32),
        jax.ShapeDtypeStruct((length, D), bf16),
        jax.ShapeDtypeStruct((8, 128), f32),
    ]
    results = pl.pallas_call(
        functools.partial(back_kernel, want, clip, g_offset, length, chained),
        out_shape=out_shape,
        in_specs=[
            pl.BlockSpec(memory_space=pltpu.SMEM),
            pl.BlockSpec(memory_space=pltpu.SMEM),
            pl.BlockSpec(memory_space=pltpu.VMEM),
        ]
        + [any_spec] * (len(operands) - 3),
        out_specs=[any_spec] * len(out_shape),
        scratch_shapes=[pltpu.VMEM((DOWN_END, D), bf16)]
        + [pltpu.VMEM(*kept_shapes[name]) for name in BACK_NEEDS]
        + [pltpu.VMEM(*shapes[name]) for name in BACK_STATE]
        + [
            pltpu.VMEM((length, D), bf16),
            pltpu.VMEM((length, D), f32),
            pltpu.VMEM((length, D), f32),
            pltpu.VMEM((length, D), bf16),
            pltpu.VMEM((length, D), bf16),
            pltpu.SemaphoreType.DMA((4,)),
            pltpu.SemaphoreType.DMA,
            pltpu.SemaphoreType.DMA((len(BACK_NEEDS),)),
            pltpu.SemaphoreType.DMA((len(BACK_STATE) + 2,)),
        ],
        input_output_aliases=aliases,
        compiler_params=pltpu.CompilerParams(vmem_limit_bytes=VMEM_LIMIT),
        cost_estimate=pl.CostEstimate(
            flops=2 * length * DOWN_END * D * 2, bytes_accessed=30 << 20, transcendentals=length * length * HEADS
        ),
        name=f"block_back_{want}_{clip}",
    )(*operands)
    return dict(zip(BACK_STATE, results)), results[-3], results[-2], results[-1]


GRAD_PAIRS = (("z", "db", UP_END), ("du", "h2", PROJ_END), ("da", "o", QKV_END), ("dqkv", "h1", 0))


def grads_kernel(clips, length, panel_rows, first_size, two, dest_ref, *refs):
    count = 2 * len(GRAD_PAIRS) * clips
    sources = refs[:count]
    outs = refs[count : count + (2 if two else 1)]
    scratch = refs[count + (2 if two else 1) :]
    values = scratch[: 2 * len(GRAD_PAIRS)]
    tile_v, in_sem, out_sem = scratch[2 * len(GRAD_PAIRS) :]
    get = []
    for n in range(2 * len(GRAD_PAIRS)):
        get.append(
            [
                start(sources[n * clips + c], values[n].at[pl.ds(c * length, length)], in_sem.at[n, c])
                for c in range(clips)
            ]
        )
    tiles = []
    for n, (left, right, base) in enumerate(GRAD_PAIRS):
        width = values[2 * n].shape[1]
        tiles += [(n, column, base + column) for column in range(0, width, D)]
    per_tile = D // panel_rows
    seen = set()

    def drain(slot):
        pltpu.make_async_copy(outs[0].at[pl.ds(0, per_tile)], tile_v.at[slot], out_sem.at[slot]).wait()

    for t, (n, column, first_row) in enumerate(tiles):
        slot = t % 2
        if n not in seen:
            seen.add(n)
            for copy in get[2 * n] + get[2 * n + 1]:
                copy.wait()
        if t >= 2:
            drain(slot)
        part = dot_tn(values[2 * n][:, column : column + D], values[2 * n + 1][...])
        tile_v[slot, :, :, :] = part.astype(bf16).reshape(per_tile, panel_rows, D)

        @pl.loop(0, per_tile)
        def _(p):
            where = dest_ref[first_row // panel_rows + p]
            if not two:
                pltpu.make_async_copy(tile_v.at[slot, p], outs[0].at[where], out_sem.at[slot]).start()
            else:

                @pl.when(where < first_size)
                def _():
                    pltpu.make_async_copy(tile_v.at[slot, p], outs[0].at[where], out_sem.at[slot]).start()

                @pl.when(where >= first_size)
                def _():
                    pltpu.make_async_copy(
                        tile_v.at[slot, p], outs[1].at[where - first_size], out_sem.at[slot]
                    ).start()

    drain(0)
    drain(1)


def weight_grads(dest, kept, backs, length, panel_rows, sizes):
    clips = len(kept)
    any_spec = pl.BlockSpec(memory_space=pl.ANY)
    operands, scratch = [], []
    for left, right, _ in GRAD_PAIRS:
        for name in (left, right):
            arrays = [{**kept[c], **backs[c]}[name] for c in range(clips)]
            operands += arrays
            scratch.append(pltpu.VMEM((clips * length, arrays[0].shape[1]), bf16))
    two = len(sizes) == 2
    return pl.pallas_call(
        functools.partial(grads_kernel, clips, length, panel_rows, sizes[0], two),
        out_shape=[jax.ShapeDtypeStruct((size, panel_rows, D), bf16) for size in sizes],
        in_specs=[pl.BlockSpec(memory_space=pltpu.SMEM)] + [any_spec] * len(operands),
        out_specs=[any_spec] * len(sizes),
        scratch_shapes=scratch
        + [
            pltpu.VMEM((2, D // panel_rows, panel_rows, D), bf16),
            pltpu.SemaphoreType.DMA((2 * len(GRAD_PAIRS), clips)),
            pltpu.SemaphoreType.DMA((2,)),
        ],
        compiler_params=pltpu.CompilerParams(vmem_limit_bytes=VMEM_LIMIT),
        cost_estimate=pl.CostEstimate(
            flops=2 * clips * length * DOWN_END * D, bytes_accessed=40 << 20, transcendentals=0
        ),
        name="weight_grads",
    )(dest, *operands)


def adam_kernel(kind_ref, row_ref, master, first, second, sums, dmod, cond, master_o, first_o, second_o, copy_o):
    slot = pl.program_id(0)
    rows = master.shape[1]
    kind = kind_ref[slot]

    def update(grad):
        first_next = beta_one * first[0] + (1.0 - beta_one) * grad
        second_next = beta_two * second[0] + (1.0 - beta_two) * grad * grad
        first_hat = first_next / (1.0 - beta_one**STEP)
        second_hat = second_next / (1.0 - beta_two**STEP)
        value = master[0] - learn_rate * (
            first_hat / (jnp.sqrt(second_hat) + adam_eps) + decay_rate * master[0]
        )
        master_o[0] = value
        first_o[0] = first_next
        second_o[0] = second_next
        copy_o[0] = value.astype(bf16)

    @pl.when(kind == 0)
    def _():
        update(jnp.zeros((rows, D), f32))

    @pl.when(kind == 1)
    def _():
        update(sums[0].astype(f32))

    @pl.when(kind == 2)
    def _():
        at = pl.multiple_of(row_ref[slot], rows)
        update(dot_nn(dmod[pl.ds(at, rows), :], cond[...]))


def adam(kind, row, master, first, second, sums, dmod, cond):
    slots, rows = master.shape[0], master.shape[1]
    block = pl.BlockSpec((1, rows, D), lambda s, *_: (s, 0, 0))
    return pl.pallas_call(
        adam_kernel,
        grid_spec=pltpu.PrefetchScalarGridSpec(
            num_scalar_prefetch=2,
            grid=(slots,),
            in_specs=[block] * 4
            + [
                pl.BlockSpec(dmod.shape, lambda s, *_: (0, 0)),
                pl.BlockSpec(cond.shape, lambda s, *_: (0, 0)),
            ],
            out_specs=[block] * 4,
        ),
        out_shape=[jax.ShapeDtypeStruct(master.shape, f32)] * 3 + [jax.ShapeDtypeStruct(master.shape, bf16)],
        cost_estimate=pl.CostEstimate(flops=0, bytes_accessed=slots * rows * D * 30, transcendentals=0),
        name="adam",
    )(kind, row, master, first, second, sums, dmod, cond)


def time_features(steps_in):
    half_width = D // 2
    freqs = jnp.exp(-math.log(10000.0) * jnp.arange(half_width, dtype=f32) / half_width)
    angles = steps_in.astype(f32)[:, None] * freqs[None, :]
    return jnp.concatenate([jnp.cos(angles), jnp.sin(angles)], axis=1)


def body(tokens, cotangent, loss_weight, timesteps, owners, master, first_moment, second_moment):
    section_index = lax.axis_index("section")
    me = lax.axis_index("batch")
    owner_total = lax.axis_size("batch")
    slots, panel_rows = master.shape[1], master.shape[2]
    clips = timesteps.shape[0]
    length = tokens.shape[0] // clips
    owner = owners[0]
    panels = owner.shape[0]
    moved = DOWN_END // panel_rows
    cap = min(slots, max(4, (slots * 27 + 30) // 31))
    section = jnp.reshape(section_index, (1,)).astype(jnp.int32)

    number = jnp.arange(panels, dtype=jnp.int32)
    same = (owner[:, None] == owner[None, :]) & (number[None, :] < number[:, None])
    rank = jnp.sum(same.astype(jnp.int32), axis=1)
    first_size = owner_total * cap
    place = jnp.where(
        rank < cap, owner * cap + rank, first_size + owner * (slots - cap) + rank - cap
    )[:moved]
    mine = (owner[None, :] == me) & (
        rank[None, :] == jnp.arange(slots, dtype=jnp.int32)[:, None]
    )
    slot_panel = jnp.sum(jnp.where(mine, number[None, :] + 1, 0), axis=1) - 1
    kind = jnp.where(slot_panel < 0, 0, jnp.where(slot_panel < moved, 1, 2)).astype(jnp.int32)
    mod_row = jnp.where(kind == 2, (slot_panel - moved) * panel_rows, 0).astype(jnp.int32)

    low = master[0].astype(bf16)
    sources = [lax.all_gather(low[:cap], "batch", axis=0, tiled=True)]
    over = None
    if cap < slots:
        beyond = jnp.max(jnp.where(number < moved, rank, 0)) >= cap
        over = lax.pmax(beyond.astype(f32), "section") > 0.5
        rest = low[cap:]
        rest_shape = (owner_total * (slots - cap), panel_rows, D)
        sources.append(
            lax.cond(
                over,
                lambda part: lax.all_gather(part, "batch", axis=0, tiled=True),
                lambda part: jnp.zeros(rest_shape, bf16),
                rest,
            )
        )
    sheet = assemble(place, sources, moved).reshape(moved * panel_rows, D)

    all_steps = lax.all_gather(timesteps, "batch", axis=0, tiled=True)
    cond = jax.nn.silu(time_features(all_steps)).astype(bf16)
    clip_total = cond.shape[0]
    share = jnp.einsum("cd,sd->cs", cond, low.reshape(slots * panel_rows, D), preferred_element_type=f32)
    share = lax.all_to_all(
        share.reshape(owner_total, clips, slots * panel_rows), "batch", split_axis=0, concat_axis=0, tiled=True
    )
    share = share.reshape(owner_total, clips, slots, panel_rows).transpose(1, 0, 2, 3)
    share = share.reshape(clips, owner_total * slots, panel_rows)
    pick = (
        (owner * slots + rank)[moved:, None] == jnp.arange(owner_total * slots, dtype=jnp.int32)[None, :]
    ).astype(f32)
    mod = jnp.einsum("ps,csr->cpr", pick, share, precision=lax.Precision.HIGHEST)
    mod = mod.reshape(clips, 6, D)

    run = functools.partial
    fwd = run(forward, clips=clips, length=length, section=section, mod=mod, sheet=sheet)
    bwd = run(back, clips=clips, length=length, section=section, loss_weight=loss_weight, mod=mod, sheet=sheet)
    token = jnp.zeros((8, 128), f32)
    kept, sent, outs = [None] * clips, [None] * clips, None
    for c in range(clips):
        kept[c], outs, sent[c] = fwd(0, c, x=tokens, x_offset=c * length, token=token, state=None, outs=outs)
    received = [lax.ppermute(rows, "section", [(0, 1)]) for rows in sent]
    backs, gin = [None] * clips, None
    for c in range(clips):
        kept[c], outs, _ = fwd(1, c, x=received[c], x_offset=0, token=token, state=kept[c], outs=outs)
        backs[c], gin, sent[c], token = bwd(1, c, g=cotangent, g_offset=c * length, kept=kept[c], state=None, gin=gin)
    received = [lax.ppermute(rows, "section", [(1, 0)]) for rows in sent]
    for c in range(clips):
        backs[c], gin, _, token = bwd(0, c, g=received[c], g_offset=0, kept=kept[c], state=backs[c], gin=gin)

    sizes = [first_size] + ([owner_total * (slots - cap)] if cap < slots else [])
    grads = weight_grads(place, kept, backs, length, panel_rows, sizes)
    sums = lax.psum_scatter(grads[0], "batch", scatter_dimension=0, tiled=True)
    if cap < slots:
        more = lax.cond(
            over,
            lambda part: lax.psum_scatter(part, "batch", scatter_dimension=0, tiled=True),
            lambda part: jnp.zeros((slots - cap, panel_rows, D), bf16),
            grads[1],
        )
        sums = jnp.concatenate([sums, more], axis=0)
    dmod = jnp.stack([b["dmod"] for b in backs]).reshape(clips, 6 * D).astype(bf16)
    dmod = lax.all_gather(dmod, "batch", axis=0, tiled=True).T
    results = adam(kind, mod_row, master[0], first_moment[0], second_moment[0], sums, dmod, cond)
    return (outs[None], gin[None], *(r[None] for r in results))


def solution(mesh):
    placed = (
        P("batch", None),
        P("batch", None),
        P("batch"),
        P("batch"),
        P("section", None),
        P("section", "batch", None, None),
        P("section", "batch", None, None),
        P("section", "batch", None, None),
    )
    return jax.shard_map(
        body,
        mesh=mesh,
        in_specs=placed,
        out_specs=(
            P("section", "batch", None),
            P("section", "batch", None),
            P("section", "batch", None, None),
            P("section", "batch", None, None),
            P("section", "batch", None, None),
            P("section", "batch", None, None),
        ),
        check_vma=False,
    )
```

```python
import functools
import math

import jax
import jax.numpy as jnp
from jax import lax
from jax.experimental import pallas as pl
from jax.experimental.pallas import tpu as pltpu
from jax.sharding import PartitionSpec as P

D = 768
HEADS = 12
HEAD_DIM = 64
FF = 3072
STEP = 10
QKV_END = 3 * D
PROJ_END = 4 * D
UP_END = 4 * D + FF
DOWN_END = 4 * D + 2 * FF

norm_eps = 1e-06
adam_eps = 1e-08
learn_rate = 0.03
decay_rate = 0.1
beta_one = 0.5
beta_two = 0.5

bf16 = jnp.bfloat16
f32 = jnp.float32
VMEM_LIMIT = 60 * 1024 * 1024
ROWS = 128
GELU_C = math.sqrt(2.0 / math.pi)


def dot_nn(a, b):
    return lax.dot_general(a, b, (((1,), (0,)), ((), ())), preferred_element_type=f32)


def dot_nt(a, b):
    return lax.dot_general(a, b, (((1,), (1,)), ((), ())), preferred_element_type=f32)


def dot_tn(a, b):
    return lax.dot_general(a, b, (((0,), (0,)), ((), ())), preferred_element_type=f32)


def start(src, dst, sem):
    copy = pltpu.make_async_copy(src, dst, sem)
    copy.start()
    return copy


def norm(values):
    average = jnp.mean(values, axis=-1, keepdims=True)
    centred = values - average
    variance = jnp.mean(centred * centred, axis=-1, keepdims=True)
    inverse = lax.rsqrt(variance + norm_eps)
    return centred * inverse, inverse


def norm_back(grad, values, scale_row):
    normed, inverse = norm(values)
    dn = grad * (1.0 + scale_row)
    mean_one = jnp.mean(dn, axis=-1, keepdims=True)
    mean_two = jnp.mean(dn * normed, axis=-1, keepdims=True)
    dx = inverse * (dn - mean_one - normed * mean_two)
    return dx, jnp.sum(grad, axis=0, keepdims=True), jnp.sum(grad * normed, axis=0, keepdims=True)


def gelu(u):
    return 0.5 * u * (1.0 + jnp.tanh(GELU_C * (u + 0.044715 * (u * u * u))))


def gelu_slope(u):
    square = u * u
    t = jnp.tanh(GELU_C * (u + 0.044715 * (square * u)))
    return 0.5 * (1.0 + t) + 0.5 * u * (1.0 - t * t) * (GELU_C * (1.0 + 3.0 * 0.044715 * square))


PARTS = 4


def assemble_kernel(panels, first_size, index_ref, *refs):
    sources, sheet, held, in_sem, out_sem = refs[:-4], refs[-4], refs[-3], refs[-2], refs[-1]
    size = panels // PARTS
    for part in range(PARTS):

        @pl.loop(part * size, (part + 1) * size)
        def _(p):
            where = index_ref[p]
            if len(sources) == 1:
                pltpu.make_async_copy(sources[0].at[where], held.at[p], in_sem.at[part]).start()
            else:

                @pl.when(where < first_size)
                def _():
                    pltpu.make_async_copy(sources[0].at[where], held.at[p], in_sem.at[part]).start()

                @pl.when(where >= first_size)
                def _():
                    pltpu.make_async_copy(sources[1].at[where - first_size], held.at[p], in_sem.at[part]).start()

    for part in range(PARTS):
        span = pl.ds(part * size, size)
        pltpu.make_async_copy(sheet.at[span], held.at[span], in_sem.at[part]).wait()
        pltpu.make_async_copy(held.at[span], sheet.at[span], out_sem.at[part]).start()
    for part in range(PARTS):
        span = pl.ds(part * size, size)
        pltpu.make_async_copy(held.at[span], sheet.at[span], out_sem.at[part]).wait()


def assemble(index, sources, panels):
    first_size = sources[0].shape[0]
    rows = sources[0].shape[1]
    return pl.pallas_call(
        functools.partial(assemble_kernel, panels, first_size),
        out_shape=jax.ShapeDtypeStruct((panels, rows, D), bf16),
        in_specs=[pl.BlockSpec(memory_space=pltpu.SMEM)]
        + [pl.BlockSpec(memory_space=pl.ANY)] * len(sources),
        out_specs=pl.BlockSpec(memory_space=pl.ANY),
        scratch_shapes=[
            pltpu.VMEM((panels, rows, D), bf16),
            pltpu.SemaphoreType.DMA((PARTS,)),
            pltpu.SemaphoreType.DMA((PARTS,)),
        ],
        compiler_params=pltpu.CompilerParams(vmem_limit_bytes=VMEM_LIMIT),
        cost_estimate=pl.CostEstimate(flops=0, bytes_accessed=4 * panels * rows * D, transcendentals=0),
        name="assemble",
    )(index, *sources)


FORWARD_STATE = ("xin", "h1", "qkv", "lse", "o", "a", "x1", "h2", "u", "z", "b")


def forward_shapes(length):
    return {
        "xin": ((length, D), bf16),
        "h1": ((length, D), bf16),
        "qkv": ((length, 3 * D), bf16),
        "lse": ((16, length), f32),
        "o": ((length, D), bf16),
        "a": ((length, D), bf16),
        "x1": ((length, D), f32),
        "h2": ((length, D), bf16),
        "u": ((length, FF), f32),
        "z": ((length, FF), bf16),
        "b": ((length, D), bf16),
    }


def forward_kernel(want, clip, x_offset, length, chained, *refs):
    n_state = len(FORWARD_STATE)
    sec_ref, mod_ref, x_hbm, w_hbm = refs[:4]
    refs = refs[4 + 1 :]
    refs = refs[(n_state if chained else 0) + (1 if clip or chained else 0) :]
    state = dict(zip(FORWARD_STATE, refs[:n_state]))
    outs_hbm, sent_hbm = refs[n_state : n_state + 2]
    scratch = refs[n_state + 2 :]
    w, keep, out_v, acc, score, soft, lse_cols, w_sem, x_sem, o_sem = (
        scratch[0],
        dict(zip(FORWARD_STATE, scratch[1 : 1 + n_state])),
        *scratch[1 + n_state :],
    )

    @pl.when(sec_ref[0] == want)
    def _():
        get_x = start(x_hbm.at[pl.ds(x_offset, length)], keep["xin"], x_sem)
        bounds = (0, QKV_END, PROJ_END, UP_END, DOWN_END)
        get_w = [
            start(
                w_hbm.at[pl.ds(bounds[i], bounds[i + 1] - bounds[i])],
                w.at[pl.ds(bounds[i], bounds[i + 1] - bounds[i])],
                w_sem.at[i],
            )
            for i in range(4)
        ]
        row = lambda n: mod_ref[clip, n : n + 1, :]
        put = []

        def save(name):
            put.append(start(keep[name], state[name], o_sem.at[len(put)]))

        get_x.wait()
        save("xin")
        for r in range(0, length, ROWS):
            block = pl.ds(r, ROWS)
            normed, _ = norm(keep["xin"][block, :].astype(f32))
            keep["h1"][block, :] = (normed * (1.0 + row(1)) + row(0)).astype(bf16)
        save("h1")
        get_w[0].wait()
        for n in range(3):
            part = dot_nt(keep["h1"][...], w[n * D : (n + 1) * D, :])
            keep["qkv"][:, n * D : (n + 1) * D] = part.astype(bf16)
        save("qkv")
        lse_cols[...] = jnp.zeros_like(lse_cols)
        low_lanes = lax.broadcasted_iota(jnp.int32, (1, 128), 1) < HEAD_DIM

        @pl.loop(0, HEADS // 2)
        def _(pair):
            at = lambda n: pl.ds(pl.multiple_of(n * D + pair * 128, 128), 128)
            q = keep["qkv"][:, at(0)] * jnp.asarray(HEAD_DIM ** (-0.5), bf16)
            k = keep["qkv"][:, at(1)]
            v = keep["qkv"][:, at(2)]
            mixed = []
            for h in range(2):
                qh = jnp.where(low_lanes if h == 0 else ~low_lanes, q, jnp.zeros_like(q))
                score[h, :, :] = dot_nt(qh, k)
                lane = lax.broadcasted_iota(jnp.int32, (1, 128), 1) == pair * 2 + h
                for r in range(0, length, ROWS):
                    block = pl.ds(r, ROWS)
                    s = score[h, block, :]
                    top = jnp.max(s, axis=-1, keepdims=True)
                    e = jnp.exp(s - top)
                    total = jnp.sum(e, axis=-1, keepdims=True)
                    soft[h, block, :] = (e * (1.0 / total)).astype(bf16)
                    lse_cols[block, :] = jnp.where(lane, top + jnp.log(total), lse_cols[block, :])
                mixed.append(dot_nn(soft[h, :, :], v))
            keep["o"][:, at(0)] = jnp.where(low_lanes, mixed[0], mixed[1]).astype(bf16)

        keep["lse"][...] = lse_cols[...].T[:16, :]
        save("lse")
        save("o")
        get_w[1].wait()
        acc[...] = dot_nt(keep["o"][...], w[QKV_END:PROJ_END, :])
        for r in range(0, length, ROWS):
            block = pl.ds(r, ROWS)
            branch = acc[block, :]
            keep["a"][block, :] = branch.astype(bf16)
            middle = keep["xin"][block, :].astype(f32) + row(2) * branch
            keep["x1"][block, :] = middle
            normed, _ = norm(middle)
            keep["h2"][block, :] = (normed * (1.0 + row(4)) + row(3)).astype(bf16)
        save("a")
        save("x1")
        save("h2")
        get_w[2].wait()
        get_w[3].wait()
        tile = D
        for n in range(FF // tile):
            span = slice(n * tile, (n + 1) * tile)
            keep["u"][:, span] = dot_nt(keep["h2"][...], w[PROJ_END + n * tile : PROJ_END + (n + 1) * tile, :])
            for r in range(0, length, ROWS):
                block = pl.ds(r, ROWS)
                keep["z"][block, span] = gelu(keep["u"][block, span]).astype(bf16)
            part = dot_nn(keep["z"][:, span], w[UP_END + n * tile : UP_END + (n + 1) * tile, :])
            if n:
                acc[...] += part
            else:
                acc[...] = part
        save("u")
        save("z")
        for r in range(0, length, ROWS):
            block = pl.ds(r, ROWS)
            branch = acc[block, :]
            keep["b"][block, :] = branch.astype(bf16)
            out_v[block, :] = (keep["x1"][block, :] + row(5) * branch).astype(bf16)
        save("b")
        put.append(start(out_v, outs_hbm.at[pl.ds(clip * length, length)], o_sem.at[len(put)]))
        put.append(start(out_v, sent_hbm, o_sem.at[len(put)]))
        for copy in put:
            copy.wait()


def forward(want, clip, clips, length, section, mod, x, x_offset, sheet, token, state, outs):
    shapes = forward_shapes(length)
    any_spec = pl.BlockSpec(memory_space=pl.ANY)
    chained = state is not None
    operands = [section, mod, x, sheet, token]
    aliases = {}
    if chained:
        for n, name in enumerate(FORWARD_STATE):
            aliases[len(operands)] = n
            operands.append(state[name])
    if outs is not None:
        aliases[len(operands)] = len(FORWARD_STATE)
        operands.append(outs)
    out_shape = [jax.ShapeDtypeStruct(*shapes[name]) for name in FORWARD_STATE]
    out_shape += [
        jax.ShapeDtypeStruct((clips * length, D), bf16),
        jax.ShapeDtypeStruct((length, D), bf16),
    ]
    results = pl.pallas_call(
        functools.partial(forward_kernel, want, clip, x_offset, length, chained),
        out_shape=out_shape,
        in_specs=[
            pl.BlockSpec(memory_space=pltpu.SMEM),
            pl.BlockSpec(memory_space=pltpu.VMEM),
        ]
        + [any_spec] * (len(operands) - 2),
        out_specs=[any_spec] * len(out_shape),
        scratch_shapes=[pltpu.VMEM((DOWN_END, D), bf16)]
        + [pltpu.VMEM(*shapes[name]) for name in FORWARD_STATE]
        + [
            pltpu.VMEM((length, D), bf16),
            pltpu.VMEM((length, D), f32),
            pltpu.VMEM((2, length, length), f32),
            pltpu.VMEM((2, length, length), bf16),
            pltpu.VMEM((length, 128), f32),
            pltpu.SemaphoreType.DMA((4,)),
            pltpu.SemaphoreType.DMA,
            pltpu.SemaphoreType.DMA((len(FORWARD_STATE) + 2,)),
        ],
        input_output_aliases=aliases,
        compiler_params=pltpu.CompilerParams(vmem_limit_bytes=VMEM_LIMIT),
        cost_estimate=pl.CostEstimate(
            flops=2 * length * DOWN_END * D * 2, bytes_accessed=20 << 20, transcendentals=length * length * HEADS
        ),
        name=f"block_forward_{want}_{clip}",
    )(*operands)
    return dict(zip(FORWARD_STATE, results)), results[-2], results[-1]


FFN_NEEDS = ("b", "u", "x1", "a")
FFN_STATE = ("db", "du", "da", "dx1", "dmod_ffn")
ATT_NEEDS = ("da", "qkv", "lse", "dx1", "xin")
ATT_STATE = ("dqkv", "dmod_att")


def back_shapes(length):
    return {
        "db": ((length, D), bf16),
        "du": ((length, FF), bf16),
        "da": ((length, D), bf16),
        "dx1": ((length, D), f32),
        "dmod_ffn": ((4, D), f32),
        "dqkv": ((length, 3 * D), bf16),
        "dmod_att": ((2, D), f32),
    }


def back_ffn_kernel(want, clip, g_offset, length, chained, *refs):
    n_need, n_state = len(FFN_NEEDS), len(FFN_STATE)
    sec_ref, loss_ref, mod_ref, g_hbm, w_hbm = refs[:5]
    needs = dict(zip(FFN_NEEDS, refs[5 : 5 + n_need]))
    refs = refs[5 + n_need + (n_state if chained else 0) :]
    state = dict(zip(FFN_STATE, refs[:n_state]))
    scratch = refs[n_state:]
    w = scratch[0]
    have = dict(zip(FFN_NEEDS, scratch[1 : 1 + n_need]))
    keep = dict(zip(FFN_STATE, scratch[1 + n_need : 1 + n_need + n_state]))
    g_low, acc, w_sem, g_sem, h_sem, o_sem = scratch[1 + n_need + n_state :]

    @pl.when(sec_ref[0] == want)
    def _():
        get_g = start(g_hbm.at[pl.ds(g_offset, length)], g_low, g_sem)
        get = {}

        def fetch(name):
            get[name] = start(needs[name], have[name], h_sem.at[FFN_NEEDS.index(name)])

        fetch("b")
        get_down = start(w_hbm.at[pl.ds(UP_END, FF)], w.at[pl.ds(FF, FF)], w_sem.at[0])
        fetch("u")
        get_up = start(w_hbm.at[pl.ds(PROJ_END, FF)], w.at[pl.ds(0, FF)], w_sem.at[1])
        fetch("x1")
        fetch("a")
        row = lambda n: mod_ref[clip, n : n + 1, :]
        put = []

        def save(name):
            put.append(start(keep[name], state[name], o_sem.at[len(put)]))

        get_g.wait()
        get["b"].wait()
        dx1 = keep["dx1"]
        gate_two = jnp.zeros((1, D), f32)
        for r in range(0, length, ROWS):
            block = pl.ds(r, ROWS)
            g = g_low[block, :].astype(f32)
            if want:
                g = g * loss_ref[clip]
            dx1[block, :] = g
            keep["db"][block, :] = (row(5) * g).astype(bf16)
            gate_two += jnp.sum(g * have["b"][block, :].astype(f32), axis=0, keepdims=True)
        keep["dmod_ffn"][3:4, :] = gate_two
        save("db")
        get_down.wait()
        get["u"].wait()
        get_up.wait()
        tile = D
        for n in range(FF // tile):
            span = slice(n * tile, (n + 1) * tile)
            dz = dot_nt(keep["db"][...], w[FF + n * tile : FF + (n + 1) * tile, :])
            keep["du"][:, span] = (dz * gelu_slope(have["u"][:, span])).astype(bf16)
            part = dot_nn(keep["du"][:, span], w[n * tile : (n + 1) * tile, :])
            if n:
                acc[...] += part
            else:
                acc[...] = part
        save("du")
        get["x1"].wait()
        get["a"].wait()
        shift_two = jnp.zeros((1, D), f32)
        scale_two = jnp.zeros((1, D), f32)
        gate_one = jnp.zeros((1, D), f32)
        for r in range(0, length, ROWS):
            block = pl.ds(r, ROWS)
            dx, shift_part, scale_part = norm_back(acc[block, :], have["x1"][block, :], row(4))
            total = dx1[block, :] + dx
            dx1[block, :] = total
            shift_two += shift_part
            scale_two += scale_part
            gate_one += jnp.sum(total * have["a"][block, :].astype(f32), axis=0, keepdims=True)
            keep["da"][block, :] = (row(2) * total).astype(bf16)
        keep["dmod_ffn"][0:1, :] = gate_one
        keep["dmod_ffn"][1:2, :] = shift_two
        keep["dmod_ffn"][2:3, :] = scale_two
        save("da")
        save("dx1")
        save("dmod_ffn")
        for copy in put:
            copy.wait()


def back_att_kernel(want, clip, length, chained, *refs):
    n_need, n_state = len(ATT_NEEDS), len(ATT_STATE)
    sec_ref, mod_ref, w_hbm = refs[:3]
    needs = dict(zip(ATT_NEEDS, refs[3 : 3 + n_need]))
    refs = refs[3 + n_need + (n_state if chained else 0) + (1 if clip or chained else 0) :]
    state = dict(zip(ATT_STATE, refs[:n_state]))
    gin_hbm, sent_hbm, token_hbm = refs[n_state : n_state + 3]
    scratch = refs[n_state + 3 :]
    w = scratch[0]
    have = dict(zip(ATT_NEEDS, scratch[1 : 1 + n_need]))
    keep = dict(zip(ATT_STATE, scratch[1 + n_need : 1 + n_need + n_state]))
    acc, do, sent_v, w_sem, h_sem, o_sem = scratch[1 + n_need + n_state :]

    @pl.when(sec_ref[0] == want)
    def _():
        get = {}

        def fetch(name):
            get[name] = start(needs[name], have[name], h_sem.at[ATT_NEEDS.index(name)])

        fetch("da")
        get_proj = start(w_hbm.at[pl.ds(QKV_END, D)], w.at[pl.ds(QKV_END, D)], w_sem.at[0])
        fetch("qkv")
        fetch("lse")
        get_qkv = start(w_hbm.at[pl.ds(0, QKV_END)], w.at[pl.ds(0, QKV_END)], w_sem.at[1])
        fetch("dx1")
        fetch("xin")
        row = lambda n: mod_ref[clip, n : n + 1, :]
        put = []

        def save(name):
            put.append(start(keep[name], state[name], o_sem.at[len(put)]))

        dx1 = have["dx1"]
        get["da"].wait()
        get_proj.wait()
        do[...] = dot_nn(have["da"][...], w[QKV_END:PROJ_END, :]).astype(bf16)
        get["qkv"].wait()
        get["lse"].wait()
        low_lanes = lax.broadcasted_iota(jnp.int32, (1, 128), 1) < HEAD_DIM
        scale = HEAD_DIM ** (-0.5)

        @pl.loop(0, HEADS // 2)
        def _(pair):
            at = lambda n: pl.ds(pl.multiple_of(n * D + pair * 128, 128), 128)
            q = have["qkv"][:, at(0)]
            k = have["qkv"][:, at(1)]
            v = have["qkv"][:, at(2)]
            dop = do[:, at(0)]
            zero = jnp.zeros_like(q)
            dq = dk = dv = None
            for h in range(2):
                lanes = low_lanes if h == 0 else ~low_lanes
                qh = jnp.where(lanes, q, zero)
                kh = jnp.where(lanes, k, zero)
                doh = jnp.where(lanes, dop, zero)
                st = dot_nt(k, qh * jnp.asarray(scale, bf16))
                pt = jnp.exp(st - have["lse"][pl.ds(pair * 2 + h, 1), :])
                dpt = dot_nt(v, doh)
                dv_part = dot_nn(pt.astype(bf16), doh)
                inner = jnp.sum(dpt * pt, axis=0, keepdims=True)
                drt = (pt * (dpt - inner) * scale).astype(bf16)
                dk_part = dot_nn(drt, qh)
                dq_part = dot_tn(drt, kh)
                dq = dq_part if h == 0 else dq + dq_part
                dk = dk_part if h == 0 else dk + dk_part
                dv = dv_part if h == 0 else dv + dv_part
            keep["dqkv"][:, at(0)] = dq.astype(bf16)
            keep["dqkv"][:, at(1)] = dk.astype(bf16)
            keep["dqkv"][:, at(2)] = dv.astype(bf16)

        save("dqkv")
        get_qkv.wait()
        acc[...] = dot_nn(keep["dqkv"][...], w[0:QKV_END, :])
        get["xin"].wait()
        get["dx1"].wait()
        shift_one = jnp.zeros((1, D), f32)
        scale_one = jnp.zeros((1, D), f32)
        for r in range(0, length, ROWS):
            block = pl.ds(r, ROWS)
            dx, shift_part, scale_part = norm_back(acc[block, :], have["xin"][block, :].astype(f32), row(1))
            total = dx1[block, :] + dx
            dx1[block, :] = total
            sent_v[block, :] = total.astype(bf16)
            shift_one += shift_part
            scale_one += scale_part
        keep["dmod_att"][0:1, :] = shift_one
        keep["dmod_att"][1:2, :] = scale_one
        put.append(start(sent_v, sent_hbm, o_sem.at[len(put)]))
        save("dmod_att")
        put.append(start(dx1, gin_hbm.at[pl.ds(clip * length, length)], o_sem.at[len(put)]))
        for copy in put:
            copy.wait()


def back_ffn(want, clip, clips, length, section, loss_weight, mod, g, g_offset, sheet, kept, state):
    shapes, kept_shapes = back_shapes(length), forward_shapes(length)
    any_spec = pl.BlockSpec(memory_space=pl.ANY)
    chained = state is not None
    operands = [section, loss_weight, mod, g, sheet] + [kept[name] for name in FFN_NEEDS]
    aliases = {}
    if chained:
        for n, name in enumerate(FFN_STATE):
            aliases[len(operands)] = n
            operands.append(state[name])
    out_shape = [jax.ShapeDtypeStruct(*shapes[name]) for name in FFN_STATE]
    results = pl.pallas_call(
        functools.partial(back_ffn_kernel, want, clip, g_offset, length, chained),
        out_shape=out_shape,
        in_specs=[
            pl.BlockSpec(memory_space=pltpu.SMEM),
            pl.BlockSpec(memory_space=pltpu.SMEM),
            pl.BlockSpec(memory_space=pltpu.VMEM),
        ]
        + [any_spec] * (len(operands) - 3),
        out_specs=[any_spec] * len(out_shape),
        scratch_shapes=[pltpu.VMEM((2 * FF, D), bf16)]
        + [pltpu.VMEM(*kept_shapes[name]) for name in FFN_NEEDS]
        + [pltpu.VMEM(*shapes[name]) for name in FFN_STATE]
        + [
            pltpu.VMEM((length, D), bf16),
            pltpu.VMEM((length, D), f32),
            pltpu.SemaphoreType.DMA((2,)),
            pltpu.SemaphoreType.DMA,
            pltpu.SemaphoreType.DMA((len(FFN_NEEDS),)),
            pltpu.SemaphoreType.DMA((len(FFN_STATE),)),
        ],
        input_output_aliases=aliases,
        compiler_params=pltpu.CompilerParams(vmem_limit_bytes=VMEM_LIMIT),
        cost_estimate=pl.CostEstimate(flops=15 * 10**9, bytes_accessed=24 << 20, transcendentals=0),
        name=f"back_ffn_{want}_{clip}",
    )(*operands)
    return dict(zip(FFN_STATE, results))


def back_att(want, clip, clips, length, section, mod, sheet, kept, ffn, state, gin):
    shapes, kept_shapes = back_shapes(length), forward_shapes(length)
    every = {**kept_shapes, **shapes}
    any_spec = pl.BlockSpec(memory_space=pl.ANY)
    chained = state is not None
    operands = [section, mod, sheet] + [{**kept, **ffn}[name] for name in ATT_NEEDS]
    aliases = {}
    if chained:
        for n, name in enumerate(ATT_STATE):
            aliases[len(operands)] = n
            operands.append(state[name])
    if gin is not None:
        aliases[len(operands)] = len(ATT_STATE)
        operands.append(gin)
    out_shape = [jax.ShapeDtypeStruct(*shapes[name]) for name in ATT_STATE]
    out_shape += [
        jax.ShapeDtypeStruct((clips * length, D), f32),
        jax.ShapeDtypeStruct((length, D), bf16),
        jax.ShapeDtypeStruct((8, 128), f32),
    ]
    results = pl.pallas_call(
        functools.partial(back_att_kernel, want, clip, length, chained),
        out_shape=out_shape,
        in_specs=[
            pl.BlockSpec(memory_space=pltpu.SMEM),
            pl.BlockSpec(memory_space=pltpu.VMEM),
        ]
        + [any_spec] * (len(operands) - 2),
        out_specs=[any_spec] * len(out_shape),
        scratch_shapes=[pltpu.VMEM((PROJ_END, D), bf16)]
        + [pltpu.VMEM(*every[name]) for name in ATT_NEEDS]
        + [pltpu.VMEM(*shapes[name]) for name in ATT_STATE]
        + [
            pltpu.VMEM((length, D), f32),
            pltpu.VMEM((length, D), bf16),
            pltpu.VMEM((length, D), bf16),
            pltpu.SemaphoreType.DMA((2,)),
            pltpu.SemaphoreType.DMA((len(ATT_NEEDS),)),
            pltpu.SemaphoreType.DMA((len(ATT_STATE) + 2,)),
        ],
        input_output_aliases=aliases,
        compiler_params=pltpu.CompilerParams(vmem_limit_bytes=VMEM_LIMIT),
        cost_estimate=pl.CostEstimate(flops=20 * 10**9, bytes_accessed=16 << 20, transcendentals=0),
        name=f"back_att_{want}_{clip}",
    )(*operands)
    return dict(zip(ATT_STATE, results)), results[-3], results[-2], results[-1]


def grads_kernel(jobs, clips, length, panel_rows, own, threaded, code_ref, index_ref, *refs):
    count = 2 * len(jobs) * clips
    sources = refs[:count]
    refs = refs[count + threaded :]
    outs = refs[:own]
    scratch = refs[own:]
    values = scratch[: 2 * len(jobs)]
    tile_v, in_sem, out_sem = scratch[2 * len(jobs) :]
    get = [
        [
            start(sources[n * clips + c], values[n].at[pl.ds(c * length, length)], in_sem.at[n, c])
            for c in range(clips)
        ]
        for n in range(2 * len(jobs))
    ]
    tiles = []
    for n, (left, right, base) in enumerate(jobs):
        tiles += [(n, column, base + column) for column in range(0, values[2 * n].shape[1], D)]
    per_tile = D // panel_rows
    seen = set()

    def drain(slot):
        pltpu.make_async_copy(outs[-1].at[pl.ds(0, per_tile)], tile_v.at[slot], out_sem.at[slot]).wait()

    for t, (n, column, first_row) in enumerate(tiles):
        slot = t % 2
        if n not in seen:
            seen.add(n)
            for copy in get[2 * n] + get[2 * n + 1]:
                copy.wait()
        if t >= 2:
            drain(slot)
        part = dot_tn(values[2 * n][:, column : column + D], values[2 * n + 1][...])
        tile_v[slot, :, :, :] = part.astype(bf16).reshape(per_tile, panel_rows, D)

        @pl.loop(0, per_tile)
        def _(p):
            code = code_ref[first_row // panel_rows + p]
            where = index_ref[first_row // panel_rows + p]
            for n_out in range(own):

                @pl.when(code == n_out)
                def _():
                    pltpu.make_async_copy(tile_v.at[slot, p], outs[n_out].at[where], out_sem.at[slot]).start()

    for slot in range(min(2, len(tiles))):
        drain(slot)


def weight_grads(jobs, code, index, every, length, panel_rows, sizes, thread):
    clips = len(every)
    any_spec = pl.BlockSpec(memory_space=pl.ANY)
    operands, scratch = [code, index], []
    for left, right, _ in jobs:
        for name in (left, right):
            arrays = [every[c][name] for c in range(clips)]
            operands += arrays
            scratch.append(pltpu.VMEM((clips * length, arrays[0].shape[1]), bf16))
    aliases = {}
    for n, array in enumerate(thread):
        aliases[len(operands)] = len(sizes) - len(thread) + n
        operands.append(array)
    width = sum(s.shape[1] for s in scratch[0::2])
    return pl.pallas_call(
        functools.partial(grads_kernel, jobs, clips, length, panel_rows, len(sizes), len(thread)),
        out_shape=[jax.ShapeDtypeStruct((size, panel_rows, D), bf16) for size in sizes],
        in_specs=[pl.BlockSpec(memory_space=pltpu.SMEM)] * 2 + [any_spec] * (len(operands) - 2),
        out_specs=[any_spec] * len(sizes),
        scratch_shapes=scratch
        + [
            pltpu.VMEM((2, D // panel_rows, panel_rows, D), bf16),
            pltpu.SemaphoreType.DMA((2 * len(jobs), clips)),
            pltpu.SemaphoreType.DMA((2,)),
        ],
        input_output_aliases=aliases,
        compiler_params=pltpu.CompilerParams(vmem_limit_bytes=VMEM_LIMIT),
        cost_estimate=pl.CostEstimate(
            flops=4 * clips * length * width * D, bytes_accessed=12 << 20, transcendentals=0
        ),
        name="weight_grads_" + jobs[0][0],
    )(*operands)


GROUP = 8


def adam_kernel(n_sums, code_ref, index_ref, row_ref, master, first, second, dmod, cond, *refs):
    sums = refs[:n_sums]
    outs = refs[n_sums : n_sums + 4]
    scratch = refs[n_sums + 4 :]
    held = scratch[:3]
    made = scratch[3:7]
    grad_v, in_sem, grad_sem, out_sem = scratch[7:]
    slots, rows = master.shape[0], master.shape[1]
    groups = [(g, min(GROUP, slots - g)) for g in range(0, slots, GROUP)]
    get = [
        [start(a.at[pl.ds(g, size)], h.at[pl.ds(g, size)], in_sem.at[n, i]) for i, (a, h) in enumerate(zip((master, first, second), held))]
        for n, (g, size) in enumerate(groups)
    ]
    for n, (g, size) in enumerate(groups):

        @pl.loop(g, g + size)
        def _(slot):
            code = code_ref[slot]
            where = index_ref[slot]
            for n_sum in range(n_sums):

                @pl.when(code == n_sum)
                def _():
                    pltpu.make_async_copy(sums[n_sum].at[where], grad_v.at[slot], grad_sem.at[n]).start()

    put = []
    for n, (g, size) in enumerate(groups):
        for copy in get[n]:
            copy.wait()
        span = pl.ds(g, size)

        @pl.loop(g, g + size)
        def _(slot):
            code = code_ref[slot]

            @pl.when(code < n_sums)
            def _():
                pltpu.make_async_copy(sums[0].at[0], grad_v.at[slot], grad_sem.at[n]).wait()

        @pl.loop(g, g + size)
        def _(slot):
            code = code_ref[slot]

            def update(grad):
                first_next = beta_one * held[1][slot] + (1.0 - beta_one) * grad
                second_next = beta_two * held[2][slot] + (1.0 - beta_two) * grad * grad
                first_hat = first_next / (1.0 - beta_one**STEP)
                second_hat = second_next / (1.0 - beta_two**STEP)
                value = held[0][slot] - learn_rate * (
                    first_hat / (jnp.sqrt(second_hat) + adam_eps) + decay_rate * held[0][slot]
                )
                made[0][slot] = value
                made[1][slot] = first_next
                made[2][slot] = second_next
                made[3][slot] = value.astype(bf16)

            @pl.when(code < n_sums)
            def _():
                update(grad_v[slot].astype(f32))

            @pl.when(code == n_sums)
            def _():
                at = pl.multiple_of(row_ref[slot], rows)
                update(dot_nn(dmod[pl.ds(at, rows), :], cond[...]))

            @pl.when(code > n_sums)
            def _():
                update(jnp.zeros((rows, D), f32))

        for i in range(4):
            put.append(start(made[i].at[span], outs[i].at[span], out_sem.at[n, i]))
    for copy in put:
        copy.wait()


def adam(code, index, row, master, first, second, dmod, cond, sums):
    slots, rows = master.shape[0], master.shape[1]
    any_spec = pl.BlockSpec(memory_space=pl.ANY)
    smem, vmem = pl.BlockSpec(memory_space=pltpu.SMEM), pl.BlockSpec(memory_space=pltpu.VMEM)
    kinds = [f32, f32, f32, bf16]
    groups = -(-slots // GROUP)
    return pl.pallas_call(
        functools.partial(adam_kernel, len(sums)),
        in_specs=[smem] * 3 + [any_spec] * 3 + [vmem] * 2 + [any_spec] * len(sums),
        out_specs=[any_spec] * 4,
        out_shape=[jax.ShapeDtypeStruct(master.shape, kind) for kind in kinds],
        scratch_shapes=[pltpu.VMEM(master.shape, f32)] * 3
        + [pltpu.VMEM(master.shape, kind) for kind in kinds]
        + [
            pltpu.VMEM(master.shape, bf16),
            pltpu.SemaphoreType.DMA((groups, 3)),
            pltpu.SemaphoreType.DMA((groups,)),
            pltpu.SemaphoreType.DMA((groups, 4)),
        ],
        compiler_params=pltpu.CompilerParams(vmem_limit_bytes=VMEM_LIMIT),
        cost_estimate=pl.CostEstimate(flops=0, bytes_accessed=slots * rows * D * 30, transcendentals=0),
        name="adam",
    )(code, index, row, master, first, second, dmod, cond, *sums)


CHIPS = 8
LOOP = (0, 2, 4, 6, 7, 5, 3, 1)


def swap_cores(value):
    return lax.ppermute(value, "batch", [(d, d ^ 1) for d in range(2 * CHIPS)])


def along(value, step):
    pairs = [
        (2 * LOOP[n] + core, 2 * LOOP[(n + step) % CHIPS] + core) for n in range(CHIPS) for core in range(2)
    ]
    return lax.ppermute(value, "batch", pairs)


def ring_sum(place, mine, other):
    size = mine.shape[0] // CHIPS
    half = size // 2
    partner = swap_cores(other)

    def term(offset, low, high):
        first = ((place + offset) % CHIPS) * size + low
        return sum(
            lax.dynamic_slice_in_dim(a, first, high - low, 0).astype(f32) for a in (mine, partner)
        )

    ahead = along(term(4, 0, half).astype(bf16), 1)
    behind = along(term(-4, half, size).astype(bf16), -1)
    ahead = jnp.concatenate([(term(3, 0, half) + ahead.astype(f32)).astype(bf16), term(3, half, size).astype(bf16)])
    behind = jnp.concatenate([term(-3, 0, half).astype(bf16), (term(-3, half, size) + behind.astype(f32)).astype(bf16)])
    for hop in (2, 1):
        ahead, behind = along(ahead, 1), along(behind, -1)
        ahead = (term(hop, 0, size) + ahead.astype(f32)).astype(bf16)
        behind = (term(-hop, 0, size) + behind.astype(f32)).astype(bf16)
    ahead, behind = along(ahead, 1), along(behind, -1)
    return (term(0, 0, size) + ahead.astype(f32) + behind.astype(f32)).astype(bf16)


def time_features(steps_in):
    half_width = D // 2
    freqs = jnp.exp(-math.log(10000.0) * jnp.arange(half_width, dtype=f32) / half_width)
    angles = steps_in.astype(f32)[:, None] * freqs[None, :]
    return jnp.concatenate([jnp.cos(angles), jnp.sin(angles)], axis=1)


def body(tokens, cotangent, loss_weight, timesteps, owners, master, first_moment, second_moment):
    section_index = lax.axis_index("section")
    me = lax.axis_index("batch")
    owner_total = lax.axis_size("batch")
    slots, panel_rows = master.shape[1], master.shape[2]
    clips = timesteps.shape[0]
    length = tokens.shape[0] // clips
    owner = owners[0]
    panels = owner.shape[0]
    moved = DOWN_END // panel_rows
    cap = min(slots, max(4, (slots * 27 + 30) // 31))
    section = jnp.reshape(section_index, (1,)).astype(jnp.int32)

    number = jnp.arange(panels, dtype=jnp.int32)
    same = (owner[:, None] == owner[None, :]) & (number[None, :] < number[:, None])
    rank = jnp.sum(same.astype(jnp.int32), axis=1)
    first_size = owner_total * cap
    place = jnp.where(
        rank < cap, owner * cap + rank, first_size + owner * (slots - cap) + rank - cap
    )[:moved]
    mine = (owner[None, :] == me) & (
        rank[None, :] == jnp.arange(slots, dtype=jnp.int32)[:, None]
    )
    slot_panel = jnp.sum(jnp.where(mine, number[None, :] + 1, 0), axis=1) - 1
    kind = jnp.where(slot_panel < 0, 0, jnp.where(slot_panel < moved, 1, 2)).astype(jnp.int32)
    mod_row = jnp.where(kind == 2, (slot_panel - moved) * panel_rows, 0).astype(jnp.int32)

    low = master[0].astype(bf16)
    sources = [lax.all_gather(low[:cap], "batch", axis=0, tiled=True)]
    over = None
    if cap < slots:
        beyond = jnp.max(jnp.where(number < moved, rank, 0)) >= cap
        over = lax.pmax(beyond.astype(f32), "section") > 0.5
        rest = low[cap:]
        rest_shape = (owner_total * (slots - cap), panel_rows, D)
        sources.append(
            lax.cond(
                over,
                lambda part: lax.all_gather(part, "batch", axis=0, tiled=True),
                lambda part: jnp.zeros(rest_shape, bf16),
                rest,
            )
        )
    sheet = assemble(place, sources, moved).reshape(moved * panel_rows, D)

    all_steps = lax.all_gather(timesteps, "batch", axis=0, tiled=True)
    cond = jax.nn.silu(time_features(all_steps)).astype(bf16)
    clip_total = cond.shape[0]
    share = jnp.einsum("cd,sd->cs", cond, low.reshape(slots * panel_rows, D), preferred_element_type=f32)
    share = lax.all_to_all(
        share.reshape(owner_total, clips, slots * panel_rows), "batch", split_axis=0, concat_axis=0, tiled=True
    )
    share = share.reshape(owner_total, clips, slots, panel_rows).transpose(1, 0, 2, 3)
    share = share.reshape(clips, owner_total * slots, panel_rows)
    pick = (
        (owner * slots + rank)[moved:, None] == jnp.arange(owner_total * slots, dtype=jnp.int32)[None, :]
    ).astype(f32)
    mod = jnp.einsum("ps,csr->cpr", pick, share, precision=lax.Precision.HIGHEST)
    mod = mod.reshape(clips, 6, D)

    run = functools.partial
    fwd = run(forward, clips=clips, length=length, section=section, mod=mod, sheet=sheet)
    ffn = run(back_ffn, clips=clips, length=length, section=section, loss_weight=loss_weight, mod=mod, sheet=sheet)
    att = run(back_att, clips=clips, length=length, section=section, mod=mod, sheet=sheet)
    token = jnp.zeros((8, 128), f32)
    kept, sent, outs = [None] * clips, [None] * clips, None
    for c in range(clips):
        kept[c], outs, sent[c] = fwd(0, c, x=tokens, x_offset=c * length, token=token, state=None, outs=outs)
    received = [lax.ppermute(rows, "section", [(0, 1)]) for rows in sent]
    backs, atts, gin = [None] * clips, [None] * clips, None
    for c in range(clips):
        kept[c], outs, _ = fwd(1, c, x=received[c], x_offset=0, token=token, state=kept[c], outs=outs)
        backs[c] = ffn(1, c, g=cotangent, g_offset=c * length, kept=kept[c], state=None)
        atts[c], gin, sent[c], token = att(1, c, kept=kept[c], ffn=backs[c], state=None, gin=gin)
    received = [lax.ppermute(rows, "section", [(1, 0)]) for rows in sent]
    for c in range(clips):
        backs[c] = ffn(0, c, g=received[c], g_offset=0, kept=kept[c], state=backs[c])
        if c < clips - 1:
            atts[c], gin, _, token = att(0, c, kept=kept[c], ffn=backs[c], state=atts[c], gin=gin)

    code, index, slot_code, slot_index, sizes, beyond = routes(owner, rank, mine, me, owner_total, slots, moved)
    if beyond is not None:
        beyond = lax.pmax(beyond.astype(f32), "section") > 0.5
    grads = run(weight_grads, code=code, index=index, length=length, panel_rows=panel_rows)
    last = clips - 1
    every = [{**kept[c], **backs[c]} for c in range(clips)]
    if owner_total == 2 * CHIPS:
        place = me // 4 + (me // 2) % 2 * (CHIPS - 1 - 2 * (me // 4))
        sums, thread = [], []
        for jobs, chunk in (((("z", "db", UP_END),), 0), ((("du", "h2", PROJ_END),), 1), ((("da", "o", QKV_END), ("dqkv", "h1", 0)), 2)):
            if chunk == 2:
                atts[last], gin, _, token = att(
                    0, last, kept=kept[last], ffn=backs[last], state=atts[last], gin=gin
                )
                every = [{**every[c], **atts[c]} for c in range(clips)]
                made = grads(jobs, every=every, sizes=[sizes[2]] * 2 + [sizes[3]], thread=thread)
                pair = made[:2]
                rest = made[2]
            else:
                made = grads(
                    jobs, every=every, sizes=[sizes[chunk]] * 2 + [sizes[2]] * 2 + [sizes[3]], thread=thread
                )
                pair, thread = made[:2], made[2:]
            half = ring_sum(place, *pair)
            sums += [half, swap_cores(half)]
        sums.append(
            lax.cond(
                beyond,
                lambda part: lax.psum_scatter(part, "batch", scatter_dimension=0, tiled=True),
                lambda part: jnp.zeros((slots, panel_rows, D), bf16),
                rest,
            )
        )
    else:
        atts[last], gin, _, token = att(0, last, kept=kept[last], ffn=backs[last], state=atts[last], gin=gin)
        every = [{**every[c], **atts[c]} for c in range(clips)]
        jobs = (("z", "db", UP_END), ("du", "h2", PROJ_END), ("da", "o", QKV_END), ("dqkv", "h1", 0))
        (made,) = grads(jobs, every=every, sizes=[sizes[0]], thread=[])
        sums = [lax.psum_scatter(made, "batch", scatter_dimension=0, tiled=True)]
    dmod = [jnp.concatenate([t["dmod_att"], b["dmod_ffn"]]) for t, b in zip(atts, backs)]
    dmod = jnp.stack(dmod).reshape(clips, 6 * D).astype(bf16)
    dmod = lax.all_gather(dmod, "batch", axis=0, tiled=True).T
    slot_code = jnp.where(kind == 1, slot_code, jnp.where(kind == 2, len(sums), len(sums) + 1))
    results = adam(
        slot_code, slot_index, mod_row, master[0], first_moment[0], second_moment[0], dmod, cond, sums
    )
    return (outs[None], gin[None], *(r[None] for r in results))


CAPS = (12, 12, 26)


def count_before(flag, group):
    number = jnp.arange(group.shape[0], dtype=jnp.int32)
    before = (group[:, None] == group[None, :]) & (number[None, :] < number[:, None]) & flag[None, :]
    return jnp.sum(before.astype(jnp.int32), axis=1)


def routes(owner, rank, mine, me, owner_total, slots, moved):
    if owner_total != 2 * CHIPS:
        code = jnp.zeros((moved,), jnp.int32)
        return code, (owner * slots + rank)[:moved], jnp.zeros((slots,), jnp.int32), jnp.arange(slots, dtype=jnp.int32), [owner_total * slots], None
    number = jnp.arange(moved, dtype=jnp.int32)
    held, core = owner[:moved], me % 2
    chip = held // 2
    spot = chip // 2 + chip % 2 * (CHIPS - 1 - 2 * (chip // 2))
    per_row = DOWN_END // moved
    down, up = number >= UP_END // per_row, (number >= PROJ_END // per_row) & (number < UP_END // per_row)
    kind = jnp.where(down, 0, jnp.where(up, 1, 2))
    order = jnp.where(
        down, count_before(down, chip), jnp.where(up, count_before(up, chip), 0)
    )
    cap = jnp.where(down, CAPS[0], jnp.where(up, CAPS[1], 0))
    late = order >= cap
    order = jnp.where(late, count_before(late, chip), order)
    chunk = jnp.where(late, 2, kind)
    rest = late & (order >= CAPS[2])
    half = order % 2
    size = jnp.where(chunk == 0, CAPS[0] // 2, jnp.where(chunk == 1, CAPS[1] // 2, CAPS[2] // 2))
    index = jnp.where(rest, held * slots + rank[:moved], spot * size + order // 2)
    away = (half != core).astype(jnp.int32)
    code = jnp.where(rest, 4, jnp.where(chunk == 2, 2 + away, away))
    last = number < PROJ_END // per_row
    code = jnp.where(last, code - 2, code).astype(jnp.int32)
    taken = mine[:, :moved].astype(jnp.int32)
    found = jnp.where(rest, 6, 2 * chunk + away)
    slot_code = jnp.sum(taken * found[None, :], axis=1)
    slot_index = jnp.sum(taken * jnp.where(rest, rank[:moved], order // 2)[None, :], axis=1)
    sizes = [CHIPS * CAPS[n] // 2 for n in range(3)] + [owner_total * slots]
    return code, index.astype(jnp.int32), slot_code.astype(jnp.int32), slot_index.astype(jnp.int32), sizes, jnp.any(rest)


def solution(mesh):
    placed = (
        P("batch", None),
        P("batch", None),
        P("batch"),
        P("batch"),
        P("section", None),
        P("section", "batch", None, None),
        P("section", "batch", None, None),
        P("section", "batch", None, None),
    )
    return jax.shard_map(
        body,
        mesh=mesh,
        in_specs=placed,
        out_specs=(
            P("section", "batch", None),
            P("section", "batch", None),
            P("section", "batch", None, None),
            P("section", "batch", None, None),
            P("section", "batch", None, None),
            P("section", "batch", None, None),
        ),
        check_vma=False,
    )
```

```python
import functools
import math

import jax
import jax.numpy as jnp
from jax import lax
from jax.experimental import pallas as pl
from jax.experimental.pallas import tpu as pltpu
from jax.sharding import PartitionSpec as P

D = 768
HEADS = 12
HEAD_DIM = 64
FF = 3072
STEP = 10
QKV_END = 3 * D
PROJ_END = 4 * D
UP_END = 4 * D + FF
DOWN_END = 4 * D + 2 * FF

norm_eps = 1e-06
adam_eps = 1e-08
learn_rate = 0.03
decay_rate = 0.1
beta_one = 0.5
beta_two = 0.5

bf16 = jnp.bfloat16
f32 = jnp.float32
SECTION, BATCH = "section", "batch"
VMEM_LIMIT = 46 * 1024 * 1024
VMEM_ALL = 58 * 1024 * 1024
ROWS = 128
GELU_C = math.sqrt(2.0 / math.pi)


def dot_nn(a, b):
    return lax.dot_general(a, b, (((1,), (0,)), ((), ())), preferred_element_type=f32)


def dot_nt(a, b):
    return lax.dot_general(a, b, (((1,), (1,)), ((), ())), preferred_element_type=f32)


def dot_tn(a, b):
    return lax.dot_general(a, b, (((0,), (0,)), ((), ())), preferred_element_type=f32)


def in_hbm(arrays):
    return [pltpu.with_memory_space_constraint(a, pltpu.HBM) for a in arrays]


def start(src, dst, sem):
    copy = pltpu.make_async_copy(src, dst, sem)
    copy.start()
    return copy


def norm(values):
    average = jnp.mean(values, axis=-1, keepdims=True)
    centred = values - average
    variance = jnp.mean(centred * centred, axis=-1, keepdims=True)
    inverse = lax.rsqrt(variance + norm_eps)
    return centred * inverse, inverse


def norm_back(grad, values, scale_row):
    normed, inverse = norm(values)
    dn = grad * (1.0 + scale_row)
    mean_one = jnp.mean(dn, axis=-1, keepdims=True)
    mean_two = jnp.mean(dn * normed, axis=-1, keepdims=True)
    dx = inverse * (dn - mean_one - normed * mean_two)
    return dx, jnp.sum(grad, axis=0, keepdims=True), jnp.sum(grad * normed, axis=0, keepdims=True)


def gelu_both(u):
    square = u * u
    half = 0.5 * jnp.tanh(u * (square * (0.044715 * GELU_C) + GELU_C)) + 0.5
    bend = u * (square * (6.0 * 0.044715 * GELU_C) + 2.0 * GELU_C)
    return u * half, half + half * (1.0 - half) * bend


def assemble_kernel(panels, first_size, index_ref, *refs):
    sources, sheet, sem = refs[:-2], refs[-2], refs[-1]
    rows = sheet.shape[0] // panels

    @pl.loop(0, panels, unroll=4)
    def _(p):
        where = index_ref[p]
        target = sheet.at[pl.ds(pl.multiple_of(p * rows, rows), rows)]
        if len(sources) == 1:
            pltpu.make_async_copy(sources[0].at[where], target, sem).start()
        else:

            @pl.when(where < first_size)
            def _():
                pltpu.make_async_copy(sources[0].at[where], target, sem).start()

            @pl.when(where >= first_size)
            def _():
                pltpu.make_async_copy(sources[1].at[where - first_size], target, sem).start()

    pltpu.make_async_copy(sheet, sheet, sem).wait()


def assemble(index, sources, panels):
    first_size = sources[0].shape[0]
    rows = sources[0].shape[1]
    return pl.pallas_call(
        functools.partial(assemble_kernel, panels, first_size),
        out_shape=pltpu.VMEM((panels * rows, D), bf16),
        in_specs=[pl.BlockSpec(memory_space=pltpu.SMEM)]
        + [pl.BlockSpec(memory_space=pltpu.HBM)] * len(sources),
        out_specs=pl.BlockSpec(memory_space=pltpu.VMEM),
        scratch_shapes=[pltpu.SemaphoreType.DMA],
        compiler_params=pltpu.CompilerParams(vmem_limit_bytes=VMEM_LIMIT),
        cost_estimate=pl.CostEstimate(flops=0, bytes_accessed=2 * panels * rows * D, transcendentals=0),
        name="assemble",
    )(index, *in_hbm(sources))


(
    N_XIN,
    N_H1,
    N_QKV,
    N_LSE,
    N_O,
    N_A,
    N_X1,
    N_H2,
    N_SLOPE,
    N_Z,
    N_B,
    N_OUT,
    N_DB,
    N_DU,
    N_DA,
    N_DX1,
    N_DMOD_FFN,
    N_DQKV,
    N_DMOD_ATT,
    N_G,
    N_SENT,
    N_DO,
    N_ACC,
    N_LSE_COLS,
    N_OUTS,
    N_GIN,
    N_MOD,
    N_X,
    N_AFTER,
    N_SECTION,
    N_LOSS,
) = range(31)


TILE = D
TILES = FF // TILE
PAIRS = HEADS // 2


def shapes_of(length):
    return {
        N_XIN: ((length, D), bf16),
        N_H1: ((length, D), bf16),
        N_QKV: ((length, 3 * D), bf16),
        N_LSE: ((16, length), f32),
        N_O: ((length, D), bf16),
        N_A: ((length, D), bf16),
        N_X1: ((length, D), f32),
        N_H2: ((length, D), bf16),
        N_SLOPE: ((length, FF), f32),
        N_Z: ((length, FF), bf16),
        N_B: ((length, D), bf16),
        N_OUT: ((length, D), bf16),
        N_DB: ((length, D), bf16),
        N_DU: ((length, FF), bf16),
        N_DA: ((length, D), bf16),
        N_DX1: ((length, D), f32),
        N_DMOD_FFN: ((4, D), f32),
        N_DQKV: ((length, 3 * D), bf16),
        N_DMOD_ATT: ((2, D), f32),
        N_G: ((length, D), bf16),
        N_SENT: ((length, D), bf16),
        N_DO: ((length, D), bf16),
        N_ACC: ((length, D), f32),
        N_LSE_COLS: ((length, 128), f32),
    }


def blocks_of(length):
    return [pl.ds(r, ROWS) for r in range(0, length, ROWS)]


def low_half():
    return lax.broadcasted_iota(jnp.int32, (1, 128), 1) < HEAD_DIM


def forward_qkv(v, w_qkv, row, length):
    for block in blocks_of(length):
        normed, _ = norm(v[N_XIN][block, :].astype(f32))
        v[N_H1][block, :] = (normed * (1.0 + row(1)) + row(0)).astype(bf16)
    for n in range(3):
        part = dot_nt(v[N_H1][...], w_qkv(n))
        v[N_QKV][:, n * D : (n + 1) * D] = part.astype(bf16)


def forward_attention(v, length):
    v[N_LSE_COLS][...] = jnp.zeros_like(v[N_LSE_COLS])
    low_lanes = low_half()

    @pl.loop(0, PAIRS, unroll=PAIRS)
    def _(pair):
        at = lambda n: pl.ds(pl.multiple_of(n * D + pair * 128, 128), 128)
        q = v[N_QKV][:, at(0)] * jnp.asarray(HEAD_DIM ** (-0.5), bf16)
        k = v[N_QKV][:, at(1)]
        value = v[N_QKV][:, at(2)]
        mixed = []
        for h in range(2):
            qh = jnp.where(low_lanes if h == 0 else ~low_lanes, q, jnp.zeros_like(q))
            v[N_SLOPE][:, h * length : (h + 1) * length] = dot_nt(qh, k)
        for h in range(2):
            lane = lax.broadcasted_iota(jnp.int32, (1, 128), 1) == pair * 2 + h
            span = slice(h * length, (h + 1) * length)
            for block in blocks_of(length):
                s = v[N_SLOPE][block, span]
                top = jnp.max(s, axis=-1, keepdims=True)
                e = jnp.exp(s - top)
                total = jnp.sum(e, axis=-1, keepdims=True)
                v[N_Z][block, span] = (e * (1.0 / total)).astype(bf16)
                v[N_LSE_COLS][block, :] = jnp.where(lane, top + jnp.log(total), v[N_LSE_COLS][block, :])
            mixed.append(dot_nn(v[N_Z][:, span], value))
        v[N_O][:, at(0)] = jnp.where(low_lanes, mixed[0], mixed[1]).astype(bf16)

    v[N_LSE][...] = v[N_LSE_COLS][...].T[:16, :]


def forward_proj(v, w_proj, row, length):
    v[N_ACC][...] = dot_nt(v[N_O][...], w_proj)
    for block in blocks_of(length):
        branch = v[N_ACC][block, :]
        v[N_A][block, :] = branch.astype(bf16)
        middle = v[N_XIN][block, :].astype(f32) + row(2) * branch
        v[N_X1][block, :] = middle
        normed, _ = norm(middle)
        v[N_H2][block, :] = (normed * (1.0 + row(4)) + row(3)).astype(bf16)


def forward_ffn(v, w_up, w_down, row, length, after):
    for n in range(TILES):
        span = slice(n * TILE, (n + 1) * TILE)
        v[N_SLOPE][:, span] = dot_nt(v[N_H2][...], w_up(n))
        for block in blocks_of(length):
            value, slope = gelu_both(v[N_SLOPE][block, span])
            v[N_Z][block, span] = value.astype(bf16)
            v[N_SLOPE][block, span] = slope
        part = dot_nn(v[N_Z][:, span], w_down(n))
        if n:
            v[N_ACC][...] += part
        else:
            v[N_ACC][...] = part
        after(n)
    for block in blocks_of(length):
        branch = v[N_ACC][block, :]
        v[N_B][block, :] = branch.astype(bf16)
        v[N_OUT][block, :] = (v[N_X1][block, :] + row(5) * branch).astype(bf16)


def back_gate(v, row, length, scale):
    gate_two = jnp.zeros((1, D), f32)
    for block in blocks_of(length):
        g = v[N_G][block, :].astype(f32)
        if scale is not None:
            g = g * scale
        v[N_DX1][block, :] = g
        v[N_DB][block, :] = (row(5) * g).astype(bf16)
        gate_two += jnp.sum(g * v[N_B][block, :].astype(f32), axis=0, keepdims=True)
    v[N_DMOD_FFN][3:4, :] = gate_two


def back_ffn_part(v, w_up, w_down, row, length, before, after):
    for n in range(TILES):
        span = slice(n * TILE, (n + 1) * TILE)
        before(n)
        dz = dot_nt(v[N_DB][...], w_down(n))
        v[N_DU][:, span] = (dz * v[N_SLOPE][:, span]).astype(bf16)
        part = dot_nn(v[N_DU][:, span], w_up(n))
        if n:
            v[N_ACC][...] += part
        else:
            v[N_ACC][...] = part
        after(n)


def back_middle(v, row, length):
    shift_two = jnp.zeros((1, D), f32)
    scale_two = jnp.zeros((1, D), f32)
    gate_one = jnp.zeros((1, D), f32)
    for block in blocks_of(length):
        dx, shift_part, scale_part = norm_back(v[N_ACC][block, :], v[N_X1][block, :], row(4))
        total = v[N_DX1][block, :] + dx
        v[N_DX1][block, :] = total
        shift_two += shift_part
        scale_two += scale_part
        gate_one += jnp.sum(total * v[N_A][block, :].astype(f32), axis=0, keepdims=True)
        v[N_DA][block, :] = (row(2) * total).astype(bf16)
    v[N_DMOD_FFN][0:1, :] = gate_one
    v[N_DMOD_FFN][1:2, :] = shift_two
    v[N_DMOD_FFN][2:3, :] = scale_two


def back_attention(v, w_proj, length):
    v[N_DO][...] = dot_nn(v[N_DA][...], w_proj).astype(bf16)
    low_lanes = low_half()
    scale = HEAD_DIM ** (-0.5)

    @pl.loop(0, PAIRS, unroll=PAIRS)
    def _(pair):
        at = lambda n: pl.ds(pl.multiple_of(n * D + pair * 128, 128), 128)
        q = v[N_QKV][:, at(0)]
        k = v[N_QKV][:, at(1)]
        value = v[N_QKV][:, at(2)]
        dop = v[N_DO][:, at(0)]
        zero = jnp.zeros_like(q)
        dq = dk = dv = None
        for h in range(2):
            lanes = low_lanes if h == 0 else ~low_lanes
            qh = jnp.where(lanes, q, zero)
            kh = jnp.where(lanes, k, zero)
            doh = jnp.where(lanes, dop, zero)
            st = dot_nt(k, qh * jnp.asarray(scale, bf16))
            pt = jnp.exp(st - v[N_LSE][pl.ds(pair * 2 + h, 1), :])
            dpt = dot_nt(value, doh)
            dv_part = dot_nn(pt.astype(bf16), doh)
            inner = jnp.sum(dpt * pt, axis=0, keepdims=True)
            drt = (pt * (dpt - inner) * scale).astype(bf16)
            dk_part = dot_nn(drt, qh)
            dq_part = dot_tn(drt, kh)
            dq = dq_part if h == 0 else dq + dq_part
            dk = dk_part if h == 0 else dk + dk_part
            dv = dv_part if h == 0 else dv + dv_part
        v[N_DQKV][:, at(0)] = dq.astype(bf16)
        v[N_DQKV][:, at(1)] = dk.astype(bf16)
        v[N_DQKV][:, at(2)] = dv.astype(bf16)


def back_input(v, w_qkv, row, length):
    v[N_ACC][...] = dot_nn(v[N_DQKV][...], w_qkv)
    shift_one = jnp.zeros((1, D), f32)
    scale_one = jnp.zeros((1, D), f32)
    for block in blocks_of(length):
        dx, shift_part, scale_part = norm_back(v[N_ACC][block, :], v[N_XIN][block, :].astype(f32), row(1))
        total = v[N_DX1][block, :] + dx
        v[N_DX1][block, :] = total
        v[N_SENT][block, :] = total.astype(bf16)
        shift_one += shift_part
        scale_one += scale_part
    v[N_DMOD_ATT][0:1, :] = shift_one
    v[N_DMOD_ATT][1:2, :] = scale_one


class Mover:
    def __init__(self, sems):
        self.sems, self.used, self.coming, self.going = sems, 0, {}, []

    def start(self, src, dst):
        copy = pltpu.make_async_copy(src, dst, self.sems.at[self.used])
        self.used += 1
        copy.start()
        return copy

    def fetch(self, name, src, dst):
        self.coming[name] = self.start(src, dst)

    def need(self, *names):
        for name in names:
            if name in self.coming:
                self.coming.pop(name).wait()

    def save(self, src, dst):
        self.going.append(self.start(src, dst))

    def finish(self):
        assert not self.coming
        for copy in self.going:
            copy.wait()


SEMS = 48


def call_block(kernel, name, want, clip, length, smem, sheet, read, write, hold, shared, chain, flops, moved, loose=None):
    any_spec = pl.BlockSpec(memory_space=pltpu.HBM)
    shapes = shapes_of(length)
    s_names, r_names, w_names = list(smem), list(read), list(write)
    chained = [n for n in w_names if chain.get(n) is not None]
    operands = [smem[n] for n in s_names] + [pltpu.with_memory_space_constraint(sheet, pltpu.VMEM)]
    operands += [read[n] if n == loose else in_hbm([read[n]])[0] for n in r_names]
    aliases = {len(operands) + i: w_names.index(n) for i, n in enumerate(chained)}
    operands += in_hbm([chain[n] for n in chained])

    def run(*refs):
        refs = list(refs)
        take = lambda names: dict(zip(names, [refs.pop(0) for _ in names]))
        s, w, r = take(s_names), refs.pop(0), take(r_names)
        take(chained)
        o = take(w_names)
        v = take(hold)
        v |= {n: v[other] for n, other in shared.items()}
        m, sems = refs

        @pl.when(s[N_SECTION][0] == want)
        def _():
            kernel(clip, length, s, m, r, o, v, w, Mover(sems))

    results = pl.pallas_call(
        run,
        out_shape=[pltpu.HBM(*write[n]) for n in w_names],
        in_specs=[pl.BlockSpec(memory_space=pltpu.SMEM)] * len(s_names)
        + [pl.BlockSpec(memory_space=pltpu.VMEM)]
        + [any_spec] * (len(r_names) + len(chained)),
        out_specs=[any_spec] * len(w_names),
        scratch_shapes=[pltpu.VMEM(*shapes[n]) for n in hold]
        + [pltpu.VMEM((6, D), f32), pltpu.SemaphoreType.DMA((SEMS,))],
        input_output_aliases=aliases,
        compiler_params=pltpu.CompilerParams(vmem_limit_bytes=VMEM_LIMIT),
        cost_estimate=pl.CostEstimate(flops=flops, bytes_accessed=moved, transcendentals=0),
        name=f"{name}_{clip}",
    )(*operands)
    return dict(zip(w_names, results))


def mod_row(m):
    return lambda n: m[n : n + 1, :]


def forward_body(clip, length, x_offset, m, r, v, w, mover, keep):
    row = mod_row(m)
    mover.fetch(N_MOD, r[N_MOD].at[clip], m)
    mover.fetch(N_XIN, r[N_X].at[pl.ds(x_offset, length)], v[N_XIN])
    mover.need(N_MOD, N_XIN)
    forward_qkv(v, lambda n: w[n * D : (n + 1) * D, :], row, length)
    keep(N_H1)
    keep(N_QKV)
    forward_attention(v, length)
    keep(N_LSE)
    keep(N_O)
    forward_proj(v, w[QKV_END:PROJ_END, :], row, length)
    keep(N_A)
    keep(N_X1)
    keep(N_H2)
    forward_ffn(
        v,
        lambda n: w[PROJ_END + n * D : PROJ_END + (n + 1) * D, :],
        lambda n: w[UP_END + n * D : UP_END + (n + 1) * D, :],
        row,
        length,
        lambda n: (keep(N_SLOPE, n), keep(N_Z, n)),
    )
    keep(N_B)


def saver(mover, v, o):
    def keep(name, n=None):
        if name not in o:
            return
        if n is None:
            mover.save(v[name], o[name])
        else:
            span = pl.ds(n * TILE, TILE)
            mover.save(v[name].at[:, span], o[name].at[:, span])

    return keep


FIRST_KEEP = (N_H1, N_QKV, N_LSE, N_O, N_A, N_X1, N_H2, N_SLOPE, N_Z, N_B)
BOTH_KEEP = (N_H1, N_O, N_H2, N_Z, N_DB, N_DU, N_DA, N_DQKV, N_DMOD_FFN, N_DMOD_ATT)


def first_forward(clip, clips, length, section, mod, x, sheet, outs):
    def kernel(clip, length, s, m, r, o, v, w, mover):
        forward_body(clip, length, clip * length, m, r, v, w, mover, saver(mover, v, o))
        mover.save(v[N_OUT], o[N_SENT])
        mover.save(v[N_OUT], o[N_OUTS].at[pl.ds(clip * length, length)])
        mover.finish()

    shapes = shapes_of(length)
    write = {n: shapes[n] for n in FIRST_KEEP}
    write |= {N_OUTS: ((clips * length, D), bf16), N_SENT: ((length, D), bf16)}
    hold = FIRST_KEEP + (N_XIN, N_OUT, N_ACC, N_LSE_COLS)
    return call_block(
        kernel, "first_forward", 0, clip, length, {N_SECTION: section}, sheet, {N_MOD: mod, N_X: x},
        write, hold, {}, {N_OUTS: outs}, 17 * 10**9, 30 << 20,
    )


def second_both(clip, clips, length, section, loss_weight, mod, x, g, sheet, chain):
    def kernel(clip, length, s, m, r, o, v, w, mover):
        keep = saver(mover, v, o)
        row = mod_row(m)
        forward_body(clip, length, 0, m, r, v, w, mover, keep)
        mover.fetch(N_G, r[N_G].at[pl.ds(clip * length, length)], v[N_G])
        mover.save(v[N_OUT], o[N_OUTS].at[pl.ds(clip * length, length)])
        mover.need(N_G)
        back_gate(v, row, length, s[N_LOSS][clip])
        keep(N_DB)
        back_ffn_part(
            v,
            lambda n: w[PROJ_END + n * D : PROJ_END + (n + 1) * D, :],
            lambda n: w[UP_END + n * D : UP_END + (n + 1) * D, :],
            row, length, lambda n: None, lambda n: keep(N_DU, n),
        )
        back_middle(v, row, length)
        keep(N_DA)
        keep(N_DMOD_FFN)
        back_attention(v, w[QKV_END:PROJ_END, :], length)
        keep(N_DQKV)
        back_input(v, w[0:QKV_END, :], row, length)
        mover.save(v[N_SENT], o[N_SENT])
        keep(N_DMOD_ATT)
        mover.save(v[N_DX1], o[N_GIN].at[pl.ds(clip * length, length)])
        mover.finish()

    shapes = shapes_of(length)
    write = {n: shapes[n] for n in BOTH_KEEP}
    write |= {N_OUTS: ((clips * length, D), bf16), N_GIN: ((clips * length, D), f32), N_SENT: ((length, D), bf16)}
    hold = (N_XIN, N_H1, N_QKV, N_LSE, N_O, N_A, N_X1, N_H2, N_SLOPE, N_Z, N_B, N_OUT, N_DB, N_DU, N_DX1)
    hold += (N_DMOD_FFN, N_DMOD_ATT, N_G, N_ACC, N_LSE_COLS)
    shared = {N_DQKV: N_QKV, N_DO: N_B, N_DA: N_A, N_SENT: N_G}
    return call_block(
        kernel, "second_both", 1, clip, length, {N_SECTION: section, N_LOSS: loss_weight},  sheet,
        {N_MOD: mod, N_X: x, N_G: g}, write, hold, shared, chain, 40 * 10**9, 40 << 20, N_X,
    )


BACK_MAKES = (N_DB, N_DU, N_DA, N_DQKV, N_DMOD_FFN, N_DMOD_ATT)


def first_back(clip, clips, length, section, mod, x, g, sheet, kept, chain, after):
    def kernel(clip, length, s, m, r, o, v, w, mover):
        keep = saver(mover, v, o)
        row = mod_row(m)
        mover.fetch(N_MOD, r[N_MOD].at[clip], m)
        mover.fetch(N_G, r[N_G], v[N_G])
        mover.fetch(N_B, r[N_B], v[N_B])
        for n in range(TILES):
            span = pl.ds(n * TILE, TILE)
            mover.fetch((N_SLOPE, n), r[N_SLOPE].at[:, span], v[N_SLOPE].at[:, span])
        for name in (N_X1, N_A, N_QKV, N_LSE):
            mover.fetch(name, r[name], v[name])
        mover.fetch(N_XIN, r[N_X].at[pl.ds(clip * length, length)], v[N_XIN])
        mover.need(N_MOD, N_G, N_B)
        back_gate(v, row, length, None)
        keep(N_DB)
        back_ffn_part(
            v,
            lambda n: w[PROJ_END + n * D : PROJ_END + (n + 1) * D, :],
            lambda n: w[UP_END + n * D : UP_END + (n + 1) * D, :],
            row, length, lambda n: mover.need((N_SLOPE, n)), lambda n: keep(N_DU, n),
        )
        mover.need(N_X1, N_A)
        back_middle(v, row, length)
        keep(N_DA)
        keep(N_DMOD_FFN)
        mover.need(N_QKV, N_LSE)
        back_attention(v, w[QKV_END:PROJ_END, :], length)
        keep(N_DQKV)
        mover.need(N_XIN)
        back_input(v, w[0:QKV_END, :], row, length)
        keep(N_DMOD_ATT)
        mover.save(v[N_DX1], o[N_GIN].at[pl.ds(clip * length, length)])
        mover.finish()

    shapes = shapes_of(length)
    read = {N_MOD: mod, N_X: x, N_G: g} | {n: kept[n] for n in (N_B, N_SLOPE, N_X1, N_A, N_QKV, N_LSE)}
    read[N_AFTER] = after
    write = {n: shapes[n] for n in BACK_MAKES} | {N_GIN: ((clips * length, D), f32)}
    hold = (N_G, N_B, N_SLOPE, N_X1, N_A, N_QKV, N_LSE, N_XIN, N_DB, N_DU, N_DX1, N_DMOD_FFN, N_DMOD_ATT, N_ACC)
    shared = {N_DQKV: N_QKV, N_DO: N_B, N_DA: N_A, N_SENT: N_G}
    return call_block(
        kernel, "first_back", 0, clip, length, {N_SECTION: section}, sheet, read,
        write, hold, shared, chain, 25 * 10**9, 30 << 20, N_G,
    )


def grads_kernel(jobs, clips, length, panel_rows, own, passed, others, code_ref, index_ref, *refs):
    count = 2 * len(jobs) * clips
    sources = refs[:count]
    refs = refs[count + others :]
    outs = refs[:own]
    scratch = refs[own + passed :]
    values = scratch[: 2 * len(jobs)]
    tile_v, in_sem, out_sem = scratch[2 * len(jobs) :]
    tiles = []
    for n, (left, right, base) in enumerate(jobs):
        tiles += [(n, column, base + column) for column in range(0, values[2 * n].shape[1], D)]
    get = {}

    def fetch(n, column):
        get[n, column] = [
            start(
                sources[n * clips + c].at[:, pl.ds(column, D)],
                values[n].at[pl.ds(c * length, length), pl.ds(column, D)],
                in_sem.at[len(get), c],
            )
            for c in range(clips)
        ]

    def fetch_tile(t):
        if t < len(tiles):
            n, column, _ = tiles[t]
            if column == 0:
                fetch(2 * n + 1, 0)
            fetch(2 * n, column)

    for t in range(3):
        fetch_tile(t)
    per_tile = D // panel_rows

    def drain(slot):
        pltpu.make_async_copy(outs[-1].at[pl.ds(0, per_tile)], tile_v.at[slot], out_sem.at[slot]).wait()

    for t, (n, column, first_row) in enumerate(tiles):
        slot = t % 2
        if column == 0:
            for copy in get[2 * n + 1, 0]:
                copy.wait()
        for copy in get[2 * n, column]:
            copy.wait()
        fetch_tile(t + 3)
        if t >= 2:
            drain(slot)
        part = dot_tn(values[2 * n][:, column : column + D], values[2 * n + 1][...])
        tile_v[slot, :, :, :] = part.astype(bf16).reshape(per_tile, panel_rows, D)

        @pl.loop(0, per_tile)
        def _(p):
            code = code_ref[first_row // panel_rows + p]
            where = index_ref[first_row // panel_rows + p]

            def put(numbers):
                for n_out in numbers:

                    @pl.when(code == n_out)
                    def _():
                        pltpu.make_async_copy(tile_v.at[slot, p], outs[n_out].at[where], out_sem.at[slot]).start()

            put(range(min(2, own)))
            if own > 2:

                @pl.when(code >= 2)
                def _():
                    put(range(2, own))

    for slot in range(min(2, len(tiles))):
        drain(slot)


def weight_grads(jobs, code, index, every, length, panel_rows, sizes, thread, after, through=()):
    clips = len(every)
    any_spec = pl.BlockSpec(memory_space=pltpu.HBM)
    operands, scratch = [code, index], []
    for left, right, _ in jobs:
        for name in (left, right):
            arrays = [every[c][name] for c in range(clips)]
            operands += arrays
            scratch.append(pltpu.VMEM((clips * length, arrays[0].shape[1]), bf16))
    aliases = {}
    for n, array in enumerate(thread):
        aliases[len(operands)] = len(sizes) - len(thread) + n
        operands.append(array)
    passed = [pltpu.HBM(a.shape, a.dtype) for a in through]
    for n, array in enumerate(through):
        aliases[len(operands)] = len(sizes) + n
        operands.append(array)
    operands += after
    width = sum(s.shape[1] for s in scratch[0::2])
    return pl.pallas_call(
        functools.partial(grads_kernel, jobs, clips, length, panel_rows, len(sizes), len(passed), len(thread) + len(through) + len(after)),
        out_shape=[pltpu.HBM((size, panel_rows, D), bf16) for size in sizes] + passed,
        in_specs=[pl.BlockSpec(memory_space=pltpu.SMEM)] * 2 + [any_spec] * (len(operands) - 2),
        out_specs=[any_spec] * (len(sizes) + len(passed)),
        scratch_shapes=scratch
        + [
            pltpu.VMEM((2, D // panel_rows, panel_rows, D), bf16),
            pltpu.SemaphoreType.DMA((width // D + len(jobs), clips)),
            pltpu.SemaphoreType.DMA((2,)),
        ],
        input_output_aliases=aliases,
        compiler_params=pltpu.CompilerParams(vmem_limit_bytes=VMEM_ALL),
        cost_estimate=pl.CostEstimate(
            flops=4 * clips * length * width * D, bytes_accessed=12 << 20, transcendentals=0
        ),
        name=f"grads_{jobs[0][2]}",
    )(*operands[:2], *in_hbm(operands[2:]))


GROUP = 8


def adam_kernel(n_sums, code_ref, index_ref, row_ref, master, first, second, dmod, cond, *refs):
    sums = refs[:n_sums]
    outs = refs[n_sums : n_sums + 4]
    scratch = refs[n_sums + 4 :]
    held = scratch[:3]
    made = scratch[3:7]
    grad_v, in_sem, grad_sem, out_sem = scratch[7:]
    slots, rows = master.shape[0], master.shape[1]
    groups = [(g, min(GROUP, slots - g)) for g in range(0, slots, GROUP)]
    get = [
        [start(a.at[pl.ds(g, size)], h.at[pl.ds(g, size)], in_sem.at[n, i]) for i, (a, h) in enumerate(zip((master, first, second), held))]
        for n, (g, size) in enumerate(groups)
    ]
    for n, (g, size) in enumerate(groups):

        @pl.loop(g, g + size)
        def _(slot):
            code = code_ref[slot]
            where = index_ref[slot]
            for n_sum in range(n_sums):

                @pl.when(code == n_sum)
                def _():
                    pltpu.make_async_copy(sums[n_sum].at[where], grad_v.at[slot], grad_sem.at[n]).start()

    put = []
    for n, (g, size) in enumerate(groups):
        for copy in get[n]:
            copy.wait()
        span = pl.ds(g, size)

        @pl.loop(g, g + size)
        def _(slot):
            code = code_ref[slot]

            @pl.when(code < n_sums)
            def _():
                pltpu.make_async_copy(sums[0].at[0], grad_v.at[slot], grad_sem.at[n]).wait()

        @pl.loop(g, g + size)
        def _(slot):
            code = code_ref[slot]

            def update(grad):
                first_next = beta_one * held[1][slot] + (1.0 - beta_one) * grad
                second_next = beta_two * held[2][slot] + (1.0 - beta_two) * grad * grad
                first_hat = first_next / (1.0 - beta_one**STEP)
                second_hat = second_next / (1.0 - beta_two**STEP)
                value = held[0][slot] - learn_rate * (
                    first_hat / (jnp.sqrt(second_hat) + adam_eps) + decay_rate * held[0][slot]
                )
                made[0][slot] = value
                made[1][slot] = first_next
                made[2][slot] = second_next
                made[3][slot] = value.astype(bf16)

            @pl.when(code < n_sums)
            def _():
                update(grad_v[slot].astype(f32))

            @pl.when(code == n_sums)
            def _():
                at = pl.multiple_of(row_ref[slot], rows)
                update(dot_nn(dmod[pl.ds(at, rows), :], cond[...]))

            @pl.when(code > n_sums)
            def _():
                update(jnp.zeros((rows, D), f32))

        for i in range(4):
            put.append(start(made[i].at[span], outs[i].at[span], out_sem.at[n, i]))
    for copy in put:
        copy.wait()


def adam(code, index, row, master, first, second, dmod, cond, sums):
    slots, rows = master.shape[0], master.shape[1]
    any_spec = pl.BlockSpec(memory_space=pltpu.HBM)
    smem, vmem = pl.BlockSpec(memory_space=pltpu.SMEM), pl.BlockSpec(memory_space=pltpu.VMEM)
    kinds = [f32, f32, f32, bf16]
    groups = -(-slots // GROUP)
    return pl.pallas_call(
        functools.partial(adam_kernel, len(sums)),
        in_specs=[smem] * 3 + [any_spec] * 3 + [vmem] * 2 + [any_spec] * len(sums),
        out_specs=[any_spec] * 4,
        out_shape=[pltpu.HBM(master.shape, kind) for kind in kinds],
        scratch_shapes=[pltpu.VMEM(master.shape, f32)] * 3
        + [pltpu.VMEM(master.shape, kind) for kind in kinds]
        + [
            pltpu.VMEM(master.shape, bf16),
            pltpu.SemaphoreType.DMA((groups, 3)),
            pltpu.SemaphoreType.DMA((groups,)),
            pltpu.SemaphoreType.DMA((groups, 4)),
        ],
        compiler_params=pltpu.CompilerParams(vmem_limit_bytes=VMEM_ALL),
        cost_estimate=pl.CostEstimate(flops=0, bytes_accessed=slots * rows * D * 30, transcendentals=0),
        name="adam",
    )(code, index, row, *in_hbm((master, first, second)), dmod, cond, *in_hbm(sums))


CHIPS = 8
LOOP = (0, 2, 4, 6, 7, 5, 3, 1)


def swap_cores(value):
    return lax.ppermute(value, BATCH, [(d, d ^ 1) for d in range(2 * CHIPS)])


def along(value, step):
    pairs = [
        (2 * LOOP[n] + core, 2 * LOOP[(n + step) % CHIPS] + core) for n in range(CHIPS) for core in range(2)
    ]
    return lax.ppermute(value, BATCH, pairs)


class Ring:
    def __init__(self, place, mine, other):
        self.place, self.size, self.left = place, mine.shape[0] // CHIPS, 4
        self.half = self.size // 2
        self.terms = (mine, swap_cores(other))

    def term(self, offset, low, high):
        first = ((self.place + offset) % CHIPS) * self.size + low
        return sum(lax.dynamic_slice_in_dim(a, first, high - low, 0).astype(f32) for a in self.terms)

    def hop(self):
        n, half, size = self.left, self.half, self.size
        if n == 4:
            ahead, behind = self.term(4, 0, half), self.term(-4, half, size)
        elif n == 3:
            ahead = jnp.concatenate([self.term(3, 0, half) + self.ahead.astype(f32), self.term(3, half, size)])
            behind = jnp.concatenate([self.term(-3, 0, half), self.term(-3, half, size) + self.behind.astype(f32)])
        else:
            ahead = self.term(n, 0, size) + self.ahead.astype(f32)
            behind = self.term(-n, 0, size) + self.behind.astype(f32)
        self.payload = [ahead.astype(bf16), behind.astype(bf16)]
        self.left -= 1
        self.send()

    def send(self):
        self.ahead, self.behind = along(self.payload[0], 1), along(self.payload[1], -1)

    def held(self, count=2):
        self.count = count
        return list(self.terms[:count])

    def later(self, made):
        self.terms = tuple(made[-self.count :]) + self.terms[self.count :]
        return made[: -self.count]

    def finish(self):
        while self.left:
            self.hop()
        return (self.term(0, 0, self.size) + self.ahead.astype(f32) + self.behind.astype(f32)).astype(bf16)


def time_features(steps_in):
    half_width = D // 2
    freqs = jnp.exp(-math.log(10000.0) * jnp.arange(half_width, dtype=f32) / half_width)
    angles = steps_in.astype(f32)[:, None] * freqs[None, :]
    return jnp.concatenate([jnp.cos(angles), jnp.sin(angles)], axis=1)


def body(tokens, cotangent, loss_weight, timesteps, owners, master, first_moment, second_moment):
    section_index = lax.axis_index(SECTION)
    me = lax.axis_index(BATCH)
    owner_total = lax.axis_size(BATCH)
    slots, panel_rows = master.shape[1], master.shape[2]
    clips = timesteps.shape[0]
    length = tokens.shape[0] // clips
    owner = owners[0]
    panels = owner.shape[0]
    moved = DOWN_END // panel_rows
    cap = min(slots, max(4, (slots * 27 + 30) // 31))
    section = jnp.reshape(section_index, (1,)).astype(jnp.int32)

    number = jnp.arange(panels, dtype=jnp.int32)
    same = (owner[:, None] == owner[None, :]) & (number[None, :] < number[:, None])
    rank = jnp.sum(same.astype(jnp.int32), axis=1)
    first_size = owner_total * cap
    place = jnp.where(
        rank < cap, owner * cap + rank, first_size + owner * (slots - cap) + rank - cap
    )[:moved]
    mine = (owner[None, :] == me) & (
        rank[None, :] == jnp.arange(slots, dtype=jnp.int32)[:, None]
    )
    slot_panel = jnp.sum(jnp.where(mine, number[None, :] + 1, 0), axis=1) - 1
    kind = jnp.where(slot_panel < 0, 0, jnp.where(slot_panel < moved, 1, 2)).astype(jnp.int32)
    grad_row = jnp.where(kind == 2, (slot_panel - moved) * panel_rows, 0).astype(jnp.int32)

    rings = owner_total == 2 * CHIPS
    code, index, slot_code, slot_index, sizes, beyond = routes(owner, rank, mine, me, owner_total, slots, moved)
    low = master[0].astype(bf16)
    gathered = lax.all_gather(low[:cap], BATCH, axis=0, tiled=True)
    spot = jnp.arange(owner_total * clips, dtype=jnp.int32) // clips == me
    news = [jnp.where(spot, jnp.tile(timesteps.astype(f32), owner_total), 0.0)]
    past = jnp.max(jnp.where(number < moved, rank, 0)) >= cap
    news.append(jnp.stack([past, beyond]).astype(f32) + 0.0 * low[0, 0, 0].astype(f32))
    news = lax.pmax(jnp.concatenate(news), (SECTION, BATCH))
    all_steps = news[:-2]
    beyond = news[-1] > 0.5
    sources = [gathered]
    if cap < slots:
        rest_shape = (owner_total * (slots - cap), panel_rows, D)
        sources.append(
            lax.cond(
                news[-2] + 0.0 * gathered[0, 0, 0].astype(f32) > 0.5,
                lambda part: lax.all_gather(part, BATCH, axis=0, tiled=True),
                lambda part: jnp.zeros(rest_shape, bf16),
                low[cap:],
            )
        )
    sheet = assemble(place, sources, moved)

    cond = jax.nn.silu(time_features(all_steps)).astype(bf16)
    clip_total = cond.shape[0]
    share = jnp.einsum("cd,sd->cs", cond, low.reshape(slots * panel_rows, D), preferred_element_type=f32)
    share = lax.all_to_all(
        share.reshape(owner_total, clips, slots * panel_rows), BATCH, split_axis=0, concat_axis=0, tiled=True
    )
    share = share.reshape(owner_total, clips, slots, panel_rows).transpose(1, 0, 2, 3)
    share = share.reshape(clips, owner_total * slots, panel_rows)
    pick = (
        (owner * slots + rank)[moved:, None] == jnp.arange(owner_total * slots, dtype=jnp.int32)[None, :]
    ).astype(f32)
    mod = jnp.einsum("ps,csr->cpr", pick, share, precision=lax.Precision.HIGHEST)
    mod = mod.reshape(clips, 6, D)

    run = functools.partial
    base = dict(clips=clips, length=length, section=section, mod=mod, sheet=sheet)
    firsts, outs = [], None
    for c in range(clips):
        firsts.append(first_forward(c, x=tokens, outs=outs, **base))
        outs = firsts[c][N_OUTS]
    received = [lax.ppermute(f[N_SENT], SECTION, [(0, 1)]) for f in firsts]
    seconds, gin = [], None
    for c in range(clips):
        chain = {n: firsts[c][n] for n in (N_H1, N_O, N_H2, N_Z)} | {N_OUTS: outs, N_GIN: gin}
        seconds.append(second_both(c, loss_weight=loss_weight, x=received[c], g=cotangent, chain=chain, **base))
        outs, gin = seconds[c][N_OUTS], seconds[c][N_GIN]
    received = [lax.ppermute(f[N_SENT], SECTION, [(1, 0)]) for f in seconds]
    every = [dict(f) for f in seconds]

    for c in range(clips):
        chain = {n: every[c][n] for n in BACK_MAKES} | {N_GIN: gin}
        every[c] |= first_back(c, x=tokens, g=received[c], kept=firsts[c], chain=chain, after=every[0][N_DMOD_ATT] if c else mod, **base)
        gin = every[c][N_GIN]

    dmod = [jnp.concatenate([e[N_DMOD_ATT], e[N_DMOD_FFN]]) for e in every]
    dmod = jnp.stack(dmod).reshape(1, clips, 6 * D).astype(bf16)
    dmod = lax.all_to_all(jnp.broadcast_to(dmod, (owner_total, clips, 6 * D)), BATCH, split_axis=0, concat_axis=0, tiled=True)
    dmod = dmod.reshape(clip_total, 6 * D).T
    grads = run(weight_grads, code=code, index=index, every=every, length=length, panel_rows=panel_rows)
    if rings:
        place = me // 4 + (me // 2) % 2 * (CHIPS - 1 - 2 * (me // 4))
        wide = [sizes[1]] * 2 + [sizes[2]]
        first_jobs = ((N_DA, N_O, QKV_END), (N_DQKV, N_H1, 0), (N_DU, N_H2, PROJ_END))
        made = grads(first_jobs, sizes=[sizes[0]] * 2 + wide, thread=[], after=[])
        first = Ring(place, *made[:2])
        made = grads(((N_Z, N_DB, UP_END),), sizes=wide, thread=made[2:], after=[dmod], through=first.held(1))
        made = first.later(made)
        second = Ring(place, *made[:2])
        sums = []
        for ring in (first, second):
            half = ring.finish()
            sums += [half, swap_cores(half)]
        sums.append(
            lax.cond(
                beyond,
                lambda part: lax.psum_scatter(part, BATCH, scatter_dimension=0, tiled=True),
                lambda part: jnp.zeros((slots, panel_rows, D), bf16),
                made[2],
            )
        )
    else:
        jobs = ((N_Z, N_DB, UP_END), (N_DU, N_H2, PROJ_END), (N_DA, N_O, QKV_END), (N_DQKV, N_H1, 0))
        (made,) = grads(jobs, sizes=[sizes[0]], thread=[], after=[])
        sums = [lax.psum_scatter(made, BATCH, scatter_dimension=0, tiled=True)]
    slot_code = jnp.where(kind == 1, slot_code, jnp.where(kind == 2, len(sums), len(sums) + 1))
    results = adam(
        slot_code, slot_index, grad_row, master[0], first_moment[0], second_moment[0], dmod, cond, sums
    )
    return (outs[None], gin[None], *(r[None] for r in results))


CAPS = (24, 24)


def count_before(flag, group):
    number = jnp.arange(group.shape[0], dtype=jnp.int32)
    before = (group[:, None] == group[None, :]) & (number[None, :] < number[:, None]) & flag[None, :]
    return jnp.sum(before.astype(jnp.int32), axis=1)


def routes(owner, rank, mine, me, owner_total, slots, moved):
    if owner_total != 2 * CHIPS:
        code = jnp.zeros((moved,), jnp.int32)
        return code, (owner * slots + rank)[:moved], jnp.zeros((slots,), jnp.int32), jnp.arange(slots, dtype=jnp.int32), [owner_total * slots], jnp.bool_(False)
    number = jnp.arange(moved, dtype=jnp.int32)
    held, core = owner[:moved], me % 2
    chip = held // 2
    spot = chip // 2 + chip % 2 * (CHIPS - 1 - 2 * (chip // 2))
    per_row = DOWN_END // moved
    down = number >= UP_END // per_row
    order = count_before(~down, chip)
    late = down | (order >= CAPS[0])
    order = jnp.where(late, count_before(late, chip), order)
    rest = late & (order >= CAPS[1])
    half = order % 2
    size = jnp.where(late, CAPS[1] // 2, CAPS[0] // 2)
    index = jnp.where(rest, held * slots + rank[:moved], spot * size + order // 2)
    away = (half != core).astype(jnp.int32)
    code = jnp.where(rest, 4, jnp.where(late, 2 + away, away))
    code = jnp.where(down, code - 2, code).astype(jnp.int32)
    taken = mine[:, :moved].astype(jnp.int32)
    found = jnp.where(rest, 4, 2 * late.astype(jnp.int32) + away)
    slot_code = jnp.sum(taken * found[None, :], axis=1)
    slot_index = jnp.sum(taken * jnp.where(rest, rank[:moved], order // 2)[None, :], axis=1)
    sizes = [CHIPS * cap // 2 for cap in CAPS] + [owner_total * slots]
    return code, index.astype(jnp.int32), slot_code.astype(jnp.int32), slot_index.astype(jnp.int32), sizes, jnp.any(rest)


def solution(mesh):
    placed = (
        P(BATCH, None),
        P(BATCH, None),
        P(BATCH),
        P(BATCH),
        P(SECTION, None),
        P(SECTION, BATCH, None, None),
        P(SECTION, BATCH, None, None),
        P(SECTION, BATCH, None, None),
    )
    return jax.shard_map(
        body,
        mesh=mesh,
        in_specs=placed,
        out_specs=(
            P(SECTION, BATCH, None),
            P(SECTION, BATCH, None),
            P(SECTION, BATCH, None, None),
            P(SECTION, BATCH, None, None),
            P(SECTION, BATCH, None, None),
            P(SECTION, BATCH, None, None),
        ),
        check_vma=False,
    )
```

```python
import functools
import math

import jax
import jax.numpy as jnp
from jax import lax
from jax.experimental import pallas as pl
from jax.experimental.pallas import tpu as pltpu
from jax.sharding import PartitionSpec as P

D = 768
HEADS = 12
HEAD_DIM = 64
FF = 3072
STEP = 10
QKV_END = 3 * D
PROJ_END = 4 * D
UP_END = 4 * D + FF
DOWN_END = 4 * D + 2 * FF

norm_eps = 1e-06
adam_eps = 1e-08
learn_rate = 0.03
decay_rate = 0.1
beta_one = 0.5
beta_two = 0.5

bf16 = jnp.bfloat16
f32 = jnp.float32
SECTION, BATCH = "section", "batch"
VMEM_LIMIT = 46 * 1024 * 1024
VMEM_ALL = 58 * 1024 * 1024
ROWS = 128
GELU_C = math.sqrt(2.0 / math.pi)


def dot_nn(a, b):
    return lax.dot_general(a, b, (((1,), (0,)), ((), ())), preferred_element_type=f32)


def dot_nt(a, b):
    return lax.dot_general(a, b, (((1,), (1,)), ((), ())), preferred_element_type=f32)


def dot_tn(a, b):
    return lax.dot_general(a, b, (((0,), (0,)), ((), ())), preferred_element_type=f32)


def in_hbm(arrays):
    return [pltpu.with_memory_space_constraint(a, pltpu.HBM) for a in arrays]


def start(src, dst, sem):
    copy = pltpu.make_async_copy(src, dst, sem)
    copy.start()
    return copy


def norm(values):
    average = jnp.mean(values, axis=-1, keepdims=True)
    centred = values - average
    variance = jnp.mean(centred * centred, axis=-1, keepdims=True)
    inverse = lax.rsqrt(variance + norm_eps)
    return centred * inverse, inverse


def norm_back(grad, values, scale_row):
    normed, inverse = norm(values)
    dn = grad * (1.0 + scale_row)
    mean_one = jnp.mean(dn, axis=-1, keepdims=True)
    mean_two = jnp.mean(dn * normed, axis=-1, keepdims=True)
    dx = inverse * (dn - mean_one - normed * mean_two)
    return dx, jnp.sum(grad, axis=0, keepdims=True), jnp.sum(grad * normed, axis=0, keepdims=True)


def gelu_both(u):
    square = u * u
    half = 0.5 * jnp.tanh(u * (square * (0.044715 * GELU_C) + GELU_C)) + 0.5
    bend = u * (square * (6.0 * 0.044715 * GELU_C) + 2.0 * GELU_C)
    return u * half, half + half * (1.0 - half) * bend


def assemble_kernel(panels, first_size, index_ref, *refs):
    sources, sheet, sem = refs[:-2], refs[-2], refs[-1]
    rows = sheet.shape[0] // panels

    @pl.loop(0, panels, unroll=4)
    def _(p):
        where = index_ref[p]
        target = sheet.at[pl.ds(pl.multiple_of(p * rows, rows), rows)]
        if len(sources) == 1:
            pltpu.make_async_copy(sources[0].at[where], target, sem).start()
        else:

            @pl.when(where < first_size)
            def _():
                pltpu.make_async_copy(sources[0].at[where], target, sem).start()

            @pl.when(where >= first_size)
            def _():
                pltpu.make_async_copy(sources[1].at[where - first_size], target, sem).start()

    pltpu.make_async_copy(sheet, sheet, sem).wait()


def assemble(index, sources, panels):
    first_size = sources[0].shape[0]
    rows = sources[0].shape[1]
    return pl.pallas_call(
        functools.partial(assemble_kernel, panels, first_size),
        out_shape=pltpu.VMEM((panels * rows, D), bf16),
        in_specs=[pl.BlockSpec(memory_space=pltpu.SMEM)]
        + [pl.BlockSpec(memory_space=pltpu.HBM)] * len(sources),
        out_specs=pl.BlockSpec(memory_space=pltpu.VMEM),
        scratch_shapes=[pltpu.SemaphoreType.DMA],
        compiler_params=pltpu.CompilerParams(vmem_limit_bytes=VMEM_LIMIT),
        cost_estimate=pl.CostEstimate(flops=0, bytes_accessed=2 * panels * rows * D, transcendentals=0),
        name="assemble",
    )(index, *in_hbm(sources))


(
    N_XIN,
    N_H1,
    N_QKV,
    N_LSE,
    N_O,
    N_A,
    N_X1,
    N_H2,
    N_SLOPE,
    N_Z,
    N_B,
    N_OUT,
    N_DB,
    N_DU,
    N_DA,
    N_DX1,
    N_DMOD_FFN,
    N_DQKV,
    N_DMOD_ATT,
    N_G,
    N_SENT,
    N_DO,
    N_ACC,
    N_LSE_COLS,
    N_OUTS,
    N_GIN,
    N_MOD,
    N_X,
    N_AFTER,
    N_SECTION,
    N_LOSS,
) = range(31)


TILE = D
TILES = FF // TILE
PAIRS = HEADS // 2


def shapes_of(length):
    return {
        N_XIN: ((length, D), bf16),
        N_H1: ((length, D), bf16),
        N_QKV: ((length, 3 * D), bf16),
        N_LSE: ((16, length), f32),
        N_O: ((length, D), bf16),
        N_A: ((length, D), bf16),
        N_X1: ((length, D), f32),
        N_H2: ((length, D), bf16),
        N_SLOPE: ((length, FF), f32),
        N_Z: ((length, FF), bf16),
        N_B: ((length, D), bf16),
        N_OUT: ((length, D), bf16),
        N_DB: ((length, D), bf16),
        N_DU: ((length, FF), bf16),
        N_DA: ((length, D), bf16),
        N_DX1: ((length, D), f32),
        N_DMOD_FFN: ((4, D), f32),
        N_DQKV: ((length, 3 * D), bf16),
        N_DMOD_ATT: ((2, D), f32),
        N_G: ((length, D), bf16),
        N_SENT: ((length, D), bf16),
        N_DO: ((length, D), bf16),
        N_ACC: ((length, D), f32),
        N_LSE_COLS: ((length, 128), f32),
    }


def blocks_of(length):
    return [pl.ds(r, ROWS) for r in range(0, length, ROWS)]


def low_half():
    return lax.broadcasted_iota(jnp.int32, (1, 128), 1) < HEAD_DIM


def forward_qkv(v, w_qkv, row, length):
    for block in blocks_of(length):
        normed, _ = norm(v[N_XIN][block, :].astype(f32))
        v[N_H1][block, :] = (normed * (1.0 + row(1)) + row(0)).astype(bf16)
    for n in range(3):
        part = dot_nt(v[N_H1][...], w_qkv(n))
        v[N_QKV][:, n * D : (n + 1) * D] = part.astype(bf16)


def forward_attention(v, length):
    low_lanes = low_half()
    room = FF // length
    columns = lax.broadcasted_iota(jnp.int32, (1, 128), 1)

    def scores(head):
        at = slice(head // 2 * 128, head // 2 * 128 + 128)
        q = v[N_QKV][:, at] * jnp.asarray(HEAD_DIM ** (-0.5), bf16)
        qh = jnp.where(low_lanes if head % 2 == 0 else ~low_lanes, q, jnp.zeros_like(q))
        first = head % room * length
        v[N_SLOPE][:, first : first + length] = dot_nt(qh, v[N_QKV][:, D + at.start : D + at.stop])

    def softmax(head):
        span = slice(head % room * length, head % room * length + length)
        for block in blocks_of(length):
            s = v[N_SLOPE][block, span]
            top = jnp.max(s, axis=-1, keepdims=True)
            e = jnp.exp(s - top)
            total = jnp.sum(e, axis=-1, keepdims=True)
            v[N_Z][block, span] = (e * (1.0 / total)).astype(bf16)
            line = top + jnp.log(total)
            v[N_LSE_COLS][block, :] = jnp.where(columns == head, line, v[N_LSE_COLS][block, :]) if head else jnp.where(columns == 0, line, 0.0)

    def mix(head):
        at = slice(2 * D + head // 2 * 128, 2 * D + head // 2 * 128 + 128)
        span = slice(head % room * length, head % room * length + length)
        return dot_nn(v[N_Z][:, span], v[N_QKV][:, at])

    scores(0)
    mixed = [None] * HEADS
    for head in range(HEADS):
        if head + 1 < HEADS:
            scores(head + 1)
        softmax(head)
        mixed[head] = mix(head)
        if head % 2:
            at = slice(head // 2 * 128, head // 2 * 128 + 128)
            v[N_O][:, at] = jnp.where(low_lanes, mixed[head - 1], mixed[head]).astype(bf16)
    v[N_LSE][...] = v[N_LSE_COLS][...].T[:16, :]


def forward_proj(v, w_proj, row, length):
    v[N_ACC][...] = dot_nt(v[N_O][...], w_proj)
    for block in blocks_of(length):
        branch = v[N_ACC][block, :]
        v[N_A][block, :] = branch.astype(bf16)
        middle = v[N_XIN][block, :].astype(f32) + row(2) * branch
        v[N_X1][block, :] = middle
        normed, _ = norm(middle)
        v[N_H2][block, :] = (normed * (1.0 + row(4)) + row(3)).astype(bf16)


def forward_ffn(v, w_up, w_down, row, length, after):
    for n in range(TILES):
        span = slice(n * TILE, (n + 1) * TILE)
        v[N_SLOPE][:, span] = dot_nt(v[N_H2][...], w_up(n))
        for block in blocks_of(length):
            value, slope = gelu_both(v[N_SLOPE][block, span])
            v[N_Z][block, span] = value.astype(bf16)
            v[N_SLOPE][block, span] = slope
        part = dot_nn(v[N_Z][:, span], w_down(n))
        if n:
            v[N_ACC][...] += part
        else:
            v[N_ACC][...] = part
        after(n)
    for block in blocks_of(length):
        branch = v[N_ACC][block, :]
        v[N_B][block, :] = branch.astype(bf16)
        v[N_OUT][block, :] = (v[N_X1][block, :] + row(5) * branch).astype(bf16)


def back_gate(v, row, length, scale):
    gate_two = jnp.zeros((1, D), f32)
    for block in blocks_of(length):
        g = v[N_G][block, :].astype(f32)
        if scale is not None:
            g = g * scale
        v[N_DX1][block, :] = g
        v[N_DB][block, :] = (row(5) * g).astype(bf16)
        gate_two += jnp.sum(g * v[N_B][block, :].astype(f32), axis=0, keepdims=True)
    v[N_DMOD_FFN][3:4, :] = gate_two


def back_ffn_part(v, w_up, w_down, row, length, before, after):
    for n in range(TILES):
        span = slice(n * TILE, (n + 1) * TILE)
        before(n)
        dz = dot_nt(v[N_DB][...], w_down(n))
        v[N_DU][:, span] = (dz * v[N_SLOPE][:, span]).astype(bf16)
        part = dot_nn(v[N_DU][:, span], w_up(n))
        if n:
            v[N_ACC][...] += part
        else:
            v[N_ACC][...] = part
        after(n)


def back_middle(v, row, length):
    shift_two = jnp.zeros((1, D), f32)
    scale_two = jnp.zeros((1, D), f32)
    gate_one = jnp.zeros((1, D), f32)
    for block in blocks_of(length):
        dx, shift_part, scale_part = norm_back(v[N_ACC][block, :], v[N_X1][block, :], row(4))
        total = v[N_DX1][block, :] + dx
        v[N_DX1][block, :] = total
        shift_two += shift_part
        scale_two += scale_part
        gate_one += jnp.sum(total * v[N_A][block, :].astype(f32), axis=0, keepdims=True)
        v[N_DA][block, :] = (row(2) * total).astype(bf16)
    v[N_DMOD_FFN][0:1, :] = gate_one
    v[N_DMOD_FFN][1:2, :] = shift_two
    v[N_DMOD_FFN][2:3, :] = scale_two


def back_attention(v, w_proj, length):
    v[N_DO][...] = dot_nn(v[N_DA][...], w_proj).astype(bf16)
    low_lanes = low_half()
    scale = HEAD_DIM ** (-0.5)

    def parts(head):
        at = head // 2 * 128
        keep = lambda a: jnp.where(low_lanes if head % 2 == 0 else ~low_lanes, a, jnp.zeros_like(a))
        qh, doh = keep(v[N_QKV][:, at : at + 128]), keep(v[N_DO][:, at : at + 128])
        kh = keep(v[N_QKV][:, D + at : D + at + 128])
        return qh, kh, doh

    def first(head):
        at = head // 2 * 128
        qh, kh, doh = parts(head)
        st = dot_nt(v[N_QKV][:, D + at : D + at + 128], qh * jnp.asarray(scale, bf16))
        dpt = dot_nt(v[N_QKV][:, 2 * D + at : 2 * D + at + 128], doh)
        return st, dpt, qh, kh, doh

    def rest(head, st, dpt, qh, kh, doh):
        pt = jnp.exp(st - v[N_LSE][head : head + 1, :])
        dv = dot_nn(pt.astype(bf16), doh)
        inner = jnp.sum(dpt * pt, axis=0, keepdims=True)
        drt = (pt * (dpt - inner) * scale).astype(bf16)
        return dot_tn(drt, kh), dot_nn(drt, qh), dv

    ahead = first(0)
    made = None
    for head in range(HEADS):
        now = ahead
        if head + 1 < HEADS:
            ahead = first(head + 1)
        made_now = rest(head, *now)
        if head % 2:
            for n in range(3):
                at = n * D + head // 2 * 128
                v[N_DQKV][:, at : at + 128] = (made[n] + made_now[n]).astype(bf16)
        made = made_now


def back_input(v, w_qkv, row, length):
    v[N_ACC][...] = dot_nn(v[N_DQKV][...], w_qkv)
    shift_one = jnp.zeros((1, D), f32)
    scale_one = jnp.zeros((1, D), f32)
    for block in blocks_of(length):
        dx, shift_part, scale_part = norm_back(v[N_ACC][block, :], v[N_XIN][block, :].astype(f32), row(1))
        total = v[N_DX1][block, :] + dx
        v[N_DX1][block, :] = total
        v[N_SENT][block, :] = total.astype(bf16)
        shift_one += shift_part
        scale_one += scale_part
    v[N_DMOD_ATT][0:1, :] = shift_one
    v[N_DMOD_ATT][1:2, :] = scale_one


class Mover:
    def __init__(self, sems):
        self.sems, self.used, self.coming, self.going = sems, 0, {}, []

    def start(self, src, dst):
        copy = pltpu.make_async_copy(src, dst, self.sems.at[self.used])
        self.used += 1
        copy.start()
        return copy

    def fetch(self, name, src, dst):
        self.coming[name] = self.start(src, dst)

    def need(self, *names):
        for name in names:
            if name in self.coming:
                self.coming.pop(name).wait()

    def save(self, src, dst):
        self.going.append(self.start(src, dst))

    def finish(self):
        assert not self.coming
        for copy in self.going:
            copy.wait()


SEMS = 48


def call_block(kernel, name, want, clip, length, smem, sheet, read, write, hold, shared, chain, flops, moved, loose=None):
    any_spec = pl.BlockSpec(memory_space=pltpu.HBM)
    shapes = shapes_of(length)
    s_names, r_names, w_names = list(smem), list(read), list(write)
    chained = [n for n in w_names if chain.get(n) is not None]
    operands = [smem[n] for n in s_names] + [pltpu.with_memory_space_constraint(sheet, pltpu.VMEM)]
    operands += [read[n] if n == loose else in_hbm([read[n]])[0] for n in r_names]
    aliases = {len(operands) + i: w_names.index(n) for i, n in enumerate(chained)}
    operands += in_hbm([chain[n] for n in chained])

    def run(*refs):
        refs = list(refs)
        take = lambda names: dict(zip(names, [refs.pop(0) for _ in names]))
        s, w, r = take(s_names), refs.pop(0), take(r_names)
        take(chained)
        o = take(w_names)
        v = take(hold)
        v |= {n: v[other] for n, other in shared.items()}
        m, sems = refs

        @pl.when(s[N_SECTION][0] == want)
        def _():
            kernel(clip, length, s, m, r, o, v, w, Mover(sems))

    results = pl.pallas_call(
        run,
        out_shape=[pltpu.HBM(*write[n]) for n in w_names],
        in_specs=[pl.BlockSpec(memory_space=pltpu.SMEM)] * len(s_names)
        + [pl.BlockSpec(memory_space=pltpu.VMEM)]
        + [any_spec] * (len(r_names) + len(chained)),
        out_specs=[any_spec] * len(w_names),
        scratch_shapes=[pltpu.VMEM(*shapes[n]) for n in hold]
        + [pltpu.VMEM((6, D), f32), pltpu.SemaphoreType.DMA((SEMS,))],
        input_output_aliases=aliases,
        compiler_params=pltpu.CompilerParams(vmem_limit_bytes=VMEM_LIMIT),
        cost_estimate=pl.CostEstimate(flops=flops, bytes_accessed=moved, transcendentals=0),
        name=f"{name}_{clip}",
    )(*operands)
    return dict(zip(w_names, results))


def mod_row(m):
    return lambda n: m[n : n + 1, :]


def forward_body(clip, length, x_offset, m, r, v, w, mover, keep):
    row = mod_row(m)
    mover.fetch(N_MOD, r[N_MOD].at[clip], m)
    mover.fetch(N_XIN, r[N_X].at[pl.ds(x_offset, length)], v[N_XIN])
    mover.need(N_MOD, N_XIN)
    forward_qkv(v, lambda n: w[n * D : (n + 1) * D, :], row, length)
    keep(N_H1)
    keep(N_QKV)
    forward_attention(v, length)
    keep(N_LSE)
    keep(N_O)
    forward_proj(v, w[QKV_END:PROJ_END, :], row, length)
    keep(N_A)
    keep(N_X1)
    keep(N_H2)
    forward_ffn(
        v,
        lambda n: w[PROJ_END + n * D : PROJ_END + (n + 1) * D, :],
        lambda n: w[UP_END + n * D : UP_END + (n + 1) * D, :],
        row,
        length,
        lambda n: (keep(N_SLOPE, n), keep(N_Z, n)),
    )
    keep(N_B)


def saver(mover, v, o):
    def keep(name, n=None):
        if name not in o:
            return
        if n is None:
            mover.save(v[name], o[name])
        else:
            span = pl.ds(n * TILE, TILE)
            mover.save(v[name].at[:, span], o[name].at[:, span])

    return keep


FIRST_KEEP = (N_H1, N_QKV, N_LSE, N_O, N_A, N_X1, N_H2, N_SLOPE, N_Z, N_B)
BOTH_KEEP = (N_H1, N_O, N_H2, N_Z, N_DB, N_DU, N_DA, N_DQKV, N_DMOD_FFN, N_DMOD_ATT)


def first_forward(clip, clips, length, section, mod, x, sheet, outs):
    def kernel(clip, length, s, m, r, o, v, w, mover):
        forward_body(clip, length, clip * length, m, r, v, w, mover, saver(mover, v, o))
        mover.save(v[N_OUT], o[N_SENT])
        mover.save(v[N_OUT], o[N_OUTS].at[pl.ds(clip * length, length)])
        mover.finish()

    shapes = shapes_of(length)
    write = {n: shapes[n] for n in FIRST_KEEP}
    write |= {N_OUTS: ((clips * length, D), bf16), N_SENT: ((length, D), bf16)}
    hold = FIRST_KEEP + (N_XIN, N_OUT, N_ACC, N_LSE_COLS)
    return call_block(
        kernel, "first_forward", 0, clip, length, {N_SECTION: section}, sheet, {N_MOD: mod, N_X: x},
        write, hold, {}, {N_OUTS: outs}, 17 * 10**9, 30 << 20,
    )


def second_both(clip, clips, length, section, loss_weight, mod, x, g, sheet, chain):
    def kernel(clip, length, s, m, r, o, v, w, mover):
        keep = saver(mover, v, o)
        row = mod_row(m)
        forward_body(clip, length, 0, m, r, v, w, mover, keep)
        mover.fetch(N_G, r[N_G].at[pl.ds(clip * length, length)], v[N_G])
        mover.save(v[N_OUT], o[N_OUTS].at[pl.ds(clip * length, length)])
        mover.need(N_G)
        back_gate(v, row, length, s[N_LOSS][clip])
        keep(N_DB)
        back_ffn_part(
            v,
            lambda n: w[PROJ_END + n * D : PROJ_END + (n + 1) * D, :],
            lambda n: w[UP_END + n * D : UP_END + (n + 1) * D, :],
            row, length, lambda n: None, lambda n: keep(N_DU, n),
        )
        back_middle(v, row, length)
        keep(N_DA)
        keep(N_DMOD_FFN)
        back_attention(v, w[QKV_END:PROJ_END, :], length)
        keep(N_DQKV)
        back_input(v, w[0:QKV_END, :], row, length)
        mover.save(v[N_SENT], o[N_SENT])
        keep(N_DMOD_ATT)
        mover.save(v[N_DX1], o[N_GIN].at[pl.ds(clip * length, length)])
        mover.finish()

    shapes = shapes_of(length)
    write = {n: shapes[n] for n in BOTH_KEEP}
    write |= {N_OUTS: ((clips * length, D), bf16), N_GIN: ((clips * length, D), f32), N_SENT: ((length, D), bf16)}
    hold = (N_XIN, N_H1, N_QKV, N_LSE, N_O, N_A, N_X1, N_H2, N_SLOPE, N_Z, N_B, N_OUT, N_DB, N_DU, N_DX1)
    hold += (N_DMOD_FFN, N_DMOD_ATT, N_G, N_ACC, N_LSE_COLS)
    shared = {N_DQKV: N_QKV, N_DO: N_B, N_DA: N_A, N_SENT: N_G}
    return call_block(
        kernel, "second_both", 1, clip, length, {N_SECTION: section, N_LOSS: loss_weight},  sheet,
        {N_MOD: mod, N_X: x, N_G: g}, write, hold, shared, chain, 40 * 10**9, 40 << 20, N_X,
    )


BACK_MAKES = (N_DB, N_DU, N_DA, N_DQKV, N_DMOD_FFN, N_DMOD_ATT)


def first_back(clip, clips, length, section, mod, x, g, sheet, kept, chain, after):
    def kernel(clip, length, s, m, r, o, v, w, mover):
        keep = saver(mover, v, o)
        row = mod_row(m)
        mover.fetch(N_MOD, r[N_MOD].at[clip], m)
        mover.fetch(N_G, r[N_G], v[N_G])
        mover.fetch(N_B, r[N_B], v[N_B])
        for n in range(TILES):
            span = pl.ds(n * TILE, TILE)
            mover.fetch((N_SLOPE, n), r[N_SLOPE].at[:, span], v[N_SLOPE].at[:, span])
        for name in (N_X1, N_A, N_QKV, N_LSE):
            mover.fetch(name, r[name], v[name])
        mover.fetch(N_XIN, r[N_X].at[pl.ds(clip * length, length)], v[N_XIN])
        mover.need(N_MOD, N_G, N_B)
        back_gate(v, row, length, None)
        keep(N_DB)
        back_ffn_part(
            v,
            lambda n: w[PROJ_END + n * D : PROJ_END + (n + 1) * D, :],
            lambda n: w[UP_END + n * D : UP_END + (n + 1) * D, :],
            row, length, lambda n: mover.need((N_SLOPE, n)), lambda n: keep(N_DU, n),
        )
        mover.need(N_X1, N_A)
        back_middle(v, row, length)
        keep(N_DA)
        keep(N_DMOD_FFN)
        mover.need(N_QKV, N_LSE)
        back_attention(v, w[QKV_END:PROJ_END, :], length)
        keep(N_DQKV)
        mover.need(N_XIN)
        back_input(v, w[0:QKV_END, :], row, length)
        keep(N_DMOD_ATT)
        mover.save(v[N_DX1], o[N_GIN].at[pl.ds(clip * length, length)])
        mover.finish()

    shapes = shapes_of(length)
    read = {N_MOD: mod, N_X: x, N_G: g} | {n: kept[n] for n in (N_B, N_SLOPE, N_X1, N_A, N_QKV, N_LSE)}
    read[N_AFTER] = after
    write = {n: shapes[n] for n in BACK_MAKES} | {N_GIN: ((clips * length, D), f32)}
    hold = (N_G, N_B, N_SLOPE, N_X1, N_A, N_QKV, N_LSE, N_XIN, N_DB, N_DU, N_DX1, N_DMOD_FFN, N_DMOD_ATT, N_ACC)
    shared = {N_DQKV: N_QKV, N_DO: N_B, N_DA: N_A, N_SENT: N_G}
    return call_block(
        kernel, "first_back", 0, clip, length, {N_SECTION: section}, sheet, read,
        write, hold, shared, chain, 25 * 10**9, 30 << 20, N_G,
    )


def grads_kernel(jobs, clips, length, panel_rows, own, passed, others, code_ref, index_ref, *refs):
    count = 2 * len(jobs) * clips
    sources = refs[:count]
    refs = refs[count + others :]
    outs = refs[:own]
    scratch = refs[own + passed :]
    values = scratch[: 2 * len(jobs)]
    tile_v, in_sem, out_sem = scratch[2 * len(jobs) :]
    tiles = []
    for n, (left, right, base) in enumerate(jobs):
        tiles += [(n, column, base + column) for column in range(0, values[2 * n].shape[1], D)]
    get = {}

    def fetch(n, column):
        get[n, column] = [
            start(
                sources[n * clips + c].at[:, pl.ds(column, D)],
                values[n].at[pl.ds(c * length, length), pl.ds(column, D)],
                in_sem.at[len(get), c],
            )
            for c in range(clips)
        ]

    def fetch_tile(t):
        if t < len(tiles):
            n, column, _ = tiles[t]
            if column == 0:
                fetch(2 * n + 1, 0)
            fetch(2 * n, column)

    for t in range(3):
        fetch_tile(t)
    per_tile = D // panel_rows

    def drain(slot):
        pltpu.make_async_copy(outs[-1].at[pl.ds(0, per_tile)], tile_v.at[slot], out_sem.at[slot]).wait()

    for t, (n, column, first_row) in enumerate(tiles):
        slot = t % 2
        if column == 0:
            for copy in get[2 * n + 1, 0]:
                copy.wait()
        for copy in get[2 * n, column]:
            copy.wait()
        fetch_tile(t + 3)
        if t >= 2:
            drain(slot)
        part = dot_tn(values[2 * n][:, column : column + D], values[2 * n + 1][...])
        tile_v[slot, :, :, :] = part.astype(bf16).reshape(per_tile, panel_rows, D)

        @pl.loop(0, per_tile)
        def _(p):
            code = code_ref[first_row // panel_rows + p]
            where = index_ref[first_row // panel_rows + p]

            def put(numbers):
                for n_out in numbers:

                    @pl.when(code == n_out)
                    def _():
                        pltpu.make_async_copy(tile_v.at[slot, p], outs[n_out].at[where], out_sem.at[slot]).start()

            put(range(min(2, own)))
            if own > 2:

                @pl.when(code >= 2)
                def _():
                    put(range(2, own))

    for slot in range(min(2, len(tiles))):
        drain(slot)


def weight_grads(jobs, code, index, every, length, panel_rows, sizes, thread, after, through=()):
    clips = len(every)
    any_spec = pl.BlockSpec(memory_space=pltpu.HBM)
    operands, scratch = [code, index], []
    for left, right, _ in jobs:
        for name in (left, right):
            arrays = [every[c][name] for c in range(clips)]
            operands += arrays
            scratch.append(pltpu.VMEM((clips * length, arrays[0].shape[1]), bf16))
    aliases = {}
    for n, array in enumerate(thread):
        aliases[len(operands)] = len(sizes) - len(thread) + n
        operands.append(array)
    passed = [pltpu.HBM(a.shape, a.dtype) for a in through]
    for n, array in enumerate(through):
        aliases[len(operands)] = len(sizes) + n
        operands.append(array)
    operands += after
    width = sum(s.shape[1] for s in scratch[0::2])
    return pl.pallas_call(
        functools.partial(grads_kernel, jobs, clips, length, panel_rows, len(sizes), len(passed), len(thread) + len(through) + len(after)),
        out_shape=[pltpu.HBM((size, panel_rows, D), bf16) for size in sizes] + passed,
        in_specs=[pl.BlockSpec(memory_space=pltpu.SMEM)] * 2 + [any_spec] * (len(operands) - 2),
        out_specs=[any_spec] * (len(sizes) + len(passed)),
        scratch_shapes=scratch
        + [
            pltpu.VMEM((2, D // panel_rows, panel_rows, D), bf16),
            pltpu.SemaphoreType.DMA((width // D + len(jobs), clips)),
            pltpu.SemaphoreType.DMA((2,)),
        ],
        input_output_aliases=aliases,
        compiler_params=pltpu.CompilerParams(vmem_limit_bytes=VMEM_ALL),
        cost_estimate=pl.CostEstimate(
            flops=4 * clips * length * width * D, bytes_accessed=12 << 20, transcendentals=0
        ),
        name=f"grads_{jobs[0][2]}",
    )(*operands[:2], *in_hbm(operands[2:]))


def adam_kernel(low, high, n_sums, chained, code_ref, index_ref, row_ref, master, first, second, dmod, cond, *refs):
    sums = refs[:n_sums]
    refs = refs[n_sums + (4 if chained else 0) :]
    outs, held, made = refs[:4], refs[4:7], refs[7:11]
    grad_v, in_sem, grad_sem, out_sem = refs[11:]
    slots, rows = master.shape[0], master.shape[1]
    sources = (master, first, second)

    def each(step):
        @pl.loop(0, slots)
        def _(slot):
            code = code_ref[slot]

            @pl.when((code >= low) & (code < high))
            def _():
                step(slot, code)

    def fetch(slot, code):
        for source, target in zip(sources, held):
            pltpu.make_async_copy(source.at[slot], target.at[slot], in_sem.at[slot]).start()
        for n in range(max(low, 2), min(high, n_sums + 2)):

            @pl.when(code == n)
            def _():
                pltpu.make_async_copy(sums[n - 2].at[index_ref[slot]], grad_v.at[slot], grad_sem.at[slot]).start()

    def work(slot, code):
        for source, target in zip(sources, held):
            pltpu.make_async_copy(source.at[slot], target.at[slot], in_sem.at[slot]).wait()

        def update(grad):
            first_next = beta_one * held[1][slot] + (1.0 - beta_one) * grad
            second_next = beta_two * held[2][slot] + (1.0 - beta_two) * grad * grad
            first_hat = first_next / (1.0 - beta_one**STEP)
            second_hat = second_next / (1.0 - beta_two**STEP)
            value = held[0][slot] - learn_rate * (
                first_hat / (jnp.sqrt(second_hat) + adam_eps) + decay_rate * held[0][slot]
            )
            made[0][slot] = value
            made[1][slot] = first_next
            made[2][slot] = second_next
            made[3][slot] = value.astype(bf16)

        if high > 2:

            @pl.when(code >= 2)
            def _():
                pltpu.make_async_copy(sums[0].at[0], grad_v.at[slot], grad_sem.at[slot]).wait()
                update(grad_v[slot].astype(f32))

        if low < 2:

            @pl.when(code == 1)
            def _():
                at = pl.multiple_of(row_ref[slot], rows)
                update(dot_nn(dmod[pl.ds(at, rows), :], cond[...]))

            @pl.when(code == 0)
            def _():
                update(jnp.zeros((rows, D), f32))

        for source, target in zip(made, outs):
            pltpu.make_async_copy(source.at[slot], target.at[slot], out_sem.at[slot]).start()

    def close(slot, code):
        for source, target in zip(made, outs):
            pltpu.make_async_copy(source.at[slot], target.at[slot], out_sem.at[slot]).wait()

    each(fetch)
    each(work)
    each(close)


def adam(low, high, code, index, row, master, first, second, dmod, cond, sums, chain):
    slots, rows = master.shape[0], master.shape[1]
    any_spec = pl.BlockSpec(memory_space=pltpu.HBM)
    smem, vmem = pl.BlockSpec(memory_space=pltpu.SMEM), pl.BlockSpec(memory_space=pltpu.VMEM)
    kinds = [f32, f32, f32, bf16]
    return pl.pallas_call(
        functools.partial(adam_kernel, low, high, len(sums), bool(chain)),
        in_specs=[smem] * 3 + [any_spec] * 3 + [vmem] * 2 + [any_spec] * (len(sums) + len(chain)),
        out_specs=[any_spec] * 4,
        out_shape=[pltpu.HBM(master.shape, kind) for kind in kinds],
        scratch_shapes=[pltpu.VMEM(master.shape, f32)] * 3
        + [pltpu.VMEM(master.shape, kind) for kind in kinds]
        + [pltpu.VMEM(master.shape, bf16)]
        + [pltpu.SemaphoreType.DMA((slots,))] * 3,
        input_output_aliases={8 + len(sums) + n: n for n in range(len(chain))},
        compiler_params=pltpu.CompilerParams(vmem_limit_bytes=VMEM_ALL),
        cost_estimate=pl.CostEstimate(flops=0, bytes_accessed=slots * rows * D * 15, transcendentals=0),
        name=f"adam_{low}",
    )(code, index, row, *in_hbm((master, first, second)), dmod, cond, *in_hbm(list(sums) + list(chain)))


CHIPS = 8
LOOP = (0, 2, 4, 6, 7, 5, 3, 1)


def swap_cores(value):
    return lax.ppermute(value, BATCH, [(d, d ^ 1) for d in range(2 * CHIPS)])


def along(value, step):
    pairs = [
        (2 * LOOP[n] + core, 2 * LOOP[(n + step) % CHIPS] + core) for n in range(CHIPS) for core in range(2)
    ]
    return lax.ppermute(value, BATCH, pairs)


def hop_kernel(spans, adds, others, spot_ref, *refs):
    n_in = 2 + len(adds)
    terms, came, refs = refs[:2], refs[2:n_in], refs[n_in + others :]
    outs = refs[: len(spans)]
    held, sem, out_sem = refs[len(spans) : -2], refs[-2], refs[-1]
    get, at = [], 0
    parts = []
    for n, (low, high) in enumerate(spans):
        rows = []
        for source in terms:
            span = pl.ds(spot_ref[n] + low, high - low)
            get.append(start(source.at[span], held[at], sem.at[at]))
            rows.append(at)
            at += 1
        parts.append(rows)
    for n, source in enumerate(came):
        get.append(start(source, held[at], sem.at[at]))
        at += 1
    for copy in get:
        copy.wait()
    put = []
    for n, (low, high) in enumerate(spans):
        made = held[at + n]
        for r in range(high - low):
            total = held[parts[n][0]][r].astype(f32) + held[parts[n][1]][r].astype(f32)
            for m, (target, first, last, skip) in enumerate(adds):
                if target == n and first <= r + low < last:
                    total = total + held[2 * len(spans) + m][r + low - skip].astype(f32)
            made[r] = total.astype(bf16)
        put.append(start(made, outs[n], out_sem.at[n]))
    for copy in put:
        copy.wait()


def hop_sums(spots, terms, spans, adds, came, after):
    rows, width = terms[0].shape[1:]
    shapes = [(high - low, rows, width) for low, high in spans]
    scratch = [pltpu.VMEM(shape, bf16) for shape in shapes for _ in range(2)]
    scratch += [pltpu.VMEM(array.shape, bf16) for array in came] + [pltpu.VMEM(shape, bf16) for shape in shapes]
    return pl.pallas_call(
        functools.partial(hop_kernel, spans, adds, len(after)),
        in_specs=[pl.BlockSpec(memory_space=pltpu.SMEM)]
        + [pl.BlockSpec(memory_space=pltpu.HBM)] * 2
        + [pl.BlockSpec(memory_space=pl.ANY)] * (len(came) + len(after)),
        out_specs=[pl.BlockSpec(memory_space=pltpu.HBM)] * len(spans),
        out_shape=[pltpu.HBM(shape, bf16) for shape in shapes],
        scratch_shapes=scratch + [pltpu.SemaphoreType.DMA((8,)), pltpu.SemaphoreType.DMA((2,))],
        compiler_params=pltpu.CompilerParams(vmem_limit_bytes=VMEM_ALL),
        cost_estimate=pl.CostEstimate(flops=0, bytes_accessed=8 * shapes[0][0] * rows * width * 2, transcendentals=0),
        name="hop",
    )(spots, *in_hbm(terms), *came, *after)


class Ring:
    def __init__(self, place, mine, other):
        self.place, self.size, self.left = place, mine.shape[0] // CHIPS, 4
        self.half = self.size // 2
        self.terms = (mine, swap_cores(other))

    def hop(self, after=()):
        n, half, size = self.left, self.half, self.size
        spots = jnp.stack([(self.place + n) % CHIPS, (self.place - n) % CHIPS]) * size
        if n == 4:
            spans, adds, came = [(0, half), (half, size)], [], []
        else:
            spans, came = [(0, size)] * 2, [self.ahead, self.behind]
            adds = [(0, 0, half, 0), (1, half, size, half)] if n == 3 else [(0, 0, size, 0), (1, 0, size, 0)]
        ahead, behind = hop_sums(spots.astype(jnp.int32), self.terms, spans, adds, came, after)
        self.ahead, self.behind = along(ahead, 1), along(behind, -1)
        self.left -= 1

    def held(self, count=2):
        self.count = count
        return list(self.terms[:count])

    def later(self, made):
        self.terms = tuple(made[-self.count :]) + self.terms[self.count :]
        return made[: -self.count]

    def finish(self, after=()):
        spots = jnp.reshape(self.place * self.size, (1,)).astype(jnp.int32)
        adds = [(0, 0, self.size, 0)] * 2
        return hop_sums(spots, self.terms, [(0, self.size)], adds, [self.ahead, self.behind], after)[0]


def time_features(steps_in):
    half_width = D // 2
    freqs = jnp.exp(-math.log(10000.0) * jnp.arange(half_width, dtype=f32) / half_width)
    angles = steps_in.astype(f32)[:, None] * freqs[None, :]
    return jnp.concatenate([jnp.cos(angles), jnp.sin(angles)], axis=1)


def body(tokens, cotangent, loss_weight, timesteps, owners, master, first_moment, second_moment):
    section_index = lax.axis_index(SECTION)
    me = lax.axis_index(BATCH)
    owner_total = lax.axis_size(BATCH)
    slots, panel_rows = master.shape[1], master.shape[2]
    clips = timesteps.shape[0]
    length = tokens.shape[0] // clips
    owner = owners[0]
    panels = owner.shape[0]
    moved = DOWN_END // panel_rows
    cap = min(slots, max(4, (slots * 25 + 30) // 31))
    section = jnp.reshape(section_index, (1,)).astype(jnp.int32)

    number = jnp.arange(panels, dtype=jnp.int32)
    same = (owner[:, None] == owner[None, :]) & (number[None, :] < number[:, None])
    rank = jnp.sum(same.astype(jnp.int32), axis=1)
    first_size = owner_total * cap
    place = jnp.where(
        rank < cap, owner * cap + rank, first_size + owner * (slots - cap) + rank - cap
    )[:moved]
    mine = (owner[None, :] == me) & (
        rank[None, :] == jnp.arange(slots, dtype=jnp.int32)[:, None]
    )
    slot_panel = jnp.sum(jnp.where(mine, number[None, :] + 1, 0), axis=1) - 1
    kind = jnp.where(slot_panel < 0, 0, jnp.where(slot_panel < moved, 1, 2)).astype(jnp.int32)
    grad_row = jnp.where(kind == 2, (slot_panel - moved) * panel_rows, 0).astype(jnp.int32)

    rings = owner_total == 2 * CHIPS
    code, index, slot_code, slot_index, sizes, beyond = routes(owner, rank, mine, me, owner_total, slots, moved)
    low = master[0].astype(bf16)
    gathered = lax.all_gather(low[:cap], BATCH, axis=0, tiled=True)
    spot = jnp.arange(owner_total * clips, dtype=jnp.int32) // clips == me
    news = [jnp.where(spot, jnp.tile(timesteps.astype(f32), owner_total), 0.0)]
    past = jnp.max(jnp.where(number < moved, rank, 0)) >= cap
    news.append(jnp.stack([past, beyond]).astype(f32) + 0.0 * low[0, 0, 0].astype(f32))
    news = lax.pmax(jnp.concatenate(news), (SECTION, BATCH))
    all_steps = news[:-2]
    beyond = news[-1] > 0.5
    sources = [gathered]
    if cap < slots:
        rest_shape = (owner_total * (slots - cap), panel_rows, D)
        sources.append(
            lax.cond(
                news[-2] + 0.0 * gathered[0, 0, 0].astype(f32) > 0.5,
                lambda part: lax.all_gather(part, BATCH, axis=0, tiled=True),
                lambda part: jnp.zeros(rest_shape, bf16),
                low[cap:],
            )
        )
    sheet = assemble(place, sources, moved)

    cond = jax.nn.silu(time_features(all_steps)).astype(bf16)
    clip_total = cond.shape[0]
    share = jnp.einsum("cd,sd->cs", cond, low.reshape(slots * panel_rows, D), preferred_element_type=f32)
    share = lax.all_to_all(
        share.reshape(owner_total, clips, slots * panel_rows), BATCH, split_axis=0, concat_axis=0, tiled=True
    )
    share = share.reshape(owner_total, clips, slots, panel_rows).transpose(1, 0, 2, 3)
    share = share.reshape(clips, owner_total * slots, panel_rows)
    pick = (
        (owner * slots + rank)[moved:, None] == jnp.arange(owner_total * slots, dtype=jnp.int32)[None, :]
    ).astype(f32)
    mod = jnp.einsum("ps,csr->cpr", pick, share, precision=lax.Precision.HIGHEST)
    mod = mod.reshape(clips, 6, D)

    run = functools.partial
    base = dict(clips=clips, length=length, section=section, mod=mod, sheet=sheet)
    firsts, outs = [], None
    for c in range(clips):
        firsts.append(first_forward(c, x=tokens, outs=outs, **base))
        outs = firsts[c][N_OUTS]
    received = [lax.ppermute(f[N_SENT], SECTION, [(0, 1)]) for f in firsts]
    seconds, gin = [], None
    for c in range(clips):
        chain = {n: firsts[c][n] for n in (N_H1, N_O, N_H2, N_Z)} | {N_OUTS: outs, N_GIN: gin}
        seconds.append(second_both(c, loss_weight=loss_weight, x=received[c], g=cotangent, chain=chain, **base))
        outs, gin = seconds[c][N_OUTS], seconds[c][N_GIN]
    received = [lax.ppermute(f[N_SENT], SECTION, [(1, 0)]) for f in seconds]
    every = [dict(f) for f in seconds]

    for c in range(clips):
        chain = {n: every[c][n] for n in BACK_MAKES} | {N_GIN: gin}
        every[c] |= first_back(c, x=tokens, g=received[c], kept=firsts[c], chain=chain, after=every[0][N_DMOD_ATT] if c else mod, **base)
        gin = every[c][N_GIN]

    dmod = [jnp.concatenate([e[N_DMOD_ATT], e[N_DMOD_FFN]]) for e in every]
    dmod = jnp.stack(dmod).reshape(1, clips, 6 * D).astype(bf16)
    dmod = lax.all_to_all(
        jnp.broadcast_to(dmod, (owner_total, clips, 6 * D)), BATCH, split_axis=0, concat_axis=0, tiled=True
    )
    slot_code = jnp.where(kind == 1, slot_code + 2, jnp.where(kind == 2, 1, 0)).astype(jnp.int32)
    update = run(
        adam, code=slot_code, index=slot_index, row=grad_row, master=master[0], first=first_moment[0],
        second=second_moment[0], dmod=dmod.reshape(clip_total, 6 * D).T, cond=cond,
    )
    grads = run(weight_grads, code=code, index=index, every=every, length=length, panel_rows=panel_rows)
    if rings:
        place = me // 4 + (me // 2) % 2 * (CHIPS - 1 - 2 * (me // 4))
        wide = [sizes[1]] * 2 + [sizes[2]]
        first_jobs = ((N_DA, N_O, QKV_END), (N_DQKV, N_H1, 0), (N_DU, N_H2, PROJ_END))
        made = grads(first_jobs, sizes=[sizes[0]] * 2 + wide, thread=[], after=[])
        first = Ring(place, *made[:2])
        made = grads(((N_Z, N_DB, UP_END),), sizes=wide, thread=made[2:], after=[], through=first.held(1))
        made = first.later(made)
        second = Ring(place, *made[:2])
        rest = lax.cond(
            beyond,
            lambda part: lax.psum_scatter(part, BATCH, scatter_dimension=0, tiled=True),
            lambda part: jnp.zeros((slots, panel_rows, D), bf16),
            made[2],
        )
        for n in range(4):
            first.hop(after=[[], [rest], [dmod], []][n])
            second.hop()
        half = first.finish()
        sums = [half, swap_cores(half)]
        results = update(0, 4, sums=sums, chain=[])
        half = second.finish(after=results[3:])
        sums += [half, swap_cores(half), rest]
        results = update(4, 7, sums=sums, chain=results)
    else:
        jobs = ((N_Z, N_DB, UP_END), (N_DU, N_H2, PROJ_END), (N_DA, N_O, QKV_END), (N_DQKV, N_H1, 0))
        (made,) = grads(jobs, sizes=[sizes[0]], thread=[], after=[])
        sums = [lax.psum_scatter(made, BATCH, scatter_dimension=0, tiled=True)]
        results = update(0, 3, sums=sums, chain=[])
    return (outs[None], gin[None], *(r[None] for r in results))


CAPS = (24, 24)


def count_before(flag, group):
    number = jnp.arange(group.shape[0], dtype=jnp.int32)
    before = (group[:, None] == group[None, :]) & (number[None, :] < number[:, None]) & flag[None, :]
    return jnp.sum(before.astype(jnp.int32), axis=1)


def routes(owner, rank, mine, me, owner_total, slots, moved):
    if owner_total != 2 * CHIPS:
        code = jnp.zeros((moved,), jnp.int32)
        return code, (owner * slots + rank)[:moved], jnp.zeros((slots,), jnp.int32), jnp.arange(slots, dtype=jnp.int32), [owner_total * slots], jnp.bool_(False)
    number = jnp.arange(moved, dtype=jnp.int32)
    held, core = owner[:moved], me % 2
    chip = held // 2
    spot = chip // 2 + chip % 2 * (CHIPS - 1 - 2 * (chip // 2))
    per_row = DOWN_END // moved
    down = number >= UP_END // per_row
    order = count_before(~down, chip)
    late = down | (order >= CAPS[0])
    order = jnp.where(late, count_before(late, chip), order)
    rest = late & (order >= CAPS[1])
    half = order % 2
    size = jnp.where(late, CAPS[1] // 2, CAPS[0] // 2)
    index = jnp.where(rest, held * slots + rank[:moved], spot * size + order // 2)
    away = (half != core).astype(jnp.int32)
    code = jnp.where(rest, 4, jnp.where(late, 2 + away, away))
    code = jnp.where(down, code - 2, code).astype(jnp.int32)
    taken = mine[:, :moved].astype(jnp.int32)
    found = jnp.where(rest, 4, 2 * late.astype(jnp.int32) + away)
    slot_code = jnp.sum(taken * found[None, :], axis=1)
    slot_index = jnp.sum(taken * jnp.where(rest, rank[:moved], order // 2)[None, :], axis=1)
    sizes = [CHIPS * cap // 2 for cap in CAPS] + [owner_total * slots]
    return code, index.astype(jnp.int32), slot_code.astype(jnp.int32), slot_index.astype(jnp.int32), sizes, jnp.any(rest)


def solution(mesh):
    placed = (
        P(BATCH, None),
        P(BATCH, None),
        P(BATCH),
        P(BATCH),
        P(SECTION, None),
        P(SECTION, BATCH, None, None),
        P(SECTION, BATCH, None, None),
        P(SECTION, BATCH, None, None),
    )
    return jax.shard_map(
        body,
        mesh=mesh,
        in_specs=placed,
        out_specs=(
            P(SECTION, BATCH, None),
            P(SECTION, BATCH, None),
            P(SECTION, BATCH, None, None),
            P(SECTION, BATCH, None, None),
            P(SECTION, BATCH, None, None),
            P(SECTION, BATCH, None, None),
        ),
        check_vma=False,
    )
```

```python
import functools
import math

import jax
import jax.numpy as jnp
from jax import lax
from jax.experimental import pallas as pl
from jax.experimental.pallas import tpu as pltpu
from jax.sharding import PartitionSpec as P

D = 768
HEADS = 12
HEAD_DIM = 64
FF = 3072
STEP = 10
QKV_END = 3 * D
PROJ_END = 4 * D
UP_END = 4 * D + FF
DOWN_END = 4 * D + 2 * FF

norm_eps = 1e-06
adam_eps = 1e-08
learn_rate = 0.03
decay_rate = 0.1
beta_one = 0.5
beta_two = 0.5

bf16 = jnp.bfloat16
f32 = jnp.float32
SECTION, BATCH = "section", "batch"
VMEM_LIMIT = 46 * 1024 * 1024
VMEM_ALL = 58 * 1024 * 1024
ROWS = 128
GELU_C = math.sqrt(2.0 / math.pi)


def dot_nn(a, b):
    return lax.dot_general(a, b, (((1,), (0,)), ((), ())), preferred_element_type=f32)


def dot_nt(a, b):
    return lax.dot_general(a, b, (((1,), (1,)), ((), ())), preferred_element_type=f32)


def dot_tn(a, b):
    return lax.dot_general(a, b, (((0,), (0,)), ((), ())), preferred_element_type=f32)


def in_hbm(arrays):
    return [pltpu.with_memory_space_constraint(a, pltpu.HBM) for a in arrays]


def start(src, dst, sem):
    copy = pltpu.make_async_copy(src, dst, sem)
    copy.start()
    return copy


def norm(values):
    average = jnp.mean(values, axis=-1, keepdims=True)
    centred = values - average
    variance = jnp.mean(centred * centred, axis=-1, keepdims=True)
    inverse = lax.rsqrt(variance + norm_eps)
    return centred * inverse, inverse


def norm_back(grad, values, scale_row):
    normed, inverse = norm(values)
    dn = grad * (1.0 + scale_row)
    mean_one = jnp.mean(dn, axis=-1, keepdims=True)
    mean_two = jnp.mean(dn * normed, axis=-1, keepdims=True)
    dx = inverse * (dn - mean_one - normed * mean_two)
    return dx, jnp.sum(grad, axis=0, keepdims=True), jnp.sum(grad * normed, axis=0, keepdims=True)


def gelu_both(u):
    square = u * u
    half = 0.5 * jnp.tanh(u * (square * (0.044715 * GELU_C) + GELU_C)) + 0.5
    bend = u * (square * (6.0 * 0.044715 * GELU_C) + 2.0 * GELU_C)
    return u * half, half + half * (1.0 - half) * bend


def assemble_kernel(panels, first_size, index_ref, *refs):
    sources, sheet, sem = refs[:-2], refs[-2], refs[-1]
    rows = sheet.shape[0] // panels

    @pl.loop(0, panels, unroll=4)
    def _(p):
        where = index_ref[p]
        target = sheet.at[pl.ds(pl.multiple_of(p * rows, rows), rows)]
        if len(sources) == 1:
            pltpu.make_async_copy(sources[0].at[where], target, sem).start()
        else:

            @pl.when(where < first_size)
            def _():
                pltpu.make_async_copy(sources[0].at[where], target, sem).start()

            @pl.when(where >= first_size)
            def _():
                pltpu.make_async_copy(sources[1].at[where - first_size], target, sem).start()

    pltpu.make_async_copy(sheet, sheet, sem).wait()


def assemble(index, sources, panels):
    first_size = sources[0].shape[0]
    rows = sources[0].shape[1]
    return pl.pallas_call(
        functools.partial(assemble_kernel, panels, first_size),
        out_shape=pltpu.VMEM((panels * rows, D), bf16),
        in_specs=[pl.BlockSpec(memory_space=pltpu.SMEM)]
        + [pl.BlockSpec(memory_space=pltpu.HBM)] * len(sources),
        out_specs=pl.BlockSpec(memory_space=pltpu.VMEM),
        scratch_shapes=[pltpu.SemaphoreType.DMA],
        compiler_params=pltpu.CompilerParams(vmem_limit_bytes=VMEM_LIMIT),
        cost_estimate=pl.CostEstimate(flops=0, bytes_accessed=2 * panels * rows * D, transcendentals=0),
        name="assemble",
    )(index, *in_hbm(sources))


(
    N_XIN,
    N_H1,
    N_QKV,
    N_LSE,
    N_O,
    N_A,
    N_X1,
    N_H2,
    N_SLOPE,
    N_Z,
    N_B,
    N_OUT,
    N_DB,
    N_DU,
    N_DA,
    N_DX1,
    N_DMOD_FFN,
    N_DQKV,
    N_DMOD_ATT,
    N_G,
    N_SENT,
    N_DO,
    N_ACC,
    N_LSE_COLS,
    N_OUTS,
    N_GIN,
    N_MOD,
    N_X,
    N_AFTER,
    N_SECTION,
    N_LOSS,
) = range(31)


TILE = D
TILES = FF // TILE
PAIRS = HEADS // 2


def shapes_of(length):
    return {
        N_XIN: ((length, D), bf16),
        N_H1: ((length, D), bf16),
        N_QKV: ((length, 3 * D), bf16),
        N_LSE: ((16, length), f32),
        N_O: ((length, D), bf16),
        N_A: ((length, D), bf16),
        N_X1: ((length, D), f32),
        N_H2: ((length, D), bf16),
        N_SLOPE: ((length, FF), f32),
        N_Z: ((length, FF), bf16),
        N_B: ((length, D), bf16),
        N_OUT: ((length, D), bf16),
        N_DB: ((length, D), bf16),
        N_DU: ((length, FF), bf16),
        N_DA: ((length, D), bf16),
        N_DX1: ((length, D), f32),
        N_DMOD_FFN: ((4, D), f32),
        N_DQKV: ((length, 3 * D), bf16),
        N_DMOD_ATT: ((2, D), f32),
        N_G: ((length, D), bf16),
        N_SENT: ((length, D), bf16),
        N_DO: ((length, D), bf16),
        N_ACC: ((length, D), f32),
        N_LSE_COLS: ((length, 128), f32),
    }


def blocks_of(length):
    return [pl.ds(r, ROWS) for r in range(0, length, ROWS)]


def low_half():
    return lax.broadcasted_iota(jnp.int32, (1, 128), 1) < HEAD_DIM


def forward_qkv(v, w_qkv, row, length):
    for block in blocks_of(length):
        normed, _ = norm(v[N_XIN][block, :].astype(f32))
        v[N_H1][block, :] = (normed * (1.0 + row(1)) + row(0)).astype(bf16)
    for n in range(3):
        part = dot_nt(v[N_H1][...], w_qkv(n))
        v[N_QKV][:, n * D : (n + 1) * D] = part.astype(bf16)


def forward_attention(v, length):
    low_lanes = low_half()
    room = FF // length
    columns = lax.broadcasted_iota(jnp.int32, (1, 128), 1)

    def scores(head):
        at = slice(head // 2 * 128, head // 2 * 128 + 128)
        q = v[N_QKV][:, at] * jnp.asarray(HEAD_DIM ** (-0.5), bf16)
        qh = jnp.where(low_lanes if head % 2 == 0 else ~low_lanes, q, jnp.zeros_like(q))
        first = head % room * length
        v[N_SLOPE][:, first : first + length] = dot_nt(qh, v[N_QKV][:, D + at.start : D + at.stop])

    def softmax(head):
        span = slice(head % room * length, head % room * length + length)
        for block in blocks_of(length):
            s = v[N_SLOPE][block, span]
            top = jnp.max(s, axis=-1, keepdims=True)
            e = jnp.exp(s - top)
            total = jnp.sum(e, axis=-1, keepdims=True)
            v[N_Z][block, span] = (e * (1.0 / total)).astype(bf16)
            line = top + jnp.log(total)
            v[N_LSE_COLS][block, :] = jnp.where(columns == head, line, v[N_LSE_COLS][block, :]) if head else jnp.where(columns == 0, line, 0.0)

    def mix(head):
        at = slice(2 * D + head // 2 * 128, 2 * D + head // 2 * 128 + 128)
        span = slice(head % room * length, head % room * length + length)
        return dot_nn(v[N_Z][:, span], v[N_QKV][:, at])

    scores(0)
    mixed = [None] * HEADS
    for head in range(HEADS):
        if head + 1 < HEADS:
            scores(head + 1)
        softmax(head)
        mixed[head] = mix(head)
        if head % 2:
            at = slice(head // 2 * 128, head // 2 * 128 + 128)
            v[N_O][:, at] = jnp.where(low_lanes, mixed[head - 1], mixed[head]).astype(bf16)
    v[N_LSE][...] = v[N_LSE_COLS][...].T[:16, :]


def forward_proj(v, w_proj, row, length):
    v[N_ACC][...] = dot_nt(v[N_O][...], w_proj)
    for block in blocks_of(length):
        branch = v[N_ACC][block, :]
        v[N_A][block, :] = branch.astype(bf16)
        middle = v[N_XIN][block, :].astype(f32) + row(2) * branch
        v[N_X1][block, :] = middle
        normed, _ = norm(middle)
        v[N_H2][block, :] = (normed * (1.0 + row(4)) + row(3)).astype(bf16)


def forward_ffn(v, w_up, w_down, row, length, after):
    for n in range(TILES):
        span = slice(n * TILE, (n + 1) * TILE)
        v[N_SLOPE][:, span] = dot_nt(v[N_H2][...], w_up(n))
        for block in blocks_of(length):
            value, slope = gelu_both(v[N_SLOPE][block, span])
            v[N_Z][block, span] = value.astype(bf16)
            v[N_SLOPE][block, span] = slope
        part = dot_nn(v[N_Z][:, span], w_down(n))
        if n:
            v[N_ACC][...] += part
        else:
            v[N_ACC][...] = part
        after(n)
    for block in blocks_of(length):
        branch = v[N_ACC][block, :]
        v[N_B][block, :] = branch.astype(bf16)
        v[N_OUT][block, :] = (v[N_X1][block, :] + row(5) * branch).astype(bf16)


def back_gate(v, row, length, scale):
    gate_two = jnp.zeros((1, D), f32)
    for block in blocks_of(length):
        g = v[N_G][block, :].astype(f32)
        if scale is not None:
            g = g * scale
        v[N_DX1][block, :] = g
        v[N_DB][block, :] = (row(5) * g).astype(bf16)
        gate_two += jnp.sum(g * v[N_B][block, :].astype(f32), axis=0, keepdims=True)
    v[N_DMOD_FFN][3:4, :] = gate_two


def back_ffn_part(v, w_up, w_down, row, length, before, after):
    for n in range(TILES):
        span = slice(n * TILE, (n + 1) * TILE)
        before(n)
        dz = dot_nt(v[N_DB][...], w_down(n))
        v[N_DU][:, span] = (dz * v[N_SLOPE][:, span]).astype(bf16)
        part = dot_nn(v[N_DU][:, span], w_up(n))
        if n:
            v[N_ACC][...] += part
        else:
            v[N_ACC][...] = part
        after(n)


def back_middle(v, row, length):
    shift_two = jnp.zeros((1, D), f32)
    scale_two = jnp.zeros((1, D), f32)
    gate_one = jnp.zeros((1, D), f32)
    for block in blocks_of(length):
        dx, shift_part, scale_part = norm_back(v[N_ACC][block, :], v[N_X1][block, :], row(4))
        total = v[N_DX1][block, :] + dx
        v[N_DX1][block, :] = total
        shift_two += shift_part
        scale_two += scale_part
        gate_one += jnp.sum(total * v[N_A][block, :].astype(f32), axis=0, keepdims=True)
        v[N_DA][block, :] = (row(2) * total).astype(bf16)
    v[N_DMOD_FFN][0:1, :] = gate_one
    v[N_DMOD_FFN][1:2, :] = shift_two
    v[N_DMOD_FFN][2:3, :] = scale_two


def back_attention(v, w_proj, length):
    v[N_DO][...] = dot_nn(v[N_DA][...], w_proj).astype(bf16)
    low_lanes = low_half()
    scale = HEAD_DIM ** (-0.5)

    def parts(head):
        at = head // 2 * 128
        keep = lambda a: jnp.where(low_lanes if head % 2 == 0 else ~low_lanes, a, jnp.zeros_like(a))
        qh, doh = keep(v[N_QKV][:, at : at + 128]), keep(v[N_DO][:, at : at + 128])
        kh = keep(v[N_QKV][:, D + at : D + at + 128])
        return qh, kh, doh

    def first(head):
        at = head // 2 * 128
        qh, kh, doh = parts(head)
        st = dot_nt(v[N_QKV][:, D + at : D + at + 128], qh * jnp.asarray(scale, bf16))
        dpt = dot_nt(v[N_QKV][:, 2 * D + at : 2 * D + at + 128], doh)
        return st, dpt, qh, kh, doh

    def rest(head, st, dpt, qh, kh, doh):
        pt = jnp.exp(st - v[N_LSE][head : head + 1, :])
        dv = dot_nn(pt.astype(bf16), doh)
        inner = jnp.sum(dpt * pt, axis=0, keepdims=True)
        drt = (pt * (dpt - inner) * scale).astype(bf16)
        return dot_tn(drt, kh), dot_nn(drt, qh), dv

    ahead = first(0)
    made = None
    for head in range(HEADS):
        now = ahead
        if head + 1 < HEADS:
            ahead = first(head + 1)
        made_now = rest(head, *now)
        if head % 2:
            for n in range(3):
                at = n * D + head // 2 * 128
                v[N_DQKV][:, at : at + 128] = (made[n] + made_now[n]).astype(bf16)
        made = made_now


def back_input(v, w_qkv, row, length):
    v[N_ACC][...] = dot_nn(v[N_DQKV][...], w_qkv)
    shift_one = jnp.zeros((1, D), f32)
    scale_one = jnp.zeros((1, D), f32)
    for block in blocks_of(length):
        dx, shift_part, scale_part = norm_back(v[N_ACC][block, :], v[N_XIN][block, :].astype(f32), row(1))
        total = v[N_DX1][block, :] + dx
        v[N_DX1][block, :] = total
        v[N_SENT][block, :] = total.astype(bf16)
        shift_one += shift_part
        scale_one += scale_part
    v[N_DMOD_ATT][0:1, :] = shift_one
    v[N_DMOD_ATT][1:2, :] = scale_one


class Mover:
    def __init__(self, sems):
        self.sems, self.used, self.coming, self.going = sems, 0, {}, []

    def start(self, src, dst):
        copy = pltpu.make_async_copy(src, dst, self.sems.at[self.used])
        self.used += 1
        copy.start()
        return copy

    def fetch(self, name, src, dst):
        self.coming[name] = self.start(src, dst)

    def need(self, *names):
        for name in names:
            if name in self.coming:
                self.coming.pop(name).wait()

    def save(self, src, dst):
        self.going.append(self.start(src, dst))

    def finish(self):
        assert not self.coming
        for copy in self.going:
            copy.wait()


SEMS = 48


def call_block(kernel, name, want, clip, length, smem, sheet, read, write, hold, shared, chain, flops, moved, loose=None):
    any_spec = pl.BlockSpec(memory_space=pltpu.HBM)
    shapes = shapes_of(length)
    s_names, r_names, w_names = list(smem), list(read), list(write)
    chained = [n for n in w_names if chain.get(n) is not None]
    operands = [smem[n] for n in s_names] + [pltpu.with_memory_space_constraint(sheet, pltpu.VMEM)]
    operands += [read[n] if n == loose else in_hbm([read[n]])[0] for n in r_names]
    aliases = {len(operands) + i: w_names.index(n) for i, n in enumerate(chained)}
    operands += in_hbm([chain[n] for n in chained])

    def run(*refs):
        refs = list(refs)
        take = lambda names: dict(zip(names, [refs.pop(0) for _ in names]))
        s, w, r = take(s_names), refs.pop(0), take(r_names)
        take(chained)
        o = take(w_names)
        v = take(hold)
        v |= {n: v[other] for n, other in shared.items()}
        m, sems = refs

        @pl.when(s[N_SECTION][0] == want)
        def _():
            kernel(clip, length, s, m, r, o, v, w, Mover(sems))

    results = pl.pallas_call(
        run,
        out_shape=[pltpu.HBM(*write[n]) for n in w_names],
        in_specs=[pl.BlockSpec(memory_space=pltpu.SMEM)] * len(s_names)
        + [pl.BlockSpec(memory_space=pltpu.VMEM)]
        + [any_spec] * (len(r_names) + len(chained)),
        out_specs=[any_spec] * len(w_names),
        scratch_shapes=[pltpu.VMEM(*shapes[n]) for n in hold]
        + [pltpu.VMEM((6, D), f32), pltpu.SemaphoreType.DMA((SEMS,))],
        input_output_aliases=aliases,
        compiler_params=pltpu.CompilerParams(vmem_limit_bytes=VMEM_LIMIT),
        cost_estimate=pl.CostEstimate(flops=flops, bytes_accessed=moved, transcendentals=0),
        name=f"{name}_{clip}",
    )(*operands)
    return dict(zip(w_names, results))


def mod_row(m):
    return lambda n: m[n : n + 1, :]


def forward_body(clip, length, x_offset, m, r, v, w, mover, keep):
    row = mod_row(m)
    mover.fetch(N_MOD, r[N_MOD].at[clip], m)
    mover.fetch(N_XIN, r[N_X].at[pl.ds(x_offset, length)], v[N_XIN])
    mover.need(N_MOD, N_XIN)
    forward_qkv(v, lambda n: w[n * D : (n + 1) * D, :], row, length)
    keep(N_H1)
    keep(N_QKV)
    forward_attention(v, length)
    keep(N_LSE)
    keep(N_O)
    forward_proj(v, w[QKV_END:PROJ_END, :], row, length)
    keep(N_A)
    keep(N_X1)
    keep(N_H2)
    forward_ffn(
        v,
        lambda n: w[PROJ_END + n * D : PROJ_END + (n + 1) * D, :],
        lambda n: w[UP_END + n * D : UP_END + (n + 1) * D, :],
        row,
        length,
        lambda n: (keep(N_SLOPE, n), keep(N_Z, n)),
    )
    keep(N_B)


def saver(mover, v, o):
    def keep(name, n=None):
        if name not in o:
            return
        if n is None:
            mover.save(v[name], o[name])
        else:
            span = pl.ds(n * TILE, TILE)
            mover.save(v[name].at[:, span], o[name].at[:, span])

    return keep


FIRST_KEEP = (N_H1, N_QKV, N_LSE, N_O, N_A, N_X1, N_H2, N_SLOPE, N_Z, N_B)
BOTH_KEEP = (N_H1, N_O, N_H2, N_Z, N_DB, N_DU, N_DA, N_DQKV, N_DMOD_FFN, N_DMOD_ATT)


def first_forward(clip, clips, length, section, mod, x, sheet, outs):
    def kernel(clip, length, s, m, r, o, v, w, mover):
        forward_body(clip, length, clip * length, m, r, v, w, mover, saver(mover, v, o))
        mover.save(v[N_OUT], o[N_SENT])
        mover.save(v[N_OUT], o[N_OUTS].at[pl.ds(clip * length, length)])
        mover.finish()

    shapes = shapes_of(length)
    write = {n: shapes[n] for n in FIRST_KEEP}
    write |= {N_OUTS: ((clips * length, D), bf16), N_SENT: ((length, D), bf16)}
    hold = FIRST_KEEP + (N_XIN, N_OUT, N_ACC, N_LSE_COLS)
    return call_block(
        kernel, "first_forward", 0, clip, length, {N_SECTION: section}, sheet, {N_MOD: mod, N_X: x},
        write, hold, {}, {N_OUTS: outs}, 17 * 10**9, 30 << 20,
    )


def second_both(clip, clips, length, section, loss_weight, mod, x, g, sheet, chain):
    def kernel(clip, length, s, m, r, o, v, w, mover):
        keep = saver(mover, v, o)
        row = mod_row(m)
        forward_body(clip, length, 0, m, r, v, w, mover, keep)
        mover.fetch(N_G, r[N_G].at[pl.ds(clip * length, length)], v[N_G])
        mover.save(v[N_OUT], o[N_OUTS].at[pl.ds(clip * length, length)])
        mover.need(N_G)
        back_gate(v, row, length, s[N_LOSS][clip])
        keep(N_DB)
        back_ffn_part(
            v,
            lambda n: w[PROJ_END + n * D : PROJ_END + (n + 1) * D, :],
            lambda n: w[UP_END + n * D : UP_END + (n + 1) * D, :],
            row, length, lambda n: None, lambda n: keep(N_DU, n),
        )
        back_middle(v, row, length)
        keep(N_DA)
        keep(N_DMOD_FFN)
        back_attention(v, w[QKV_END:PROJ_END, :], length)
        keep(N_DQKV)
        back_input(v, w[0:QKV_END, :], row, length)
        mover.save(v[N_SENT], o[N_SENT])
        keep(N_DMOD_ATT)
        mover.save(v[N_DX1], o[N_GIN].at[pl.ds(clip * length, length)])
        mover.finish()

    shapes = shapes_of(length)
    write = {n: shapes[n] for n in BOTH_KEEP}
    write |= {N_OUTS: ((clips * length, D), bf16), N_GIN: ((clips * length, D), f32), N_SENT: ((length, D), bf16)}
    hold = (N_XIN, N_H1, N_QKV, N_LSE, N_O, N_A, N_X1, N_H2, N_SLOPE, N_Z, N_B, N_OUT, N_DB, N_DU, N_DX1)
    hold += (N_DMOD_FFN, N_DMOD_ATT, N_G, N_ACC, N_LSE_COLS)
    shared = {N_DQKV: N_QKV, N_DO: N_B, N_DA: N_A, N_SENT: N_G}
    return call_block(
        kernel, "second_both", 1, clip, length, {N_SECTION: section, N_LOSS: loss_weight},  sheet,
        {N_MOD: mod, N_X: x, N_G: g}, write, hold, shared, chain, 40 * 10**9, 40 << 20, N_X,
    )


BACK_MAKES = (N_DB, N_DU, N_DA, N_DQKV, N_DMOD_FFN, N_DMOD_ATT)


def first_back(clip, clips, length, section, mod, x, g, sheet, kept, chain, after):
    def kernel(clip, length, s, m, r, o, v, w, mover):
        keep = saver(mover, v, o)
        row = mod_row(m)
        mover.fetch(N_MOD, r[N_MOD].at[clip], m)
        mover.fetch(N_G, r[N_G], v[N_G])
        mover.fetch(N_B, r[N_B], v[N_B])
        for n in range(TILES):
            span = pl.ds(n * TILE, TILE)
            mover.fetch((N_SLOPE, n), r[N_SLOPE].at[:, span], v[N_SLOPE].at[:, span])
        for name in (N_X1, N_A, N_QKV, N_LSE):
            mover.fetch(name, r[name], v[name])
        mover.fetch(N_XIN, r[N_X].at[pl.ds(clip * length, length)], v[N_XIN])
        mover.need(N_MOD, N_G, N_B)
        back_gate(v, row, length, None)
        keep(N_DB)
        back_ffn_part(
            v,
            lambda n: w[PROJ_END + n * D : PROJ_END + (n + 1) * D, :],
            lambda n: w[UP_END + n * D : UP_END + (n + 1) * D, :],
            row, length, lambda n: mover.need((N_SLOPE, n)), lambda n: keep(N_DU, n),
        )
        mover.need(N_X1, N_A)
        back_middle(v, row, length)
        keep(N_DA)
        keep(N_DMOD_FFN)
        mover.need(N_QKV, N_LSE)
        back_attention(v, w[QKV_END:PROJ_END, :], length)
        keep(N_DQKV)
        mover.need(N_XIN)
        back_input(v, w[0:QKV_END, :], row, length)
        keep(N_DMOD_ATT)
        mover.save(v[N_DX1], o[N_GIN].at[pl.ds(clip * length, length)])
        mover.finish()

    shapes = shapes_of(length)
    read = {N_MOD: mod, N_X: x, N_G: g} | {n: kept[n] for n in (N_B, N_SLOPE, N_X1, N_A, N_QKV, N_LSE)}
    read[N_AFTER] = after
    write = {n: shapes[n] for n in BACK_MAKES} | {N_GIN: ((clips * length, D), f32)}
    hold = (N_G, N_B, N_SLOPE, N_X1, N_A, N_QKV, N_LSE, N_XIN, N_DB, N_DU, N_DX1, N_DMOD_FFN, N_DMOD_ATT, N_ACC)
    shared = {N_DQKV: N_QKV, N_DO: N_B, N_DA: N_A, N_SENT: N_G}
    return call_block(
        kernel, "first_back", 0, clip, length, {N_SECTION: section}, sheet, read,
        write, hold, shared, chain, 25 * 10**9, 30 << 20, N_G,
    )


def grads_kernel(jobs, clips, length, panel_rows, plain, added, own, passed, others, code_ref, index_ref, *refs):
    count = 2 * len(jobs) * clips
    sources, partial = refs[:count], refs[count + others - 1]
    refs = refs[count + others :]
    outs = refs[:own]
    scratch = refs[own + passed :]
    values = scratch[: 2 * len(jobs)]
    tile_v, add_v, in_sem, add_sem, out_sem = scratch[2 * len(jobs) :]
    per_tile = D // panel_rows
    tiles = []
    for n, (left, right, base) in enumerate(jobs):
        tiles += [(n, column, base + column) for column in range(0, values[2 * n].shape[1], D)]
    get, more = {}, {}

    def fetch(n, column):
        get[n, column] = [
            start(
                sources[n * clips + c].at[:, pl.ds(column, D)],
                values[n].at[pl.ds(c * length, length), pl.ds(column, D)],
                in_sem.at[len(get), c],
            )
            for c in range(clips)
        ]

    def fetch_tile(t):
        if t < len(tiles):
            n, column, _ = tiles[t]
            if column == 0:
                fetch(2 * n + 1, 0)
            fetch(2 * n, column)
            if added:
                first_panel = tiles[t][2] // panel_rows
                more[t] = start(partial.at[pl.ds(first_panel, per_tile)], add_v.at[t % 4], add_sem.at[t % 4])

    for t in range(3):
        fetch_tile(t)
    def drain(slot):
        pltpu.make_async_copy(outs[-1].at[pl.ds(0, per_tile)], tile_v.at[slot], out_sem.at[slot]).wait()

    for t, (n, column, first_row) in enumerate(tiles):
        slot = t % 2
        if column == 0:
            for copy in get[2 * n + 1, 0]:
                copy.wait()
        for copy in get[2 * n, column]:
            copy.wait()
        fetch_tile(t + 3)
        if t >= 2:
            drain(slot)
        part = dot_tn(values[2 * n][:, column : column + D], values[2 * n + 1][...])
        if added:
            more[t].wait()
            part = part + add_v[t % 4].reshape(D, D).astype(f32)
        tile_v[slot, :, :, :] = part.astype(bf16).reshape(per_tile, panel_rows, D)
        if plain:
            first_panel = first_row // panel_rows
            pltpu.make_async_copy(tile_v.at[slot], outs[0].at[pl.ds(first_panel, per_tile)], out_sem.at[slot]).start()
            continue

        @pl.loop(0, per_tile)
        def _(p):
            code = code_ref[first_row // panel_rows + p]
            where = index_ref[first_row // panel_rows + p]

            def put(numbers):
                for n_out in numbers:

                    @pl.when(code == n_out)
                    def _():
                        pltpu.make_async_copy(tile_v.at[slot, p], outs[n_out].at[where], out_sem.at[slot]).start()

            put(range(min(2, own)))
            if own > 2:

                @pl.when(code >= 2)
                def _():
                    put(range(2, own))

    for slot in range(min(2, len(tiles))):
        drain(slot)


def weight_grads(jobs, code, index, every, length, panel_rows, sizes, thread=(), after=(), through=(), partial=None, plain=False):
    clips = len(every)
    any_spec = pl.BlockSpec(memory_space=pltpu.HBM)
    operands, scratch = [code, index], []
    for left, right, _ in jobs:
        for name in (left, right):
            arrays = [every[c][name] for c in range(clips)]
            operands += arrays
            scratch.append(pltpu.VMEM((clips * length, arrays[0].shape[1]), bf16))
    aliases = {}
    for n, array in enumerate(thread):
        aliases[len(operands)] = len(sizes) - len(thread) + n
        operands.append(array)
    passed = [pltpu.HBM(a.shape, a.dtype) for a in through]
    for n, array in enumerate(through):
        aliases[len(operands)] = len(sizes) + n
        operands.append(array)
    operands += after
    if partial is not None:
        operands.append(partial)
    others = len(operands) - 2 - 2 * len(jobs) * clips
    width = sum(s.shape[1] for s in scratch[0::2])
    return pl.pallas_call(
        functools.partial(
            grads_kernel, jobs, clips, length, panel_rows, plain, partial is not None, len(sizes), len(passed), others
        ),
        out_shape=[pltpu.HBM((size, panel_rows, D), bf16) for size in sizes] + passed,
        in_specs=[pl.BlockSpec(memory_space=pltpu.SMEM)] * 2 + [any_spec] * (len(operands) - 2),
        out_specs=[any_spec] * (len(sizes) + len(passed)),
        scratch_shapes=scratch
        + [
            pltpu.VMEM((2, D // panel_rows, panel_rows, D), bf16),
            pltpu.VMEM((4 if partial is not None else 1, D // panel_rows, panel_rows, D), bf16),
            pltpu.SemaphoreType.DMA((width // D + len(jobs), clips)),
            pltpu.SemaphoreType.DMA((4,)),
            pltpu.SemaphoreType.DMA((2,)),
        ],
        input_output_aliases=aliases,
        compiler_params=pltpu.CompilerParams(vmem_limit_bytes=26 * 1024 * 1024 if plain else VMEM_ALL),
        cost_estimate=pl.CostEstimate(
            flops=4 * clips * length * width * D, bytes_accessed=12 << 20, transcendentals=0
        ),
        name=f"grads_{jobs[0][2]}_{plain:d}",
    )(*operands[:2], *in_hbm(operands[2:]))


def adam_kernel(low, high, n_sums, chained, code_ref, index_ref, row_ref, master, first, second, dmod, cond, *refs):
    sums = refs[:n_sums]
    refs = refs[n_sums + (4 if chained else 0) :]
    outs, held, made = refs[:4], refs[4:7], refs[7:11]
    grad_v, in_sem, grad_sem, out_sem = refs[11:]
    slots, rows = master.shape[0], master.shape[1]
    sources = (master, first, second)

    def each(step):
        @pl.loop(0, slots)
        def _(slot):
            code = code_ref[slot]

            @pl.when((code >= low) & (code < high))
            def _():
                step(slot, code)

    def fetch(slot, code):
        for source, target in zip(sources, held):
            pltpu.make_async_copy(source.at[slot], target.at[slot], in_sem.at[slot]).start()
        for n in range(max(low, 2), min(high, n_sums + 2)):

            @pl.when(code == n)
            def _():
                pltpu.make_async_copy(sums[n - 2].at[index_ref[slot]], grad_v.at[slot], grad_sem.at[slot]).start()

    def work(slot, code):
        for source, target in zip(sources, held):
            pltpu.make_async_copy(source.at[slot], target.at[slot], in_sem.at[slot]).wait()

        def update(grad):
            first_next = beta_one * held[1][slot] + (1.0 - beta_one) * grad
            second_next = beta_two * held[2][slot] + (1.0 - beta_two) * grad * grad
            first_hat = first_next / (1.0 - beta_one**STEP)
            second_hat = second_next / (1.0 - beta_two**STEP)
            value = held[0][slot] - learn_rate * (
                first_hat / (jnp.sqrt(second_hat) + adam_eps) + decay_rate * held[0][slot]
            )
            made[0][slot] = value
            made[1][slot] = first_next
            made[2][slot] = second_next
            made[3][slot] = value.astype(bf16)

        if high > 2:

            @pl.when(code >= 2)
            def _():
                pltpu.make_async_copy(sums[0].at[0], grad_v.at[slot], grad_sem.at[slot]).wait()
                update(grad_v[slot].astype(f32))

        if low < 2:

            @pl.when(code == 1)
            def _():
                at = pl.multiple_of(row_ref[slot], rows)
                update(dot_nn(dmod[pl.ds(at, rows), :], cond[...]))

            @pl.when(code == 0)
            def _():
                update(jnp.zeros((rows, D), f32))

        for source, target in zip(made, outs):
            pltpu.make_async_copy(source.at[slot], target.at[slot], out_sem.at[slot]).start()

    def close(slot, code):
        for source, target in zip(made, outs):
            pltpu.make_async_copy(source.at[slot], target.at[slot], out_sem.at[slot]).wait()

    each(fetch)
    each(work)
    each(close)


def adam(low, high, code, index, row, master, first, second, dmod, cond, sums, chain):
    slots, rows = master.shape[0], master.shape[1]
    any_spec = pl.BlockSpec(memory_space=pltpu.HBM)
    smem, vmem = pl.BlockSpec(memory_space=pltpu.SMEM), pl.BlockSpec(memory_space=pltpu.VMEM)
    kinds = [f32, f32, f32, bf16]
    return pl.pallas_call(
        functools.partial(adam_kernel, low, high, len(sums), bool(chain)),
        in_specs=[smem] * 3 + [any_spec] * 3 + [vmem] * 2 + [any_spec] * (len(sums) + len(chain)),
        out_specs=[any_spec] * 4,
        out_shape=[pltpu.HBM(master.shape, kind) for kind in kinds],
        scratch_shapes=[pltpu.VMEM(master.shape, f32)] * 3
        + [pltpu.VMEM(master.shape, kind) for kind in kinds]
        + [pltpu.VMEM(master.shape, bf16)]
        + [pltpu.SemaphoreType.DMA((slots,))] * 3,
        input_output_aliases={8 + len(sums) + n: n for n in range(len(chain))},
        compiler_params=pltpu.CompilerParams(vmem_limit_bytes=VMEM_ALL),
        cost_estimate=pl.CostEstimate(flops=0, bytes_accessed=slots * rows * D * 15, transcendentals=0),
        name=f"adam_{low}",
    )(code, index, row, *in_hbm((master, first, second)), dmod, cond, *in_hbm(list(sums) + list(chain)))


CHIPS = 8
LOOP = (0, 2, 4, 6, 7, 5, 3, 1)


def swap_cores(value):
    return lax.ppermute(value, BATCH, [(d, d ^ 1) for d in range(2 * CHIPS)])


def along(value, step):
    pairs = [
        (2 * LOOP[n] + core, 2 * LOOP[(n + step) % CHIPS] + core) for n in range(CHIPS) for core in range(2)
    ]
    return lax.ppermute(value, BATCH, pairs)


def hop_kernel(spans, adds, others, spot_ref, *refs):
    n_in = 2 + len(adds)
    terms, came, refs = refs[:2], refs[2:n_in], refs[n_in + others :]
    outs = refs[: len(spans)]
    held, sem, out_sem = refs[len(spans) : -2], refs[-2], refs[-1]
    get, at = [], 0
    parts = []
    for n, (low, high) in enumerate(spans):
        rows = []
        for source in terms:
            span = pl.ds(spot_ref[n] + low, high - low)
            get.append(start(source.at[span], held[at], sem.at[at]))
            rows.append(at)
            at += 1
        parts.append(rows)
    for n, source in enumerate(came):
        get.append(start(source, held[at], sem.at[at]))
        at += 1
    for copy in get:
        copy.wait()
    put = []
    for n, (low, high) in enumerate(spans):
        made = held[at + n]
        for r in range(high - low):
            total = held[parts[n][0]][r].astype(f32) + held[parts[n][1]][r].astype(f32)
            for m, (target, first, last, skip) in enumerate(adds):
                if target == n and first <= r + low < last:
                    total = total + held[2 * len(spans) + m][r + low - skip].astype(f32)
            made[r] = total.astype(bf16)
        put.append(start(made, outs[n], out_sem.at[n]))
    for copy in put:
        copy.wait()


def hop_sums(spots, terms, spans, adds, came, after):
    rows, width = terms[0].shape[1:]
    shapes = [(high - low, rows, width) for low, high in spans]
    scratch = [pltpu.VMEM(shape, bf16) for shape in shapes for _ in range(2)]
    scratch += [pltpu.VMEM(array.shape, bf16) for array in came] + [pltpu.VMEM(shape, bf16) for shape in shapes]
    return pl.pallas_call(
        functools.partial(hop_kernel, spans, adds, len(after)),
        in_specs=[pl.BlockSpec(memory_space=pltpu.SMEM)]
        + [pl.BlockSpec(memory_space=pltpu.HBM)] * 2
        + [pl.BlockSpec(memory_space=pl.ANY)] * (len(came) + len(after)),
        out_specs=[pl.BlockSpec(memory_space=pltpu.HBM)] * len(spans),
        out_shape=[pltpu.HBM(shape, bf16) for shape in shapes],
        scratch_shapes=scratch + [pltpu.SemaphoreType.DMA((8,)), pltpu.SemaphoreType.DMA((2,))],
        compiler_params=pltpu.CompilerParams(vmem_limit_bytes=VMEM_ALL),
        cost_estimate=pl.CostEstimate(flops=0, bytes_accessed=8 * shapes[0][0] * rows * width * 2, transcendentals=0),
        name="hop",
    )(spots, *in_hbm(terms), *came, *after)


class Ring:
    def __init__(self, place, mine, other):
        self.place, self.size, self.left = place, mine.shape[0] // CHIPS, 4
        self.half = self.size // 2
        self.terms = (mine, swap_cores(other))

    def hop(self, after=()):
        n, half, size = self.left, self.half, self.size
        spots = jnp.stack([(self.place + n) % CHIPS, (self.place - n) % CHIPS]) * size
        if n == 4:
            spans, adds, came = [(0, half), (half, size)], [], []
        else:
            spans, came = [(0, size)] * 2, [self.ahead, self.behind]
            adds = [(0, 0, half, 0), (1, half, size, half)] if n == 3 else [(0, 0, size, 0), (1, 0, size, 0)]
        ahead, behind = hop_sums(spots.astype(jnp.int32), self.terms, spans, adds, came, after)
        self.sent = [ahead, behind]
        self.ahead, self.behind = along(ahead, 1), along(behind, -1)
        self.left -= 1

    def held(self, count=2):
        self.count = count
        return list(self.terms[:count])

    def later(self, made):
        self.terms = tuple(made[-self.count :]) + self.terms[self.count :]
        return made[: -self.count]

    def finish(self, after=()):
        spots = jnp.reshape(self.place * self.size, (1,)).astype(jnp.int32)
        adds = [(0, 0, self.size, 0)] * 2
        return hop_sums(spots, self.terms, [(0, self.size)], adds, [self.ahead, self.behind], after)[0]


def time_features(steps_in):
    half_width = D // 2
    freqs = jnp.exp(-math.log(10000.0) * jnp.arange(half_width, dtype=f32) / half_width)
    angles = steps_in.astype(f32)[:, None] * freqs[None, :]
    return jnp.concatenate([jnp.cos(angles), jnp.sin(angles)], axis=1)


def body(tokens, cotangent, loss_weight, timesteps, owners, master, first_moment, second_moment):
    section_index = lax.axis_index(SECTION)
    me = lax.axis_index(BATCH)
    owner_total = lax.axis_size(BATCH)
    slots, panel_rows = master.shape[1], master.shape[2]
    clips = timesteps.shape[0]
    length = tokens.shape[0] // clips
    low = master[0].astype(bf16)
    owner = owners[0] + (0.0 * low[0, 0, 0].astype(f32)).astype(jnp.int32)
    panels = owner.shape[0]
    moved = DOWN_END // panel_rows
    cap = min(slots, max(4, (slots * 25 + 30) // 31))
    section = jnp.reshape(section_index, (1,)).astype(jnp.int32)

    number = jnp.arange(panels, dtype=jnp.int32)
    same = (owner[:, None] == owner[None, :]) & (number[None, :] < number[:, None])
    rank = jnp.sum(same.astype(jnp.int32), axis=1)
    first_size = owner_total * cap
    place = jnp.where(
        rank < cap, owner * cap + rank, first_size + owner * (slots - cap) + rank - cap
    )[:moved]
    mine = (owner[None, :] == me) & (
        rank[None, :] == jnp.arange(slots, dtype=jnp.int32)[:, None]
    )
    slot_panel = jnp.sum(jnp.where(mine, number[None, :] + 1, 0), axis=1) - 1
    kind = jnp.where(slot_panel < 0, 0, jnp.where(slot_panel < moved, 1, 2)).astype(jnp.int32)
    grad_row = jnp.where(kind == 2, (slot_panel - moved) * panel_rows, 0).astype(jnp.int32)

    rings = owner_total == 2 * CHIPS
    code, index, slot_code, slot_index, sizes, beyond = routes(owner, rank, mine, me, owner_total, slots, moved)
    gathered = lax.all_gather(low[:cap], BATCH, axis=0, tiled=True)
    spot = jnp.arange(owner_total * clips, dtype=jnp.int32) // clips == me
    news = [jnp.where(spot, jnp.tile(timesteps.astype(f32), owner_total), 0.0)]
    past = jnp.max(jnp.where(number < moved, rank, 0)) >= cap
    news.append(jnp.stack([past, beyond]).astype(f32) + 0.0 * low[0, 0, 0].astype(f32))
    news = lax.pmax(jnp.concatenate(news), (SECTION, BATCH))
    all_steps = news[:-2]
    beyond = news[-1] > 0.5
    sources = [gathered]
    if cap < slots:
        rest_shape = (owner_total * (slots - cap), panel_rows, D)
        sources.append(
            lax.cond(
                news[-2] + 0.0 * gathered[0, 0, 0].astype(f32) > 0.5,
                lambda part: lax.all_gather(part, BATCH, axis=0, tiled=True),
                lambda part: jnp.zeros(rest_shape, bf16),
                low[cap:],
            )
        )
    sheet = assemble(place, sources, moved)

    cond = jax.nn.silu(time_features(all_steps)).astype(bf16)
    clip_total = cond.shape[0]
    share = jnp.einsum("cd,sd->cs", cond, low.reshape(slots * panel_rows, D), preferred_element_type=f32)
    share = lax.all_to_all(
        share.reshape(owner_total, clips, slots * panel_rows), BATCH, split_axis=0, concat_axis=0, tiled=True
    )
    share = share.reshape(owner_total, clips, slots, panel_rows).transpose(1, 0, 2, 3)
    share = share.reshape(clips, owner_total * slots, panel_rows)
    pick = (
        (owner * slots + rank)[moved:, None] == jnp.arange(owner_total * slots, dtype=jnp.int32)[None, :]
    ).astype(f32)
    mod = jnp.einsum("ps,csr->cpr", pick, share, precision=lax.Precision.HIGHEST)
    mod = mod.reshape(clips, 6, D)

    run = functools.partial
    base = dict(clips=clips, length=length, section=section, mod=mod, sheet=sheet)
    firsts, outs = [], None
    for c in range(clips):
        firsts.append(first_forward(c, x=tokens, outs=outs, **base))
        outs = firsts[c][N_OUTS]
    received = [lax.ppermute(f[N_SENT], SECTION, [(0, 1)]) for f in firsts]
    seconds, gin = [], None
    for c in range(clips):
        chain = {n: firsts[c][n] for n in (N_H1, N_O, N_H2, N_Z)} | {N_OUTS: outs, N_GIN: gin}
        seconds.append(second_both(c, loss_weight=loss_weight, x=received[c], g=cotangent, chain=chain, **base))
        outs, gin = seconds[c][N_OUTS], seconds[c][N_GIN]
    received = [lax.ppermute(f[N_SENT], SECTION, [(1, 0)]) for f in seconds]
    every = [dict(f) for f in seconds]

    all_jobs = ((N_Z, N_DB, UP_END), (N_DU, N_H2, PROJ_END), (N_DA, N_O, QKV_END), (N_DQKV, N_H1, 0))
    grads = run(weight_grads, code=code, index=index, length=length, panel_rows=panel_rows)
    partial, after = None, mod
    for c in range(clips):
        chain = {n: every[c][n] for n in BACK_MAKES} | {N_GIN: gin}
        every[c] |= first_back(c, x=tokens, g=received[c], kept=firsts[c], chain=chain, after=after, **base)
        gin, after = every[c][N_GIN], every[c][N_DMOD_ATT]
        if rings and c == clips - 2:
            (partial,) = grads(all_jobs, every=every[:-1], sizes=[moved], plain=True)
            after = partial

    dmod = [jnp.concatenate([e[N_DMOD_ATT], e[N_DMOD_FFN]]) for e in every]
    dmod = jnp.stack(dmod).reshape(1, clips, 6 * D).astype(bf16)
    dmod = lax.all_to_all(
        jnp.broadcast_to(dmod, (owner_total, clips, 6 * D)), BATCH, split_axis=0, concat_axis=0, tiled=True
    )
    slot_code = jnp.where(kind == 1, slot_code + 2, jnp.where(kind == 2, 1, 0)).astype(jnp.int32)
    update = run(
        adam, code=slot_code, index=slot_index, row=grad_row, master=master[0], first=first_moment[0],
        second=second_moment[0], dmod=dmod.reshape(clip_total, 6 * D).T, cond=cond,
    )
    if rings:
        place = me // 4 + (me // 2) % 2 * (CHIPS - 1 - 2 * (me // 4))
        wide = [sizes[1]] * 2 + [sizes[2]]
        first_jobs = ((N_DA, N_O, QKV_END), (N_DQKV, N_H1, 0), (N_DU, N_H2, PROJ_END))
        now = every[-1:] if partial is not None else every
        made = grads(first_jobs, every=now, sizes=[sizes[0]] * 2 + wide, partial=partial)
        first = Ring(place, *made[:2])
        made = grads(
            ((N_Z, N_DB, UP_END),), every=now, sizes=wide, thread=made[2:], through=first.held(1), partial=partial
        )
        made = first.later(made)
        second = Ring(place, *made[:2])
        rest = lax.cond(
            beyond,
            lambda part: lax.psum_scatter(part, BATCH, scatter_dimension=0, tiled=True),
            lambda part: jnp.zeros((slots, panel_rows, D), bf16),
            made[2],
        )
        first.hop()
        second.hop()
        first.hop(after=[rest, *second.sent])
        second.hop(after=[dmod])
        results = update(0, 2, sums=[], chain=[])
        first.hop()
        second.hop(after=results[3:])
        first.hop()
        second.hop()
        half = first.finish()
        sums = [half, swap_cores(half)]
        results = update(2, 4, sums=sums, chain=results)
        half = second.finish(after=results[3:])
        sums += [half, swap_cores(half), rest]
        results = update(4, 7, sums=sums, chain=results)
    else:
        (made,) = grads(all_jobs, every=every, sizes=[sizes[0]])
        sums = [lax.psum_scatter(made, BATCH, scatter_dimension=0, tiled=True)]
        results = update(0, 3, sums=sums, chain=[])
    return (outs[None], gin[None], *(r[None] for r in results))


CAPS = (24, 24)


def count_before(flag, group):
    number = jnp.arange(group.shape[0], dtype=jnp.int32)
    before = (group[:, None] == group[None, :]) & (number[None, :] < number[:, None]) & flag[None, :]
    return jnp.sum(before.astype(jnp.int32), axis=1)


def routes(owner, rank, mine, me, owner_total, slots, moved):
    if owner_total != 2 * CHIPS:
        code = jnp.zeros((moved,), jnp.int32)
        return code, (owner * slots + rank)[:moved], jnp.zeros((slots,), jnp.int32), jnp.arange(slots, dtype=jnp.int32), [owner_total * slots], jnp.bool_(False)
    number = jnp.arange(moved, dtype=jnp.int32)
    held, core = owner[:moved], me % 2
    chip = held // 2
    spot = chip // 2 + chip % 2 * (CHIPS - 1 - 2 * (chip // 2))
    per_row = DOWN_END // moved
    down = number >= UP_END // per_row
    order = count_before(~down, chip)
    late = down | (order >= CAPS[0])
    order = jnp.where(late, count_before(late, chip), order)
    rest = late & (order >= CAPS[1])
    half = order % 2
    size = jnp.where(late, CAPS[1] // 2, CAPS[0] // 2)
    index = jnp.where(rest, held * slots + rank[:moved], spot * size + order // 2)
    away = (half != core).astype(jnp.int32)
    code = jnp.where(rest, 4, jnp.where(late, 2 + away, away))
    code = jnp.where(down, code - 2, code).astype(jnp.int32)
    taken = mine[:, :moved].astype(jnp.int32)
    found = jnp.where(rest, 4, 2 * late.astype(jnp.int32) + away)
    slot_code = jnp.sum(taken * found[None, :], axis=1)
    slot_index = jnp.sum(taken * jnp.where(rest, rank[:moved], order // 2)[None, :], axis=1)
    sizes = [CHIPS * cap // 2 for cap in CAPS] + [owner_total * slots]
    return code, index.astype(jnp.int32), slot_code.astype(jnp.int32), slot_index.astype(jnp.int32), sizes, jnp.any(rest)


def solution(mesh):
    placed = (
        P(BATCH, None),
        P(BATCH, None),
        P(BATCH),
        P(BATCH),
        P(SECTION, None),
        P(SECTION, BATCH, None, None),
        P(SECTION, BATCH, None, None),
        P(SECTION, BATCH, None, None),
    )
    return jax.shard_map(
        body,
        mesh=mesh,
        in_specs=placed,
        out_specs=(
            P(SECTION, BATCH, None),
            P(SECTION, BATCH, None),
            P(SECTION, BATCH, None, None),
            P(SECTION, BATCH, None, None),
            P(SECTION, BATCH, None, None),
            P(SECTION, BATCH, None, None),
        ),
        check_vma=False,
    )
```

```python
import functools
import math

import jax
import jax.numpy as jnp
from jax import lax
from jax.experimental import pallas as pl
from jax.experimental.pallas import tpu as pltpu
from jax.sharding import PartitionSpec as P

D = 768
HEADS = 12
HEAD_DIM = 64
FF = 3072
STEP = 10
QKV_END = 3 * D
PROJ_END = 4 * D
UP_END = 4 * D + FF
DOWN_END = 4 * D + 2 * FF

norm_eps = 1e-06
adam_eps = 1e-08
learn_rate = 0.03
decay_rate = 0.1
beta_one = 0.5
beta_two = 0.5

bf16 = jnp.bfloat16
f32 = jnp.float32
SECTION, BATCH = "section", "batch"
VMEM_LIMIT = 46 * 1024 * 1024
VMEM_ALL = 58 * 1024 * 1024
ROWS = 128
GELU_C = math.sqrt(2.0 / math.pi)


def dot_nn(a, b):
    return lax.dot_general(a, b, (((1,), (0,)), ((), ())), preferred_element_type=f32)


def dot_nt(a, b):
    return lax.dot_general(a, b, (((1,), (1,)), ((), ())), preferred_element_type=f32)


def dot_tn(a, b):
    return lax.dot_general(a, b, (((0,), (0,)), ((), ())), preferred_element_type=f32)


def in_hbm(arrays):
    return [pltpu.with_memory_space_constraint(a, pltpu.HBM) for a in arrays]


def start(src, dst, sem):
    copy = pltpu.make_async_copy(src, dst, sem)
    copy.start()
    return copy


def norm(values):
    average = jnp.mean(values, axis=-1, keepdims=True)
    centred = values - average
    variance = jnp.mean(centred * centred, axis=-1, keepdims=True)
    inverse = lax.rsqrt(variance + norm_eps)
    return centred * inverse, inverse


def norm_back(grad, values, scale_row):
    normed, inverse = norm(values)
    dn = grad * (1.0 + scale_row)
    mean_one = jnp.mean(dn, axis=-1, keepdims=True)
    mean_two = jnp.mean(dn * normed, axis=-1, keepdims=True)
    dx = inverse * (dn - mean_one - normed * mean_two)
    return dx, jnp.sum(grad, axis=0, keepdims=True), jnp.sum(grad * normed, axis=0, keepdims=True)


def gelu_both(u):
    square = u * u
    half = 0.5 * jnp.tanh(u * (square * (0.044715 * GELU_C) + GELU_C)) + 0.5
    bend = u * (square * (6.0 * 0.044715 * GELU_C) + 2.0 * GELU_C)
    return u * half, half + half * (1.0 - half) * bend


def assemble_kernel(panels, first_size, index_ref, *refs):
    sources, sheet, sem = refs[:-2], refs[-2], refs[-1]
    rows = sheet.shape[0] // panels

    @pl.loop(0, panels, unroll=4)
    def _(p):
        where = index_ref[p]
        target = sheet.at[pl.ds(pl.multiple_of(p * rows, rows), rows)]
        if len(sources) == 1:
            pltpu.make_async_copy(sources[0].at[where], target, sem).start()
        else:

            @pl.when(where < first_size)
            def _():
                pltpu.make_async_copy(sources[0].at[where], target, sem).start()

            @pl.when(where >= first_size)
            def _():
                pltpu.make_async_copy(sources[1].at[where - first_size], target, sem).start()

    pltpu.make_async_copy(sheet, sheet, sem).wait()


def assemble(index, sources, panels):
    first_size = sources[0].shape[0]
    rows = sources[0].shape[1]
    return pl.pallas_call(
        functools.partial(assemble_kernel, panels, first_size),
        out_shape=pltpu.VMEM((panels * rows, D), bf16),
        in_specs=[pl.BlockSpec(memory_space=pltpu.SMEM)]
        + [pl.BlockSpec(memory_space=pltpu.HBM)] * len(sources),
        out_specs=pl.BlockSpec(memory_space=pltpu.VMEM),
        scratch_shapes=[pltpu.SemaphoreType.DMA],
        compiler_params=pltpu.CompilerParams(vmem_limit_bytes=VMEM_LIMIT),
        cost_estimate=pl.CostEstimate(flops=0, bytes_accessed=2 * panels * rows * D, transcendentals=0),
        name="assemble",
    )(index, *in_hbm(sources))


(
    N_XIN,
    N_H1,
    N_QKV,
    N_LSE,
    N_O,
    N_A,
    N_X1,
    N_H2,
    N_SLOPE,
    N_Z,
    N_B,
    N_OUT,
    N_DB,
    N_DU,
    N_DA,
    N_DX1,
    N_DMOD_FFN,
    N_DQKV,
    N_DMOD_ATT,
    N_G,
    N_SENT,
    N_DO,
    N_ACC,
    N_LSE_COLS,
    N_OUTS,
    N_GIN,
    N_MOD,
    N_X,
    N_AFTER,
    N_SECTION,
    N_LOSS,
) = range(31)


TILE = D
TILES = FF // TILE
PAIRS = HEADS // 2


def shapes_of(length):
    return {
        N_XIN: ((length, D), bf16),
        N_H1: ((length, D), bf16),
        N_QKV: ((length, 3 * D), bf16),
        N_LSE: ((16, length), f32),
        N_O: ((length, D), bf16),
        N_A: ((length, D), bf16),
        N_X1: ((length, D), f32),
        N_H2: ((length, D), bf16),
        N_SLOPE: ((length, FF), f32),
        N_Z: ((length, FF), bf16),
        N_B: ((length, D), bf16),
        N_OUT: ((length, D), bf16),
        N_DB: ((length, D), bf16),
        N_DU: ((length, FF), bf16),
        N_DA: ((length, D), bf16),
        N_DX1: ((length, D), f32),
        N_DMOD_FFN: ((4, D), f32),
        N_DQKV: ((length, 3 * D), bf16),
        N_DMOD_ATT: ((2, D), f32),
        N_G: ((length, D), bf16),
        N_SENT: ((length, D), bf16),
        N_DO: ((length, D), bf16),
        N_ACC: ((length, D), f32),
        N_LSE_COLS: ((length, 128), f32),
    }


def blocks_of(length):
    return [pl.ds(r, ROWS) for r in range(0, length, ROWS)]


def low_half():
    return lax.broadcasted_iota(jnp.int32, (1, 128), 1) < HEAD_DIM


def forward_qkv(v, w_qkv, row, length):
    for block in blocks_of(length):
        normed, _ = norm(v[N_XIN][block, :].astype(f32))
        v[N_H1][block, :] = (normed * (1.0 + row(1)) + row(0)).astype(bf16)
    for n in range(3):
        part = dot_nt(v[N_H1][...], w_qkv(n))
        v[N_QKV][:, n * D : (n + 1) * D] = part.astype(bf16)


def forward_attention(v, length):
    low_lanes = low_half()
    room = FF // length
    columns = lax.broadcasted_iota(jnp.int32, (1, 128), 1)

    def scores(head):
        at = slice(head // 2 * 128, head // 2 * 128 + 128)
        q = v[N_QKV][:, at] * jnp.asarray(HEAD_DIM ** (-0.5), bf16)
        qh = jnp.where(low_lanes if head % 2 == 0 else ~low_lanes, q, jnp.zeros_like(q))
        first = head % room * length
        v[N_SLOPE][:, first : first + length] = dot_nt(qh, v[N_QKV][:, D + at.start : D + at.stop])

    def softmax(head):
        span = slice(head % room * length, head % room * length + length)
        for block in blocks_of(length):
            s = v[N_SLOPE][block, span]
            top = jnp.max(s, axis=-1, keepdims=True)
            e = jnp.exp(s - top)
            total = jnp.sum(e, axis=-1, keepdims=True)
            v[N_Z][block, span] = (e * (1.0 / total)).astype(bf16)
            line = top + jnp.log(total)
            v[N_LSE_COLS][block, :] = jnp.where(columns == head, line, v[N_LSE_COLS][block, :]) if head else jnp.where(columns == 0, line, 0.0)

    def mix(head):
        at = slice(2 * D + head // 2 * 128, 2 * D + head // 2 * 128 + 128)
        span = slice(head % room * length, head % room * length + length)
        return dot_nn(v[N_Z][:, span], v[N_QKV][:, at])

    scores(0)
    mixed = [None] * HEADS
    for head in range(HEADS):
        if head + 1 < HEADS:
            scores(head + 1)
        softmax(head)
        mixed[head] = mix(head)
        if head % 2:
            at = slice(head // 2 * 128, head // 2 * 128 + 128)
            v[N_O][:, at] = jnp.where(low_lanes, mixed[head - 1], mixed[head]).astype(bf16)
    v[N_LSE][...] = v[N_LSE_COLS][...].T[:16, :]


def forward_proj(v, w_proj, row, length):
    v[N_ACC][...] = dot_nt(v[N_O][...], w_proj)
    for block in blocks_of(length):
        branch = v[N_ACC][block, :]
        v[N_A][block, :] = branch.astype(bf16)
        middle = v[N_XIN][block, :].astype(f32) + row(2) * branch
        v[N_X1][block, :] = middle
        normed, _ = norm(middle)
        v[N_H2][block, :] = (normed * (1.0 + row(4)) + row(3)).astype(bf16)


def forward_ffn(v, w_up, w_down, row, length, after):
    for n in range(TILES):
        span = slice(n * TILE, (n + 1) * TILE)
        v[N_SLOPE][:, span] = dot_nt(v[N_H2][...], w_up(n))
        for block in blocks_of(length):
            value, slope = gelu_both(v[N_SLOPE][block, span])
            v[N_Z][block, span] = value.astype(bf16)
            v[N_SLOPE][block, span] = slope
        part = dot_nn(v[N_Z][:, span], w_down(n))
        if n:
            v[N_ACC][...] += part
        else:
            v[N_ACC][...] = part
        after(n)
    for block in blocks_of(length):
        branch = v[N_ACC][block, :]
        v[N_B][block, :] = branch.astype(bf16)
        v[N_OUT][block, :] = (v[N_X1][block, :] + row(5) * branch).astype(bf16)


def back_gate(v, row, length, scale):
    gate_two = jnp.zeros((1, D), f32)
    for block in blocks_of(length):
        g = v[N_G][block, :].astype(f32)
        if scale is not None:
            g = g * scale
        v[N_DX1][block, :] = g
        v[N_DB][block, :] = (row(5) * g).astype(bf16)
        gate_two += jnp.sum(g * v[N_B][block, :].astype(f32), axis=0, keepdims=True)
    v[N_DMOD_FFN][3:4, :] = gate_two


def back_ffn_part(v, w_up, w_down, row, length, before, after):
    for n in range(TILES):
        span = slice(n * TILE, (n + 1) * TILE)
        before(n)
        dz = dot_nt(v[N_DB][...], w_down(n))
        v[N_DU][:, span] = (dz * v[N_SLOPE][:, span]).astype(bf16)
        part = dot_nn(v[N_DU][:, span], w_up(n))
        if n:
            v[N_ACC][...] += part
        else:
            v[N_ACC][...] = part
        after(n)


def back_middle(v, row, length):
    shift_two = jnp.zeros((1, D), f32)
    scale_two = jnp.zeros((1, D), f32)
    gate_one = jnp.zeros((1, D), f32)
    for block in blocks_of(length):
        dx, shift_part, scale_part = norm_back(v[N_ACC][block, :], v[N_X1][block, :], row(4))
        total = v[N_DX1][block, :] + dx
        v[N_DX1][block, :] = total
        shift_two += shift_part
        scale_two += scale_part
        gate_one += jnp.sum(total * v[N_A][block, :].astype(f32), axis=0, keepdims=True)
        v[N_DA][block, :] = (row(2) * total).astype(bf16)
    v[N_DMOD_FFN][0:1, :] = gate_one
    v[N_DMOD_FFN][1:2, :] = shift_two
    v[N_DMOD_FFN][2:3, :] = scale_two


def back_attention(v, w_proj, length):
    v[N_DO][...] = dot_nn(v[N_DA][...], w_proj).astype(bf16)
    low_lanes = low_half()
    scale = HEAD_DIM ** (-0.5)

    def parts(head):
        at = head // 2 * 128
        keep = lambda a: jnp.where(low_lanes if head % 2 == 0 else ~low_lanes, a, jnp.zeros_like(a))
        qh, doh = keep(v[N_QKV][:, at : at + 128]), keep(v[N_DO][:, at : at + 128])
        kh = keep(v[N_QKV][:, D + at : D + at + 128])
        return qh, kh, doh

    def first(head):
        at = head // 2 * 128
        qh, kh, doh = parts(head)
        st = dot_nt(v[N_QKV][:, D + at : D + at + 128], qh * jnp.asarray(scale, bf16))
        dpt = dot_nt(v[N_QKV][:, 2 * D + at : 2 * D + at + 128], doh)
        return st, dpt, qh, kh, doh

    def rest(head, st, dpt, qh, kh, doh):
        pt = jnp.exp(st - v[N_LSE][head : head + 1, :])
        dv = dot_nn(pt.astype(bf16), doh)
        inner = jnp.sum(dpt * pt, axis=0, keepdims=True)
        drt = (pt * (dpt - inner) * scale).astype(bf16)
        return dot_tn(drt, kh), dot_nn(drt, qh), dv

    ahead = first(0)
    made = None
    for head in range(HEADS):
        now = ahead
        if head + 1 < HEADS:
            ahead = first(head + 1)
        made_now = rest(head, *now)
        if head % 2:
            for n in range(3):
                at = n * D + head // 2 * 128
                v[N_DQKV][:, at : at + 128] = (made[n] + made_now[n]).astype(bf16)
        made = made_now


def back_input(v, w_qkv, row, length):
    v[N_ACC][...] = dot_nn(v[N_DQKV][...], w_qkv)
    shift_one = jnp.zeros((1, D), f32)
    scale_one = jnp.zeros((1, D), f32)
    for block in blocks_of(length):
        dx, shift_part, scale_part = norm_back(v[N_ACC][block, :], v[N_XIN][block, :].astype(f32), row(1))
        total = v[N_DX1][block, :] + dx
        v[N_DX1][block, :] = total
        v[N_SENT][block, :] = total.astype(bf16)
        shift_one += shift_part
        scale_one += scale_part
    v[N_DMOD_ATT][0:1, :] = shift_one
    v[N_DMOD_ATT][1:2, :] = scale_one


class Mover:
    def __init__(self, sems):
        self.sems, self.used, self.coming, self.going = sems, 0, {}, []

    def start(self, src, dst):
        copy = pltpu.make_async_copy(src, dst, self.sems.at[self.used])
        self.used += 1
        copy.start()
        return copy

    def fetch(self, name, src, dst):
        self.coming[name] = self.start(src, dst)

    def need(self, *names):
        for name in names:
            if name in self.coming:
                self.coming.pop(name).wait()

    def save(self, src, dst):
        self.going.append(self.start(src, dst))

    def finish(self):
        assert not self.coming
        for copy in self.going:
            copy.wait()


SEMS = 48


def call_block(kernel, name, want, clip, length, smem, sheet, read, write, hold, shared, chain, flops, moved, loose=None):
    any_spec = pl.BlockSpec(memory_space=pltpu.HBM)
    shapes = shapes_of(length)
    s_names, r_names, w_names = list(smem), list(read), list(write)
    chained = [n for n in w_names if chain.get(n) is not None]
    operands = [smem[n] for n in s_names] + [pltpu.with_memory_space_constraint(sheet, pltpu.VMEM)]
    operands += [read[n] if n == loose else in_hbm([read[n]])[0] for n in r_names]
    aliases = {len(operands) + i: w_names.index(n) for i, n in enumerate(chained)}
    operands += in_hbm([chain[n] for n in chained])

    def run(*refs):
        refs = list(refs)
        take = lambda names: dict(zip(names, [refs.pop(0) for _ in names]))
        s, w, r = take(s_names), refs.pop(0), take(r_names)
        take(chained)
        o = take(w_names)
        v = take(hold)
        v |= {n: v[other] for n, other in shared.items()}
        m, sems = refs

        @pl.when(s[N_SECTION][0] == want)
        def _():
            kernel(clip, length, s, m, r, o, v, w, Mover(sems))

    results = pl.pallas_call(
        run,
        out_shape=[pltpu.HBM(*write[n]) for n in w_names],
        in_specs=[pl.BlockSpec(memory_space=pltpu.SMEM)] * len(s_names)
        + [pl.BlockSpec(memory_space=pltpu.VMEM)]
        + [any_spec] * (len(r_names) + len(chained)),
        out_specs=[any_spec] * len(w_names),
        scratch_shapes=[pltpu.VMEM(*shapes[n]) for n in hold]
        + [pltpu.VMEM((6, D), f32), pltpu.SemaphoreType.DMA((SEMS,))],
        input_output_aliases=aliases,
        compiler_params=pltpu.CompilerParams(vmem_limit_bytes=VMEM_LIMIT),
        cost_estimate=pl.CostEstimate(flops=flops, bytes_accessed=moved, transcendentals=0),
        name=f"{name}_{clip}",
    )(*operands)
    return dict(zip(w_names, results))


def mod_row(m):
    return lambda n: m[n : n + 1, :]


def forward_body(clip, length, x_offset, m, r, v, w, mover, keep):
    row = mod_row(m)
    mover.fetch(N_MOD, r[N_MOD].at[clip], m)
    mover.fetch(N_XIN, r[N_X].at[pl.ds(x_offset, length)], v[N_XIN])
    mover.need(N_MOD, N_XIN)
    forward_qkv(v, lambda n: w[n * D : (n + 1) * D, :], row, length)
    keep(N_H1)
    keep(N_QKV)
    forward_attention(v, length)
    keep(N_LSE)
    keep(N_O)
    forward_proj(v, w[QKV_END:PROJ_END, :], row, length)
    keep(N_A)
    keep(N_X1)
    keep(N_H2)
    forward_ffn(
        v,
        lambda n: w[PROJ_END + n * D : PROJ_END + (n + 1) * D, :],
        lambda n: w[UP_END + n * D : UP_END + (n + 1) * D, :],
        row,
        length,
        lambda n: (keep(N_SLOPE, n), keep(N_Z, n)),
    )
    keep(N_B)


def saver(mover, v, o):
    def keep(name, n=None):
        if name not in o:
            return
        if n is None:
            mover.save(v[name], o[name])
        else:
            span = pl.ds(n * TILE, TILE)
            mover.save(v[name].at[:, span], o[name].at[:, span])

    return keep


FIRST_KEEP = (N_H1, N_QKV, N_LSE, N_O, N_A, N_X1, N_H2, N_SLOPE, N_Z, N_B)
BOTH_KEEP = (N_H1, N_O, N_H2, N_Z, N_DB, N_DU, N_DA, N_DQKV, N_DMOD_FFN, N_DMOD_ATT)


def first_forward(clip, clips, length, section, mod, x, sheet, outs):
    def kernel(clip, length, s, m, r, o, v, w, mover):
        forward_body(clip, length, clip * length, m, r, v, w, mover, saver(mover, v, o))
        mover.save(v[N_OUT], o[N_SENT])
        mover.save(v[N_OUT], o[N_OUTS].at[pl.ds(clip * length, length)])
        mover.finish()

    shapes = shapes_of(length)
    write = {n: shapes[n] for n in FIRST_KEEP}
    write |= {N_OUTS: ((clips * length, D), bf16), N_SENT: ((length, D), bf16)}
    hold = FIRST_KEEP + (N_XIN, N_OUT, N_ACC, N_LSE_COLS)
    return call_block(
        kernel, "first_forward", 0, clip, length, {N_SECTION: section}, sheet, {N_MOD: mod, N_X: x},
        write, hold, {}, {N_OUTS: outs}, 17 * 10**9, 30 << 20,
    )


def second_both(clip, clips, length, section, loss_weight, mod, x, g, sheet, chain):
    def kernel(clip, length, s, m, r, o, v, w, mover):
        keep = saver(mover, v, o)
        row = mod_row(m)
        forward_body(clip, length, 0, m, r, v, w, mover, keep)
        mover.fetch(N_G, r[N_G].at[pl.ds(clip * length, length)], v[N_G])
        mover.save(v[N_OUT], o[N_OUTS].at[pl.ds(clip * length, length)])
        mover.need(N_G)
        back_gate(v, row, length, s[N_LOSS][clip])
        keep(N_DB)
        back_ffn_part(
            v,
            lambda n: w[PROJ_END + n * D : PROJ_END + (n + 1) * D, :],
            lambda n: w[UP_END + n * D : UP_END + (n + 1) * D, :],
            row, length, lambda n: None, lambda n: keep(N_DU, n),
        )
        back_middle(v, row, length)
        keep(N_DA)
        keep(N_DMOD_FFN)
        back_attention(v, w[QKV_END:PROJ_END, :], length)
        keep(N_DQKV)
        back_input(v, w[0:QKV_END, :], row, length)
        mover.save(v[N_SENT], o[N_SENT])
        keep(N_DMOD_ATT)
        mover.save(v[N_DX1], o[N_GIN].at[pl.ds(clip * length, length)])
        mover.finish()

    shapes = shapes_of(length)
    write = {n: shapes[n] for n in BOTH_KEEP}
    write |= {N_OUTS: ((clips * length, D), bf16), N_GIN: ((clips * length, D), f32), N_SENT: ((length, D), bf16)}
    hold = (N_XIN, N_H1, N_QKV, N_LSE, N_O, N_A, N_X1, N_H2, N_SLOPE, N_Z, N_B, N_OUT, N_DB, N_DU, N_DX1)
    hold += (N_DMOD_FFN, N_DMOD_ATT, N_G, N_ACC, N_LSE_COLS)
    shared = {N_DQKV: N_QKV, N_DO: N_B, N_DA: N_A, N_SENT: N_G}
    return call_block(
        kernel, "second_both", 1, clip, length, {N_SECTION: section, N_LOSS: loss_weight},  sheet,
        {N_MOD: mod, N_X: x, N_G: g}, write, hold, shared, chain, 40 * 10**9, 40 << 20, N_X,
    )


BACK_MAKES = (N_DB, N_DU, N_DA, N_DQKV, N_DMOD_FFN, N_DMOD_ATT)


def first_back(clip, clips, length, section, mod, x, g, sheet, kept, chain, after):
    def kernel(clip, length, s, m, r, o, v, w, mover):
        keep = saver(mover, v, o)
        row = mod_row(m)
        mover.fetch(N_MOD, r[N_MOD].at[clip], m)
        mover.fetch(N_G, r[N_G], v[N_G])
        mover.fetch(N_B, r[N_B], v[N_B])
        for n in range(TILES):
            span = pl.ds(n * TILE, TILE)
            mover.fetch((N_SLOPE, n), r[N_SLOPE].at[:, span], v[N_SLOPE].at[:, span])
        for name in (N_X1, N_A, N_QKV, N_LSE):
            mover.fetch(name, r[name], v[name])
        mover.fetch(N_XIN, r[N_X].at[pl.ds(clip * length, length)], v[N_XIN])
        mover.need(N_MOD, N_G, N_B)
        back_gate(v, row, length, None)
        keep(N_DB)
        back_ffn_part(
            v,
            lambda n: w[PROJ_END + n * D : PROJ_END + (n + 1) * D, :],
            lambda n: w[UP_END + n * D : UP_END + (n + 1) * D, :],
            row, length, lambda n: mover.need((N_SLOPE, n)), lambda n: keep(N_DU, n),
        )
        mover.need(N_X1, N_A)
        back_middle(v, row, length)
        keep(N_DA)
        keep(N_DMOD_FFN)
        mover.need(N_QKV, N_LSE)
        back_attention(v, w[QKV_END:PROJ_END, :], length)
        keep(N_DQKV)
        mover.need(N_XIN)
        back_input(v, w[0:QKV_END, :], row, length)
        keep(N_DMOD_ATT)
        mover.save(v[N_DX1], o[N_GIN].at[pl.ds(clip * length, length)])
        mover.finish()

    shapes = shapes_of(length)
    read = {N_MOD: mod, N_X: x, N_G: g} | {n: kept[n] for n in (N_B, N_SLOPE, N_X1, N_A, N_QKV, N_LSE)}
    read[N_AFTER] = after
    write = {n: shapes[n] for n in BACK_MAKES} | {N_GIN: ((clips * length, D), f32)}
    hold = (N_G, N_B, N_SLOPE, N_X1, N_A, N_QKV, N_LSE, N_XIN, N_DB, N_DU, N_DX1, N_DMOD_FFN, N_DMOD_ATT, N_ACC)
    shared = {N_DQKV: N_QKV, N_DO: N_B, N_DA: N_A, N_SENT: N_G}
    return call_block(
        kernel, "first_back", 0, clip, length, {N_SECTION: section}, sheet, read,
        write, hold, shared, chain, 25 * 10**9, 30 << 20, N_G,
    )


def grads_kernel(jobs, clips, length, panel_rows, plain, added, own, passed, others, code_ref, index_ref, *refs):
    count = 2 * len(jobs) * clips
    sources, partial = refs[:count], refs[count + others - 1]
    refs = refs[count + others :]
    outs = refs[:own]
    scratch = refs[own + passed :]
    values = scratch[: 2 * len(jobs)]
    tile_v, add_v, in_sem, add_sem, out_sem = scratch[2 * len(jobs) :]
    per_tile = D // panel_rows
    tiles = []
    for n, (left, right, base) in enumerate(jobs):
        tiles += [(n, column, base + column) for column in range(0, values[2 * n].shape[1], D)]
    get, more = {}, {}

    def fetch(n, column):
        get[n, column] = [
            start(
                sources[n * clips + c].at[:, pl.ds(column, D)],
                values[n].at[pl.ds(c * length, length), pl.ds(column, D)],
                in_sem.at[len(get), c],
            )
            for c in range(clips)
        ]

    def fetch_tile(t):
        if t < len(tiles):
            n, column, _ = tiles[t]
            if column == 0:
                fetch(2 * n + 1, 0)
            fetch(2 * n, column)
            if added:
                first_panel = tiles[t][2] // panel_rows
                more[t] = start(partial.at[pl.ds(first_panel, per_tile)], add_v.at[t % 4], add_sem.at[t % 4])

    for t in range(3):
        fetch_tile(t)
    def drain(slot):
        pltpu.make_async_copy(outs[-1].at[pl.ds(0, per_tile)], tile_v.at[slot], out_sem.at[slot]).wait()

    for t, (n, column, first_row) in enumerate(tiles):
        slot = t % 2
        if column == 0:
            for copy in get[2 * n + 1, 0]:
                copy.wait()
        for copy in get[2 * n, column]:
            copy.wait()
        fetch_tile(t + 3)
        if t >= 2:
            drain(slot)
        part = dot_tn(values[2 * n][:, column : column + D], values[2 * n + 1][...])
        if added:
            more[t].wait()
            part = part + add_v[t % 4].reshape(D, D).astype(f32)
        tile_v[slot, :, :, :] = part.astype(bf16).reshape(per_tile, panel_rows, D)
        if plain:
            first_panel = first_row // panel_rows
            pltpu.make_async_copy(tile_v.at[slot], outs[0].at[pl.ds(first_panel, per_tile)], out_sem.at[slot]).start()
            continue

        @pl.loop(0, per_tile)
        def _(p):
            code = code_ref[first_row // panel_rows + p]
            where = index_ref[first_row // panel_rows + p]

            def put(numbers):
                for n_out in numbers:

                    @pl.when(code == n_out)
                    def _():
                        pltpu.make_async_copy(tile_v.at[slot, p], outs[n_out].at[where], out_sem.at[slot]).start()

            put(range(min(2, own)))
            if own > 2:

                @pl.when(code >= 2)
                def _():
                    put(range(2, own))

    for slot in range(min(2, len(tiles))):
        drain(slot)


def weight_grads(jobs, code, index, every, length, panel_rows, sizes, thread=(), after=(), through=(), partial=None, plain=False):
    clips = len(every)
    any_spec = pl.BlockSpec(memory_space=pltpu.HBM)
    operands, scratch = [code, index], []
    for left, right, _ in jobs:
        for name in (left, right):
            arrays = [every[c][name] for c in range(clips)]
            operands += arrays
            scratch.append(pltpu.VMEM((clips * length, arrays[0].shape[1]), bf16))
    aliases = {}
    for n, array in enumerate(thread):
        aliases[len(operands)] = len(sizes) - len(thread) + n
        operands.append(array)
    passed = [pltpu.HBM(a.shape, a.dtype) for a in through]
    for n, array in enumerate(through):
        aliases[len(operands)] = len(sizes) + n
        operands.append(array)
    operands += after
    if partial is not None:
        operands.append(partial)
    others = len(operands) - 2 - 2 * len(jobs) * clips
    width = sum(s.shape[1] for s in scratch[0::2])
    return pl.pallas_call(
        functools.partial(
            grads_kernel, jobs, clips, length, panel_rows, plain, partial is not None, len(sizes), len(passed), others
        ),
        out_shape=[pltpu.HBM((size, panel_rows, D), bf16) for size in sizes] + passed,
        in_specs=[pl.BlockSpec(memory_space=pltpu.SMEM)] * 2 + [any_spec] * (len(operands) - 2),
        out_specs=[any_spec] * (len(sizes) + len(passed)),
        scratch_shapes=scratch
        + [
            pltpu.VMEM((2, D // panel_rows, panel_rows, D), bf16),
            pltpu.VMEM((4 if partial is not None else 1, D // panel_rows, panel_rows, D), bf16),
            pltpu.SemaphoreType.DMA((width // D + len(jobs), clips)),
            pltpu.SemaphoreType.DMA((4,)),
            pltpu.SemaphoreType.DMA((2,)),
        ],
        input_output_aliases=aliases,
        compiler_params=pltpu.CompilerParams(vmem_limit_bytes=26 * 1024 * 1024 if plain else VMEM_ALL),
        cost_estimate=pl.CostEstimate(
            flops=4 * clips * length * width * D, bytes_accessed=12 << 20, transcendentals=0
        ),
        name=f"grads_{jobs[0][2]}_{plain:d}",
    )(*operands[:2], *in_hbm(operands[2:]))


def adam_kernel(low, high, n_sums, chained, code_ref, index_ref, row_ref, master, first, second, dmod, cond, *refs):
    sums = refs[:n_sums]
    refs = refs[n_sums + (4 if chained else 0) :]
    outs, held, made = refs[:4], refs[4:7], refs[7:11]
    grad_v, in_sem, grad_sem, out_sem = refs[11:]
    slots, rows = master.shape[0], master.shape[1]
    sources = (master, first, second)

    def each(step):
        @pl.loop(0, slots)
        def _(slot):
            code = code_ref[slot]

            @pl.when((code >= low) & (code < high))
            def _():
                step(slot, code)

    def fetch(slot, code):
        for source, target in zip(sources, held):
            pltpu.make_async_copy(source.at[slot], target.at[slot], in_sem.at[slot]).start()
        for n in range(max(low, 2), min(high, n_sums + 2)):

            @pl.when(code == n)
            def _():
                pltpu.make_async_copy(sums[n - 2].at[index_ref[slot]], grad_v.at[slot], grad_sem.at[slot]).start()

    def work(slot, code):
        for source, target in zip(sources, held):
            pltpu.make_async_copy(source.at[slot], target.at[slot], in_sem.at[slot]).wait()

        def update(grad):
            first_next = beta_one * held[1][slot] + (1.0 - beta_one) * grad
            second_next = beta_two * held[2][slot] + (1.0 - beta_two) * grad * grad
            first_hat = first_next / (1.0 - beta_one**STEP)
            second_hat = second_next / (1.0 - beta_two**STEP)
            value = held[0][slot] - learn_rate * (
                first_hat / (jnp.sqrt(second_hat) + adam_eps) + decay_rate * held[0][slot]
            )
            made[0][slot] = value
            made[1][slot] = first_next
            made[2][slot] = second_next
            made[3][slot] = value.astype(bf16)

        if high > 2:

            @pl.when(code >= 2)
            def _():
                pltpu.make_async_copy(sums[0].at[0], grad_v.at[slot], grad_sem.at[slot]).wait()
                update(grad_v[slot].astype(f32))

        if low < 2:

            @pl.when(code == 1)
            def _():
                at = pl.multiple_of(row_ref[slot], rows)
                update(dot_nn(dmod[pl.ds(at, rows), :], cond[...]))

            @pl.when(code == 0)
            def _():
                update(jnp.zeros((rows, D), f32))

        for source, target in zip(made, outs):
            pltpu.make_async_copy(source.at[slot], target.at[slot], out_sem.at[slot]).start()

    def close(slot, code):
        for source, target in zip(made, outs):
            pltpu.make_async_copy(source.at[slot], target.at[slot], out_sem.at[slot]).wait()

    each(fetch)
    each(work)
    each(close)


def adam(low, high, code, index, row, master, first, second, dmod, cond, sums, chain):
    slots, rows = master.shape[0], master.shape[1]
    any_spec = pl.BlockSpec(memory_space=pltpu.HBM)
    smem, vmem = pl.BlockSpec(memory_space=pltpu.SMEM), pl.BlockSpec(memory_space=pltpu.VMEM)
    kinds = [f32, f32, f32, bf16]
    return pl.pallas_call(
        functools.partial(adam_kernel, low, high, len(sums), bool(chain)),
        in_specs=[smem] * 3 + [any_spec] * 3 + [vmem] * 2 + [any_spec] * (len(sums) + len(chain)),
        out_specs=[any_spec] * 4,
        out_shape=[pltpu.HBM(master.shape, kind) for kind in kinds],
        scratch_shapes=[pltpu.VMEM(master.shape, f32)] * 3
        + [pltpu.VMEM(master.shape, kind) for kind in kinds]
        + [pltpu.VMEM(master.shape, bf16)]
        + [pltpu.SemaphoreType.DMA((slots,))] * 3,
        input_output_aliases={8 + len(sums) + n: n for n in range(len(chain))},
        compiler_params=pltpu.CompilerParams(vmem_limit_bytes=VMEM_ALL),
        cost_estimate=pl.CostEstimate(flops=0, bytes_accessed=slots * rows * D * 15, transcendentals=0),
        name=f"adam_{low}",
    )(code, index, row, *in_hbm((master, first, second)), dmod, cond, *in_hbm(list(sums) + list(chain)))


CHIPS = 8
LOOP = (0, 2, 4, 6, 7, 5, 3, 1)


def swap_cores(value):
    return lax.ppermute(value, BATCH, [(d, d ^ 1) for d in range(2 * CHIPS)])


def along(value, step):
    pairs = [
        (2 * LOOP[n] + core, 2 * LOOP[(n + step) % CHIPS] + core) for n in range(CHIPS) for core in range(2)
    ]
    return lax.ppermute(value, BATCH, pairs)


def hop_kernel(spans, adds, others, spot_ref, *refs):
    n_in = 2 + len(adds)
    terms, came, refs = refs[:2], refs[2:n_in], refs[n_in + others :]
    outs = refs[: len(spans)]
    held, sem, out_sem = refs[len(spans) : -2], refs[-2], refs[-1]
    get, at = [], 0
    parts = []
    for n, (low, high) in enumerate(spans):
        rows = []
        for source in terms:
            span = pl.ds(spot_ref[n] + low, high - low)
            get.append(start(source.at[span], held[at], sem.at[at]))
            rows.append(at)
            at += 1
        parts.append(rows)
    for n, source in enumerate(came):
        get.append(start(source, held[at], sem.at[at]))
        at += 1
    for copy in get:
        copy.wait()
    put = []
    for n, (low, high) in enumerate(spans):
        made = held[at + n]
        for r in range(high - low):
            total = held[parts[n][0]][r].astype(f32) + held[parts[n][1]][r].astype(f32)
            for m, (target, first, last, skip) in enumerate(adds):
                if target == n and first <= r + low < last:
                    total = total + held[2 * len(spans) + m][r + low - skip].astype(f32)
            made[r] = total.astype(bf16)
        put.append(start(made, outs[n], out_sem.at[n]))
    for copy in put:
        copy.wait()


def hop_sums(spots, terms, spans, adds, came, after):
    rows, width = terms[0].shape[1:]
    shapes = [(high - low, rows, width) for low, high in spans]
    scratch = [pltpu.VMEM(shape, bf16) for shape in shapes for _ in range(2)]
    scratch += [pltpu.VMEM(array.shape, bf16) for array in came] + [pltpu.VMEM(shape, bf16) for shape in shapes]
    return pl.pallas_call(
        functools.partial(hop_kernel, spans, adds, len(after)),
        in_specs=[pl.BlockSpec(memory_space=pltpu.SMEM)]
        + [pl.BlockSpec(memory_space=pltpu.HBM)] * 2
        + [pl.BlockSpec(memory_space=pl.ANY)] * (len(came) + len(after)),
        out_specs=[pl.BlockSpec(memory_space=pltpu.HBM)] * len(spans),
        out_shape=[pltpu.HBM(shape, bf16) for shape in shapes],
        scratch_shapes=scratch + [pltpu.SemaphoreType.DMA((8,)), pltpu.SemaphoreType.DMA((2,))],
        compiler_params=pltpu.CompilerParams(vmem_limit_bytes=VMEM_ALL),
        cost_estimate=pl.CostEstimate(flops=0, bytes_accessed=8 * shapes[0][0] * rows * width * 2, transcendentals=0),
        name="hop",
    )(spots, *in_hbm(terms), *came, *after)


class Ring:
    def __init__(self, place, mine, other):
        self.place, self.size, self.left = place, mine.shape[0] // CHIPS, 4
        self.half = self.size // 2
        self.terms = (mine, swap_cores(other))

    def hop(self, after=()):
        n, half, size = self.left, self.half, self.size
        spots = jnp.stack([(self.place + n) % CHIPS, (self.place - n) % CHIPS]) * size
        if n == 4:
            spans, adds, came = [(0, half), (half, size)], [], []
        else:
            spans, came = [(0, size)] * 2, [self.ahead, self.behind]
            adds = [(0, 0, half, 0), (1, half, size, half)] if n == 3 else [(0, 0, size, 0), (1, 0, size, 0)]
        ahead, behind = hop_sums(spots.astype(jnp.int32), self.terms, spans, adds, came, after)
        self.sent = [ahead, behind]
        self.ahead, self.behind = along(ahead, 1), along(behind, -1)
        self.left -= 1

    def held(self, count=2):
        self.count = count
        return list(self.terms[:count])

    def later(self, made):
        self.terms = tuple(made[-self.count :]) + self.terms[self.count :]
        return made[: -self.count]

    def finish(self, after=()):
        spots = jnp.reshape(self.place * self.size, (1,)).astype(jnp.int32)
        adds = [(0, 0, self.size, 0)] * 2
        return hop_sums(spots, self.terms, [(0, self.size)], adds, [self.ahead, self.behind], after)[0]


def time_features(steps_in):
    half_width = D // 2
    freqs = jnp.exp(-math.log(10000.0) * jnp.arange(half_width, dtype=f32) / half_width)
    angles = steps_in.astype(f32)[:, None] * freqs[None, :]
    return jnp.concatenate([jnp.cos(angles), jnp.sin(angles)], axis=1)


def body(tokens, cotangent, loss_weight, timesteps, owners, master, first_moment, second_moment):
    section_index = lax.axis_index(SECTION)
    me = lax.axis_index(BATCH)
    owner_total = lax.axis_size(BATCH)
    slots, panel_rows = master.shape[1], master.shape[2]
    clips = timesteps.shape[0]
    length = tokens.shape[0] // clips
    low = master[0].astype(bf16)
    owner = owners[0] + (0.0 * low[0, 0, 0].astype(f32)).astype(jnp.int32)
    panels = owner.shape[0]
    moved = DOWN_END // panel_rows
    cap = min(slots, max(4, (slots * 25 + 30) // 31))
    section = jnp.reshape(section_index, (1,)).astype(jnp.int32)

    number = jnp.arange(panels, dtype=jnp.int32)
    same = (owner[:, None] == owner[None, :]) & (number[None, :] < number[:, None])
    rank = jnp.sum(same.astype(jnp.int32), axis=1)
    first_size = owner_total * cap
    place = jnp.where(
        rank < cap, owner * cap + rank, first_size + owner * (slots - cap) + rank - cap
    )[:moved]
    mine = (owner[None, :] == me) & (
        rank[None, :] == jnp.arange(slots, dtype=jnp.int32)[:, None]
    )
    slot_panel = jnp.sum(jnp.where(mine, number[None, :] + 1, 0), axis=1) - 1
    kind = jnp.where(slot_panel < 0, 0, jnp.where(slot_panel < moved, 1, 2)).astype(jnp.int32)
    grad_row = jnp.where(kind == 2, (slot_panel - moved) * panel_rows, 0).astype(jnp.int32)

    rings = owner_total == 2 * CHIPS
    code, index, slot_code, slot_index, sizes, beyond = routes(owner, rank, mine, me, owner_total, slots, moved)
    gathered = lax.all_gather(low[:cap], BATCH, axis=0, tiled=True)
    spot = jnp.arange(owner_total * clips, dtype=jnp.int32) // clips == me
    news = [jnp.where(spot, jnp.tile(timesteps.astype(f32), owner_total), 0.0)]
    past = jnp.max(jnp.where(number < moved, rank, 0)) >= cap
    news.append(jnp.stack([past, beyond]).astype(f32) + 0.0 * low[0, 0, 0].astype(f32))
    news = lax.pmax(jnp.concatenate(news), (SECTION, BATCH))
    all_steps = news[:-2]
    beyond = news[-1] > 0.5
    sources = [gathered]
    if cap < slots:
        rest_shape = (owner_total * (slots - cap), panel_rows, D)
        sources.append(
            lax.cond(
                news[-2] + 0.0 * gathered[0, 0, 0].astype(f32) > 0.5,
                lambda part: lax.all_gather(part, BATCH, axis=0, tiled=True),
                lambda part: jnp.zeros(rest_shape, bf16),
                low[cap:],
            )
        )
    sheet = assemble(place, sources, moved)

    cond = jax.nn.silu(time_features(all_steps)).astype(bf16)
    clip_total = cond.shape[0]
    share = jnp.einsum("cd,sd->cs", cond, low.reshape(slots * panel_rows, D), preferred_element_type=f32)
    share = lax.all_to_all(
        share.reshape(owner_total, clips, slots * panel_rows), BATCH, split_axis=0, concat_axis=0, tiled=True
    )
    share = share.reshape(owner_total, clips, slots, panel_rows).transpose(1, 0, 2, 3)
    share = share.reshape(clips, owner_total * slots, panel_rows)
    pick = (
        (owner * slots + rank)[moved:, None] == jnp.arange(owner_total * slots, dtype=jnp.int32)[None, :]
    ).astype(f32)
    mod = jnp.einsum("ps,csr->cpr", pick, share, precision=lax.Precision.HIGHEST)
    mod = mod.reshape(clips, 6, D)

    run = functools.partial
    base = dict(clips=clips, length=length, section=section, mod=mod, sheet=sheet)
    firsts, outs = [], None
    for c in range(clips):
        firsts.append(first_forward(c, x=tokens, outs=outs, **base))
        outs = firsts[c][N_OUTS]
    received = [lax.ppermute(f[N_SENT], SECTION, [(0, 1)]) for f in firsts]
    seconds, gin = [], None
    for c in range(clips):
        chain = {n: firsts[c][n] for n in (N_H1, N_O, N_H2, N_Z)} | {N_OUTS: outs, N_GIN: gin}
        seconds.append(second_both(c, loss_weight=loss_weight, x=received[c], g=cotangent, chain=chain, **base))
        outs, gin = seconds[c][N_OUTS], seconds[c][N_GIN]
    received = [lax.ppermute(f[N_SENT], SECTION, [(1, 0)]) for f in seconds]
    every = [dict(f) for f in seconds]

    all_jobs = ((N_Z, N_DB, UP_END), (N_DU, N_H2, PROJ_END), (N_DA, N_O, QKV_END), (N_DQKV, N_H1, 0))
    grads = run(weight_grads, code=code, index=index, length=length, panel_rows=panel_rows)
    partial, after = None, mod
    for c in range(clips):
        chain = {n: every[c][n] for n in BACK_MAKES} | {N_GIN: gin}
        every[c] |= first_back(c, x=tokens, g=received[c], kept=firsts[c], chain=chain, after=after, **base)
        gin, after = every[c][N_GIN], every[c][N_DMOD_ATT]
        if rings and c == clips - 2:
            (partial,) = grads(all_jobs, every=every[:-1], sizes=[moved], plain=True)
            after = partial

    dmod = [jnp.concatenate([e[N_DMOD_ATT], e[N_DMOD_FFN]]) for e in every]
    dmod = jnp.stack(dmod).reshape(1, clips, 6 * D).astype(bf16)
    dmod = lax.all_to_all(
        jnp.broadcast_to(dmod, (owner_total, clips, 6 * D)), BATCH, split_axis=0, concat_axis=0, tiled=True
    )
    slot_code = jnp.where(kind == 1, slot_code + 2, jnp.where(kind == 2, 1, 0)).astype(jnp.int32)
    update = run(
        adam, code=slot_code, index=slot_index, row=grad_row, master=master[0], first=first_moment[0],
        second=second_moment[0], dmod=dmod.reshape(clip_total, 6 * D).T, cond=cond,
    )
    if rings:
        place = me // 4 + (me // 2) % 2 * (CHIPS - 1 - 2 * (me // 4))
        wide = [sizes[1]] * 2 + [sizes[2]]
        first_jobs = ((N_DA, N_O, QKV_END), (N_DQKV, N_H1, 0), (N_DU, N_H2, PROJ_END))
        now = every[-1:] if partial is not None else every
        made = grads(first_jobs, every=now, sizes=[sizes[0]] * 2 + wide, partial=partial)
        first = Ring(place, *made[:2])
        made = grads(
            ((N_Z, N_DB, UP_END),), every=now, sizes=wide, thread=made[2:], through=first.held(1), partial=partial
        )
        made = first.later(made)
        second = Ring(place, *made[:2])
        rest = lax.cond(
            beyond,
            lambda part: lax.psum_scatter(part, BATCH, scatter_dimension=0, tiled=True),
            lambda part: jnp.zeros((slots, panel_rows, D), bf16),
            made[2],
        )
        first.hop()
        second.hop()
        first.hop(after=[rest, second.ahead, second.behind])
        second.hop()
        first.hop()
        second.hop()
        first.hop(after=[dmod])
        results = update(0, 2, sums=[], chain=[])
        second.hop(after=results[3:])
        half = first.finish()
        sums = [half, swap_cores(half)]
        results = update(2, 4, sums=sums, chain=results)
        half = second.finish(after=results[3:])
        sums += [half, swap_cores(half), rest]
        results = update(4, 7, sums=sums, chain=results)
    else:
        (made,) = grads(all_jobs, every=every, sizes=[sizes[0]])
        sums = [lax.psum_scatter(made, BATCH, scatter_dimension=0, tiled=True)]
        results = update(0, 3, sums=sums, chain=[])
    return (outs[None], gin[None], *(r[None] for r in results))


CAPS = (24, 24)


def count_before(flag, group):
    number = jnp.arange(group.shape[0], dtype=jnp.int32)
    before = (group[:, None] == group[None, :]) & (number[None, :] < number[:, None]) & flag[None, :]
    return jnp.sum(before.astype(jnp.int32), axis=1)


def routes(owner, rank, mine, me, owner_total, slots, moved):
    if owner_total != 2 * CHIPS:
        code = jnp.zeros((moved,), jnp.int32)
        return code, (owner * slots + rank)[:moved], jnp.zeros((slots,), jnp.int32), jnp.arange(slots, dtype=jnp.int32), [owner_total * slots], jnp.bool_(False)
    number = jnp.arange(moved, dtype=jnp.int32)
    held, core = owner[:moved], me % 2
    chip = held // 2
    spot = chip // 2 + chip % 2 * (CHIPS - 1 - 2 * (chip // 2))
    per_row = DOWN_END // moved
    down = number >= UP_END // per_row
    order = count_before(~down, chip)
    late = down | (order >= CAPS[0])
    order = jnp.where(late, count_before(late, chip), order)
    rest = late & (order >= CAPS[1])
    half = order % 2
    size = jnp.where(late, CAPS[1] // 2, CAPS[0] // 2)
    index = jnp.where(rest, held * slots + rank[:moved], spot * size + order // 2)
    away = (half != core).astype(jnp.int32)
    code = jnp.where(rest, 4, jnp.where(late, 2 + away, away))
    code = jnp.where(down, code - 2, code).astype(jnp.int32)
    taken = mine[:, :moved].astype(jnp.int32)
    found = jnp.where(rest, 4, 2 * late.astype(jnp.int32) + away)
    slot_code = jnp.sum(taken * found[None, :], axis=1)
    slot_index = jnp.sum(taken * jnp.where(rest, rank[:moved], order // 2)[None, :], axis=1)
    sizes = [CHIPS * cap // 2 for cap in CAPS] + [owner_total * slots]
    return code, index.astype(jnp.int32), slot_code.astype(jnp.int32), slot_index.astype(jnp.int32), sizes, jnp.any(rest)


def solution(mesh):
    placed = (
        P(BATCH, None),
        P(BATCH, None),
        P(BATCH),
        P(BATCH),
        P(SECTION, None),
        P(SECTION, BATCH, None, None),
        P(SECTION, BATCH, None, None),
        P(SECTION, BATCH, None, None),
    )
    return jax.shard_map(
        body,
        mesh=mesh,
        in_specs=placed,
        out_specs=(
            P(SECTION, BATCH, None),
            P(SECTION, BATCH, None),
            P(SECTION, BATCH, None, None),
            P(SECTION, BATCH, None, None),
            P(SECTION, BATCH, None, None),
            P(SECTION, BATCH, None, None),
        ),
        check_vma=False,
    )
```

```python
import functools
import math

import jax
import jax.numpy as jnp
from jax import lax
from jax.experimental import pallas as pl
from jax.experimental.pallas import tpu as pltpu
from jax.sharding import PartitionSpec as P

D = 768
HEADS = 12
HEAD_DIM = 64
FF = 3072
STEP = 10
QKV_END = 3 * D
PROJ_END = 4 * D
UP_END = 4 * D + FF
DOWN_END = 4 * D + 2 * FF

norm_eps = 1e-06
adam_eps = 1e-08
learn_rate = 0.03
decay_rate = 0.1
beta_one = 0.5
beta_two = 0.5

bf16 = jnp.bfloat16
f32 = jnp.float32
SECTION, BATCH = "section", "batch"
VMEM_LIMIT = 46 * 1024 * 1024
VMEM_ALL = 58 * 1024 * 1024
ROWS = 128
GELU_C = math.sqrt(2.0 / math.pi)


def dot_nn(a, b):
    return lax.dot_general(a, b, (((1,), (0,)), ((), ())), preferred_element_type=f32)


def dot_nt(a, b):
    return lax.dot_general(a, b, (((1,), (1,)), ((), ())), preferred_element_type=f32)


def dot_tn(a, b):
    return lax.dot_general(a, b, (((0,), (0,)), ((), ())), preferred_element_type=f32)


def in_hbm(arrays):
    return [pltpu.with_memory_space_constraint(a, pltpu.HBM) for a in arrays]


def start(src, dst, sem):
    copy = pltpu.make_async_copy(src, dst, sem)
    copy.start()
    return copy


def norm(values):
    average = jnp.mean(values, axis=-1, keepdims=True)
    centred = values - average
    variance = jnp.mean(centred * centred, axis=-1, keepdims=True)
    inverse = lax.rsqrt(variance + norm_eps)
    return centred * inverse, inverse


def norm_back(grad, values, scale_row):
    normed, inverse = norm(values)
    dn = grad * (1.0 + scale_row)
    mean_one = jnp.mean(dn, axis=-1, keepdims=True)
    mean_two = jnp.mean(dn * normed, axis=-1, keepdims=True)
    dx = inverse * (dn - mean_one - normed * mean_two)
    return dx, jnp.sum(grad, axis=0, keepdims=True), jnp.sum(grad * normed, axis=0, keepdims=True)


def gelu_both(u):
    square = u * u
    half = 0.5 * jnp.tanh(u * (square * (0.044715 * GELU_C) + GELU_C)) + 0.5
    bend = u * (square * (6.0 * 0.044715 * GELU_C) + 2.0 * GELU_C)
    return u * half, half + half * (1.0 - half) * bend


def assemble_kernel(panels, first_size, index_ref, *refs):
    sources, sheet, sem = refs[:-2], refs[-2], refs[-1]
    rows = sheet.shape[0] // panels

    @pl.loop(0, panels, unroll=4)
    def _(p):
        where = index_ref[p]
        target = sheet.at[pl.ds(pl.multiple_of(p * rows, rows), rows)]
        if len(sources) == 1:
            pltpu.make_async_copy(sources[0].at[where], target, sem).start()
        else:

            @pl.when(where < first_size)
            def _():
                pltpu.make_async_copy(sources[0].at[where], target, sem).start()

            @pl.when(where >= first_size)
            def _():
                pltpu.make_async_copy(sources[1].at[where - first_size], target, sem).start()

    pltpu.make_async_copy(sheet, sheet, sem).wait()


def assemble(index, sources, panels):
    first_size = sources[0].shape[0]
    rows = sources[0].shape[1]
    return pl.pallas_call(
        functools.partial(assemble_kernel, panels, first_size),
        out_shape=pltpu.VMEM((panels * rows, D), bf16),
        in_specs=[pl.BlockSpec(memory_space=pltpu.SMEM)]
        + [pl.BlockSpec(memory_space=pltpu.HBM)] * len(sources),
        out_specs=pl.BlockSpec(memory_space=pltpu.VMEM),
        scratch_shapes=[pltpu.SemaphoreType.DMA],
        compiler_params=pltpu.CompilerParams(vmem_limit_bytes=VMEM_LIMIT),
        cost_estimate=pl.CostEstimate(flops=0, bytes_accessed=2 * panels * rows * D, transcendentals=0),
        name="assemble",
    )(index, *in_hbm(sources))


(
    N_XIN,
    N_H1,
    N_QKV,
    N_LSE,
    N_O,
    N_A,
    N_X1,
    N_H2,
    N_SLOPE,
    N_Z,
    N_B,
    N_OUT,
    N_DB,
    N_DU,
    N_DA,
    N_DX1,
    N_DMOD_FFN,
    N_DQKV,
    N_DMOD_ATT,
    N_G,
    N_SENT,
    N_DO,
    N_ACC,
    N_LSE_COLS,
    N_OUTS,
    N_GIN,
    N_MOD,
    N_X,
    N_AFTER,
    N_SECTION,
    N_LOSS,
) = range(31)


TILE = D
TILES = FF // TILE
PAIRS = HEADS // 2


def shapes_of(length):
    return {
        N_XIN: ((length, D), bf16),
        N_H1: ((length, D), bf16),
        N_QKV: ((length, 3 * D), bf16),
        N_LSE: ((16, length), f32),
        N_O: ((length, D), bf16),
        N_A: ((length, D), bf16),
        N_X1: ((length, D), f32),
        N_H2: ((length, D), bf16),
        N_SLOPE: ((length, FF), f32),
        N_Z: ((length, FF), bf16),
        N_B: ((length, D), bf16),
        N_OUT: ((length, D), bf16),
        N_DB: ((length, D), bf16),
        N_DU: ((length, FF), bf16),
        N_DA: ((length, D), bf16),
        N_DX1: ((length, D), f32),
        N_DMOD_FFN: ((4, D), f32),
        N_DQKV: ((length, 3 * D), bf16),
        N_DMOD_ATT: ((2, D), f32),
        N_G: ((length, D), bf16),
        N_SENT: ((length, D), bf16),
        N_DO: ((length, D), bf16),
        N_ACC: ((length, D), f32),
        N_LSE_COLS: ((length, 128), f32),
    }


def blocks_of(length):
    return [pl.ds(r, ROWS) for r in range(0, length, ROWS)]


def low_half():
    return lax.broadcasted_iota(jnp.int32, (1, 128), 1) < HEAD_DIM


def forward_qkv(v, w_qkv, row, length):
    for block in blocks_of(length):
        normed, _ = norm(v[N_XIN][block, :].astype(f32))
        v[N_H1][block, :] = (normed * (1.0 + row(1)) + row(0)).astype(bf16)
    for n in range(3):
        part = dot_nt(v[N_H1][...], w_qkv(n))
        v[N_QKV][:, n * D : (n + 1) * D] = part.astype(bf16)


def forward_attention(v, length):
    low_lanes = low_half()
    room = FF // length
    columns = lax.broadcasted_iota(jnp.int32, (1, 128), 1)

    def scores(head):
        at = slice(head // 2 * 128, head // 2 * 128 + 128)
        q = v[N_QKV][:, at] * jnp.asarray(HEAD_DIM ** (-0.5), bf16)
        qh = jnp.where(low_lanes if head % 2 == 0 else ~low_lanes, q, jnp.zeros_like(q))
        first = head % room * length
        v[N_SLOPE][:, first : first + length] = dot_nt(qh, v[N_QKV][:, D + at.start : D + at.stop])

    def softmax(head):
        span = slice(head % room * length, head % room * length + length)
        for block in blocks_of(length):
            s = v[N_SLOPE][block, span]
            top = jnp.max(s, axis=-1, keepdims=True)
            e = jnp.exp(s - top)
            total = jnp.sum(e, axis=-1, keepdims=True)
            v[N_Z][block, span] = (e * (1.0 / total)).astype(bf16)
            line = top + jnp.log(total)
            v[N_LSE_COLS][block, :] = jnp.where(columns == head, line, v[N_LSE_COLS][block, :]) if head else jnp.where(columns == 0, line, 0.0)

    def mix(head):
        at = slice(2 * D + head // 2 * 128, 2 * D + head // 2 * 128 + 128)
        span = slice(head % room * length, head % room * length + length)
        return dot_nn(v[N_Z][:, span], v[N_QKV][:, at])

    scores(0)
    mixed = [None] * HEADS
    for head in range(HEADS):
        if head + 1 < HEADS:
            scores(head + 1)
        softmax(head)
        mixed[head] = mix(head)
        if head % 2:
            at = slice(head // 2 * 128, head // 2 * 128 + 128)
            v[N_O][:, at] = jnp.where(low_lanes, mixed[head - 1], mixed[head]).astype(bf16)
    v[N_LSE][...] = v[N_LSE_COLS][...].T[:16, :]


def forward_proj(v, w_proj, row, length):
    v[N_ACC][...] = dot_nt(v[N_O][...], w_proj)
    for block in blocks_of(length):
        branch = v[N_ACC][block, :]
        v[N_A][block, :] = branch.astype(bf16)
        middle = v[N_XIN][block, :].astype(f32) + row(2) * branch
        v[N_X1][block, :] = middle
        normed, _ = norm(middle)
        v[N_H2][block, :] = (normed * (1.0 + row(4)) + row(3)).astype(bf16)


def forward_ffn(v, w_up, w_down, row, length, after):
    for n in range(TILES):
        span = slice(n * TILE, (n + 1) * TILE)
        v[N_SLOPE][:, span] = dot_nt(v[N_H2][...], w_up(n))
        for block in blocks_of(length):
            value, slope = gelu_both(v[N_SLOPE][block, span])
            v[N_Z][block, span] = value.astype(bf16)
            v[N_SLOPE][block, span] = slope
        part = dot_nn(v[N_Z][:, span], w_down(n))
        if n:
            v[N_ACC][...] += part
        else:
            v[N_ACC][...] = part
        after(n)
    for block in blocks_of(length):
        branch = v[N_ACC][block, :]
        v[N_B][block, :] = branch.astype(bf16)
        v[N_OUT][block, :] = (v[N_X1][block, :] + row(5) * branch).astype(bf16)


def back_gate(v, row, length, scale):
    gate_two = jnp.zeros((1, D), f32)
    for block in blocks_of(length):
        g = v[N_G][block, :].astype(f32)
        if scale is not None:
            g = g * scale
        v[N_DX1][block, :] = g
        v[N_DB][block, :] = (row(5) * g).astype(bf16)
        gate_two += jnp.sum(g * v[N_B][block, :].astype(f32), axis=0, keepdims=True)
    v[N_DMOD_FFN][3:4, :] = gate_two


def back_ffn_part(v, w_up, w_down, row, length, before, after):
    for n in range(TILES):
        span = slice(n * TILE, (n + 1) * TILE)
        before(n)
        dz = dot_nt(v[N_DB][...], w_down(n))
        v[N_DU][:, span] = (dz * v[N_SLOPE][:, span]).astype(bf16)
        part = dot_nn(v[N_DU][:, span], w_up(n))
        if n:
            v[N_ACC][...] += part
        else:
            v[N_ACC][...] = part
        after(n)


def back_middle(v, row, length):
    shift_two = jnp.zeros((1, D), f32)
    scale_two = jnp.zeros((1, D), f32)
    gate_one = jnp.zeros((1, D), f32)
    for block in blocks_of(length):
        dx, shift_part, scale_part = norm_back(v[N_ACC][block, :], v[N_X1][block, :], row(4))
        total = v[N_DX1][block, :] + dx
        v[N_DX1][block, :] = total
        shift_two += shift_part
        scale_two += scale_part
        gate_one += jnp.sum(total * v[N_A][block, :].astype(f32), axis=0, keepdims=True)
        v[N_DA][block, :] = (row(2) * total).astype(bf16)
    v[N_DMOD_FFN][0:1, :] = gate_one
    v[N_DMOD_FFN][1:2, :] = shift_two
    v[N_DMOD_FFN][2:3, :] = scale_two


def back_attention(v, w_proj, length):
    v[N_DO][...] = dot_nn(v[N_DA][...], w_proj).astype(bf16)
    low_lanes = low_half()
    scale = HEAD_DIM ** (-0.5)

    def parts(head):
        at = head // 2 * 128
        keep = lambda a: jnp.where(low_lanes if head % 2 == 0 else ~low_lanes, a, jnp.zeros_like(a))
        qh, doh = keep(v[N_QKV][:, at : at + 128]), keep(v[N_DO][:, at : at + 128])
        kh = keep(v[N_QKV][:, D + at : D + at + 128])
        return qh, kh, doh

    def first(head):
        at = head // 2 * 128
        qh, kh, doh = parts(head)
        st = dot_nt(v[N_QKV][:, D + at : D + at + 128], qh * jnp.asarray(scale, bf16))
        dpt = dot_nt(v[N_QKV][:, 2 * D + at : 2 * D + at + 128], doh)
        return st, dpt, qh, kh, doh

    def rest(head, st, dpt, qh, kh, doh):
        pt = jnp.exp(st - v[N_LSE][head : head + 1, :])
        dv = dot_nn(pt.astype(bf16), doh)
        inner = jnp.sum(dpt * pt, axis=0, keepdims=True)
        drt = (pt * (dpt - inner) * scale).astype(bf16)
        return dot_tn(drt, kh), dot_nn(drt, qh), dv

    ahead = first(0)
    made = None
    for head in range(HEADS):
        now = ahead
        if head + 1 < HEADS:
            ahead = first(head + 1)
        made_now = rest(head, *now)
        if head % 2:
            for n in range(3):
                at = n * D + head // 2 * 128
                v[N_DQKV][:, at : at + 128] = (made[n] + made_now[n]).astype(bf16)
        made = made_now


def back_input(v, w_qkv, row, length):
    v[N_ACC][...] = dot_nn(v[N_DQKV][...], w_qkv)
    shift_one = jnp.zeros((1, D), f32)
    scale_one = jnp.zeros((1, D), f32)
    for block in blocks_of(length):
        dx, shift_part, scale_part = norm_back(v[N_ACC][block, :], v[N_XIN][block, :].astype(f32), row(1))
        total = v[N_DX1][block, :] + dx
        v[N_DX1][block, :] = total
        v[N_SENT][block, :] = total.astype(bf16)
        shift_one += shift_part
        scale_one += scale_part
    v[N_DMOD_ATT][0:1, :] = shift_one
    v[N_DMOD_ATT][1:2, :] = scale_one


class Mover:
    def __init__(self, sems):
        self.sems, self.used, self.coming, self.going = sems, 0, {}, []

    def start(self, src, dst):
        copy = pltpu.make_async_copy(src, dst, self.sems.at[self.used])
        self.used += 1
        copy.start()
        return copy

    def fetch(self, name, src, dst):
        self.coming[name] = self.start(src, dst)

    def need(self, *names):
        for name in names:
            if name in self.coming:
                self.coming.pop(name).wait()

    def save(self, src, dst):
        self.going.append(self.start(src, dst))

    def finish(self):
        assert not self.coming
        for copy in self.going:
            copy.wait()


SEMS = 48


def call_block(kernel, name, want, clip, length, smem, sheet, read, write, hold, shared, chain, flops, moved, loose=None):
    any_spec = pl.BlockSpec(memory_space=pltpu.HBM)
    shapes = shapes_of(length)
    s_names, r_names, w_names = list(smem), list(read), list(write)
    chained = [n for n in w_names if chain.get(n) is not None]
    operands = [smem[n] for n in s_names] + [pltpu.with_memory_space_constraint(sheet, pltpu.VMEM)]
    operands += [read[n] if n == loose else in_hbm([read[n]])[0] for n in r_names]
    aliases = {len(operands) + i: w_names.index(n) for i, n in enumerate(chained)}
    operands += in_hbm([chain[n] for n in chained])

    def run(*refs):
        refs = list(refs)
        take = lambda names: dict(zip(names, [refs.pop(0) for _ in names]))
        s, w, r = take(s_names), refs.pop(0), take(r_names)
        take(chained)
        o = take(w_names)
        v = take(hold)
        v |= {n: v[other] for n, other in shared.items()}
        m, sems = refs

        @pl.when(s[N_SECTION][0] == want)
        def _():
            kernel(clip, length, s, m, r, o, v, w, Mover(sems))

    results = pl.pallas_call(
        run,
        out_shape=[pltpu.HBM(*write[n]) for n in w_names],
        in_specs=[pl.BlockSpec(memory_space=pltpu.SMEM)] * len(s_names)
        + [pl.BlockSpec(memory_space=pltpu.VMEM)]
        + [any_spec] * (len(r_names) + len(chained)),
        out_specs=[any_spec] * len(w_names),
        scratch_shapes=[pltpu.VMEM(*shapes[n]) for n in hold]
        + [pltpu.VMEM((6, D), f32), pltpu.SemaphoreType.DMA((SEMS,))],
        input_output_aliases=aliases,
        compiler_params=pltpu.CompilerParams(vmem_limit_bytes=VMEM_LIMIT),
        cost_estimate=pl.CostEstimate(flops=flops, bytes_accessed=moved, transcendentals=0),
        name=f"{name}_{clip}",
    )(*operands)
    return dict(zip(w_names, results))


def mod_row(m):
    return lambda n: m[n : n + 1, :]


def forward_body(clip, length, x_offset, m, r, v, w, mover, keep):
    row = mod_row(m)
    mover.fetch(N_MOD, r[N_MOD].at[clip], m)
    mover.fetch(N_XIN, r[N_X].at[pl.ds(x_offset, length)], v[N_XIN])
    mover.need(N_MOD, N_XIN)
    forward_qkv(v, lambda n: w[n * D : (n + 1) * D, :], row, length)
    keep(N_H1)
    keep(N_QKV)
    forward_attention(v, length)
    keep(N_LSE)
    keep(N_O)
    forward_proj(v, w[QKV_END:PROJ_END, :], row, length)
    keep(N_A)
    keep(N_X1)
    keep(N_H2)
    forward_ffn(
        v,
        lambda n: w[PROJ_END + n * D : PROJ_END + (n + 1) * D, :],
        lambda n: w[UP_END + n * D : UP_END + (n + 1) * D, :],
        row,
        length,
        lambda n: (keep(N_SLOPE, n), keep(N_Z, n)),
    )
    keep(N_B)


def saver(mover, v, o):
    def keep(name, n=None):
        if name not in o:
            return
        if n is None:
            mover.save(v[name], o[name])
        else:
            span = pl.ds(n * TILE, TILE)
            mover.save(v[name].at[:, span], o[name].at[:, span])

    return keep


FIRST_KEEP = (N_H1, N_QKV, N_LSE, N_O, N_A, N_X1, N_H2, N_SLOPE, N_Z, N_B)
BOTH_KEEP = (N_H1, N_O, N_H2, N_Z, N_DB, N_DU, N_DA, N_DQKV, N_DMOD_FFN, N_DMOD_ATT)


def first_forward(clip, clips, length, section, mod, x, sheet, outs):
    def kernel(clip, length, s, m, r, o, v, w, mover):
        forward_body(clip, length, clip * length, m, r, v, w, mover, saver(mover, v, o))
        mover.save(v[N_OUT], o[N_SENT])
        mover.save(v[N_OUT], o[N_OUTS].at[pl.ds(clip * length, length)])
        mover.finish()

    shapes = shapes_of(length)
    write = {n: shapes[n] for n in FIRST_KEEP}
    write |= {N_OUTS: ((clips * length, D), bf16), N_SENT: ((length, D), bf16)}
    hold = FIRST_KEEP + (N_XIN, N_OUT, N_ACC, N_LSE_COLS)
    return call_block(
        kernel, "first_forward", 0, clip, length, {N_SECTION: section}, sheet, {N_MOD: mod, N_X: x},
        write, hold, {}, {N_OUTS: outs}, 17 * 10**9, 30 << 20,
    )


def second_both(clip, clips, length, section, loss_weight, mod, x, g, sheet, chain):
    def kernel(clip, length, s, m, r, o, v, w, mover):
        keep = saver(mover, v, o)
        row = mod_row(m)
        forward_body(clip, length, 0, m, r, v, w, mover, keep)
        mover.fetch(N_G, r[N_G].at[pl.ds(clip * length, length)], v[N_G])
        mover.save(v[N_OUT], o[N_OUTS].at[pl.ds(clip * length, length)])
        mover.need(N_G)
        back_gate(v, row, length, s[N_LOSS][clip])
        keep(N_DB)
        back_ffn_part(
            v,
            lambda n: w[PROJ_END + n * D : PROJ_END + (n + 1) * D, :],
            lambda n: w[UP_END + n * D : UP_END + (n + 1) * D, :],
            row, length, lambda n: None, lambda n: keep(N_DU, n),
        )
        back_middle(v, row, length)
        keep(N_DA)
        keep(N_DMOD_FFN)
        back_attention(v, w[QKV_END:PROJ_END, :], length)
        keep(N_DQKV)
        back_input(v, w[0:QKV_END, :], row, length)
        mover.save(v[N_SENT], o[N_SENT])
        keep(N_DMOD_ATT)
        mover.save(v[N_DX1], o[N_GIN].at[pl.ds(clip * length, length)])
        mover.finish()

    shapes = shapes_of(length)
    write = {n: shapes[n] for n in BOTH_KEEP}
    write |= {N_OUTS: ((clips * length, D), bf16), N_GIN: ((clips * length, D), f32), N_SENT: ((length, D), bf16)}
    hold = (N_XIN, N_H1, N_QKV, N_LSE, N_O, N_A, N_X1, N_H2, N_SLOPE, N_Z, N_B, N_OUT, N_DB, N_DU, N_DX1)
    hold += (N_DMOD_FFN, N_DMOD_ATT, N_G, N_ACC, N_LSE_COLS)
    shared = {N_DQKV: N_QKV, N_DO: N_B, N_DA: N_A, N_SENT: N_G}
    return call_block(
        kernel, "second_both", 1, clip, length, {N_SECTION: section, N_LOSS: loss_weight},  sheet,
        {N_MOD: mod, N_X: x, N_G: g}, write, hold, shared, chain, 40 * 10**9, 40 << 20, N_X,
    )


BACK_MAKES = (N_DB, N_DU, N_DA, N_DQKV, N_DMOD_FFN, N_DMOD_ATT)


def first_back(clip, clips, length, section, mod, x, g, sheet, kept, chain, after):
    def kernel(clip, length, s, m, r, o, v, w, mover):
        keep = saver(mover, v, o)
        row = mod_row(m)
        mover.fetch(N_MOD, r[N_MOD].at[clip], m)
        mover.fetch(N_G, r[N_G], v[N_G])
        mover.fetch(N_B, r[N_B], v[N_B])
        for n in range(TILES):
            span = pl.ds(n * TILE, TILE)
            mover.fetch((N_SLOPE, n), r[N_SLOPE].at[:, span], v[N_SLOPE].at[:, span])
        for name in (N_X1, N_A, N_QKV, N_LSE):
            mover.fetch(name, r[name], v[name])
        mover.fetch(N_XIN, r[N_X].at[pl.ds(clip * length, length)], v[N_XIN])
        mover.need(N_MOD, N_G, N_B)
        back_gate(v, row, length, None)
        keep(N_DB)
        back_ffn_part(
            v,
            lambda n: w[PROJ_END + n * D : PROJ_END + (n + 1) * D, :],
            lambda n: w[UP_END + n * D : UP_END + (n + 1) * D, :],
            row, length, lambda n: mover.need((N_SLOPE, n)), lambda n: keep(N_DU, n),
        )
        mover.need(N_X1, N_A)
        back_middle(v, row, length)
        keep(N_DA)
        keep(N_DMOD_FFN)
        mover.need(N_QKV, N_LSE)
        back_attention(v, w[QKV_END:PROJ_END, :], length)
        keep(N_DQKV)
        mover.need(N_XIN)
        back_input(v, w[0:QKV_END, :], row, length)
        keep(N_DMOD_ATT)
        mover.save(v[N_DX1], o[N_GIN].at[pl.ds(clip * length, length)])
        mover.finish()

    shapes = shapes_of(length)
    read = {N_MOD: mod, N_X: x, N_G: g} | {n: kept[n] for n in (N_B, N_SLOPE, N_X1, N_A, N_QKV, N_LSE)}
    read[N_AFTER] = after
    write = {n: shapes[n] for n in BACK_MAKES} | {N_GIN: ((clips * length, D), f32)}
    hold = (N_G, N_B, N_SLOPE, N_X1, N_A, N_QKV, N_LSE, N_XIN, N_DB, N_DU, N_DX1, N_DMOD_FFN, N_DMOD_ATT, N_ACC)
    shared = {N_DQKV: N_QKV, N_DO: N_B, N_DA: N_A, N_SENT: N_G}
    return call_block(
        kernel, "first_back", 0, clip, length, {N_SECTION: section}, sheet, read,
        write, hold, shared, chain, 25 * 10**9, 30 << 20, N_G,
    )


def grads_kernel(jobs, clips, length, panel_rows, plain, added, own, passed, others, code_ref, index_ref, *refs):
    count = 2 * len(jobs) * clips
    sources, partial = refs[:count], refs[count + others - 1]
    refs = refs[count + others :]
    outs = refs[:own]
    scratch = refs[own + passed :]
    values = scratch[: 2 * len(jobs)]
    tile_v, add_v, in_sem, add_sem, out_sem = scratch[2 * len(jobs) :]
    per_tile = D // panel_rows
    tiles = []
    for n, (left, right, base) in enumerate(jobs):
        tiles += [(n, column, base + column) for column in range(0, values[2 * n].shape[1], D)]
    get, more = {}, {}

    def fetch(n, column):
        get[n, column] = [
            start(
                sources[n * clips + c].at[:, pl.ds(column, D)],
                values[n].at[pl.ds(c * length, length), pl.ds(column, D)],
                in_sem.at[len(get), c],
            )
            for c in range(clips)
        ]

    def fetch_tile(t):
        if t < len(tiles):
            n, column, _ = tiles[t]
            if column == 0:
                fetch(2 * n + 1, 0)
            fetch(2 * n, column)
            if added:
                first_panel = tiles[t][2] // panel_rows
                more[t] = start(partial.at[pl.ds(first_panel, per_tile)], add_v.at[t % 4], add_sem.at[t % 4])

    for t in range(3):
        fetch_tile(t)
    def drain(slot):
        pltpu.make_async_copy(outs[-1].at[pl.ds(0, per_tile)], tile_v.at[slot], out_sem.at[slot]).wait()

    for t, (n, column, first_row) in enumerate(tiles):
        slot = t % 2
        if column == 0:
            for copy in get[2 * n + 1, 0]:
                copy.wait()
        for copy in get[2 * n, column]:
            copy.wait()
        fetch_tile(t + 3)
        if t >= 2:
            drain(slot)
        part = dot_tn(values[2 * n][:, column : column + D], values[2 * n + 1][...])
        if added:
            more[t].wait()
            part = part + add_v[t % 4].reshape(D, D).astype(f32)
        tile_v[slot, :, :, :] = part.astype(bf16).reshape(per_tile, panel_rows, D)
        if plain:
            first_panel = first_row // panel_rows
            pltpu.make_async_copy(tile_v.at[slot], outs[0].at[pl.ds(first_panel, per_tile)], out_sem.at[slot]).start()
            continue

        @pl.loop(0, per_tile)
        def _(p):
            code = code_ref[first_row // panel_rows + p]
            where = index_ref[first_row // panel_rows + p]

            def put(numbers):
                for n_out in numbers:

                    @pl.when(code == n_out)
                    def _():
                        pltpu.make_async_copy(tile_v.at[slot, p], outs[n_out].at[where], out_sem.at[slot]).start()

            put(range(min(2, own)))
            if own > 2:

                @pl.when(code >= 2)
                def _():
                    put(range(2, own))

    for slot in range(min(2, len(tiles))):
        drain(slot)


def weight_grads(jobs, code, index, every, length, panel_rows, sizes, thread=(), after=(), through=(), partial=None, plain=False):
    clips = len(every)
    any_spec = pl.BlockSpec(memory_space=pltpu.HBM)
    operands, scratch = [code, index], []
    for left, right, _ in jobs:
        for name in (left, right):
            arrays = [every[c][name] for c in range(clips)]
            operands += arrays
            scratch.append(pltpu.VMEM((clips * length, arrays[0].shape[1]), bf16))
    aliases = {}
    for n, array in enumerate(thread):
        aliases[len(operands)] = len(sizes) - len(thread) + n
        operands.append(array)
    passed = [pltpu.HBM(a.shape, a.dtype) for a in through]
    for n, array in enumerate(through):
        aliases[len(operands)] = len(sizes) + n
        operands.append(array)
    operands += after
    if partial is not None:
        operands.append(partial)
    others = len(operands) - 2 - 2 * len(jobs) * clips
    width = sum(s.shape[1] for s in scratch[0::2])
    return pl.pallas_call(
        functools.partial(
            grads_kernel, jobs, clips, length, panel_rows, plain, partial is not None, len(sizes), len(passed), others
        ),
        out_shape=[pltpu.HBM((size, panel_rows, D), bf16) for size in sizes] + passed,
        in_specs=[pl.BlockSpec(memory_space=pltpu.SMEM)] * 2 + [any_spec] * (len(operands) - 2),
        out_specs=[any_spec] * (len(sizes) + len(passed)),
        scratch_shapes=scratch
        + [
            pltpu.VMEM((2, D // panel_rows, panel_rows, D), bf16),
            pltpu.VMEM((4 if partial is not None else 1, D // panel_rows, panel_rows, D), bf16),
            pltpu.SemaphoreType.DMA((width // D + len(jobs), clips)),
            pltpu.SemaphoreType.DMA((4,)),
            pltpu.SemaphoreType.DMA((2,)),
        ],
        input_output_aliases=aliases,
        compiler_params=pltpu.CompilerParams(vmem_limit_bytes=26 * 1024 * 1024 if plain else VMEM_ALL),
        cost_estimate=pl.CostEstimate(
            flops=4 * clips * length * width * D, bytes_accessed=12 << 20, transcendentals=0
        ),
        name=f"grads_{jobs[0][2]}_{plain:d}",
    )(*operands[:2], *in_hbm(operands[2:]))


def adam_kernel(low, high, n_sums, chained, code_ref, index_ref, row_ref, master, first, second, dmod, cond, *refs):
    sums = refs[:n_sums]
    refs = refs[n_sums + (4 if chained else 0) :]
    outs, held, made = refs[:4], refs[4:7], refs[7:11]
    grad_v, in_sem, grad_sem, out_sem = refs[11:]
    slots, rows = master.shape[0], master.shape[1]
    sources = (master, first, second)

    def each(step):
        @pl.loop(0, slots)
        def _(slot):
            code = code_ref[slot]

            @pl.when((code >= low) & (code < high))
            def _():
                step(slot, code)

    def fetch(slot, code):
        for source, target in zip(sources, held):
            pltpu.make_async_copy(source.at[slot], target.at[slot], in_sem.at[slot]).start()
        for n in range(max(low, 2), min(high, n_sums + 2)):

            @pl.when(code == n)
            def _():
                pltpu.make_async_copy(sums[n - 2].at[index_ref[slot]], grad_v.at[slot], grad_sem.at[slot]).start()

    def work(slot, code):
        for source, target in zip(sources, held):
            pltpu.make_async_copy(source.at[slot], target.at[slot], in_sem.at[slot]).wait()

        def update(grad):
            first_next = beta_one * held[1][slot] + (1.0 - beta_one) * grad
            second_next = beta_two * held[2][slot] + (1.0 - beta_two) * grad * grad
            first_hat = first_next / (1.0 - beta_one**STEP)
            second_hat = second_next / (1.0 - beta_two**STEP)
            value = held[0][slot] - learn_rate * (
                first_hat / (jnp.sqrt(second_hat) + adam_eps) + decay_rate * held[0][slot]
            )
            made[0][slot] = value
            made[1][slot] = first_next
            made[2][slot] = second_next
            made[3][slot] = value.astype(bf16)

        if high > 2:

            @pl.when(code >= 2)
            def _():
                pltpu.make_async_copy(sums[0].at[0], grad_v.at[slot], grad_sem.at[slot]).wait()
                update(grad_v[slot].astype(f32))

        if low < 2:

            @pl.when(code == 1)
            def _():
                at = pl.multiple_of(row_ref[slot], rows)
                update(dot_nn(dmod[pl.ds(at, rows), :], cond[...]))

            @pl.when(code == 0)
            def _():
                update(jnp.zeros((rows, D), f32))

        for source, target in zip(made, outs):
            pltpu.make_async_copy(source.at[slot], target.at[slot], out_sem.at[slot]).start()

    def close(slot, code):
        for source, target in zip(made, outs):
            pltpu.make_async_copy(source.at[slot], target.at[slot], out_sem.at[slot]).wait()

    each(fetch)
    each(work)
    each(close)


def adam(low, high, code, index, row, master, first, second, dmod, cond, sums, chain):
    slots, rows = master.shape[0], master.shape[1]
    any_spec = pl.BlockSpec(memory_space=pltpu.HBM)
    smem, vmem = pl.BlockSpec(memory_space=pltpu.SMEM), pl.BlockSpec(memory_space=pltpu.VMEM)
    kinds = [f32, f32, f32, bf16]
    return pl.pallas_call(
        functools.partial(adam_kernel, low, high, len(sums), bool(chain)),
        in_specs=[smem] * 3 + [any_spec] * 3 + [vmem] * 2 + [any_spec] * (len(sums) + len(chain)),
        out_specs=[any_spec] * 4,
        out_shape=[pltpu.HBM(master.shape, kind) for kind in kinds],
        scratch_shapes=[pltpu.VMEM(master.shape, f32)] * 3
        + [pltpu.VMEM(master.shape, kind) for kind in kinds]
        + [pltpu.VMEM(master.shape, bf16)]
        + [pltpu.SemaphoreType.DMA((slots,))] * 3,
        input_output_aliases={8 + len(sums) + n: n for n in range(len(chain))},
        compiler_params=pltpu.CompilerParams(vmem_limit_bytes=VMEM_ALL),
        cost_estimate=pl.CostEstimate(flops=0, bytes_accessed=slots * rows * D * 15, transcendentals=0),
        name=f"adam_{low}",
    )(code, index, row, *in_hbm((master, first, second)), dmod, cond, *in_hbm(list(sums) + list(chain)))


CHIPS = 8
LOOP = (0, 2, 4, 6, 7, 5, 3, 1)


def swap_cores(value):
    return lax.ppermute(value, BATCH, [(d, d ^ 1) for d in range(2 * CHIPS)])


def along(value, step):
    pairs = [
        (2 * LOOP[n] + core, 2 * LOOP[(n + step) % CHIPS] + core) for n in range(CHIPS) for core in range(2)
    ]
    return lax.ppermute(value, BATCH, pairs)


def hop_kernel(spans, adds, others, spot_ref, *refs):
    n_in = 2 + len(adds)
    terms, came, refs = refs[:2], refs[2:n_in], refs[n_in + others :]
    outs = refs[: len(spans)]
    held, sem, out_sem = refs[len(spans) : -2], refs[-2], refs[-1]
    get, at = [], 0
    parts = []
    for n, (low, high) in enumerate(spans):
        rows = []
        for source in terms:
            span = pl.ds(spot_ref[n] + low, high - low)
            get.append(start(source.at[span], held[at], sem.at[at]))
            rows.append(at)
            at += 1
        parts.append(rows)
    for n, source in enumerate(came):
        get.append(start(source, held[at], sem.at[at]))
        at += 1
    for copy in get:
        copy.wait()
    put = []
    for n, (low, high) in enumerate(spans):
        made = held[at + n]
        mine = [(m, first, last, skip) for m, (target, first, last, skip) in enumerate(adds) if target == n]
        cuts = sorted({low, high} | {min(max(c, low), high) for _, first, last, _ in mine for c in (first, last)})
        for begin, end in zip(cuts, cuts[1:]):
            inside = [(m, skip) for m, first, last, skip in mine if first <= begin and end <= last]

            @pl.loop(begin - low, end - low)
            def _(r):
                total = held[parts[n][0]][r].astype(f32) + held[parts[n][1]][r].astype(f32)
                for m, skip in inside:
                    total = total + held[2 * len(spans) + m][r + (low - skip)].astype(f32)
                made[r] = total.astype(bf16)

        put.append(start(made, outs[n], out_sem.at[n]))
    for copy in put:
        copy.wait()


def hop_sums(spots, terms, spans, adds, came, after):
    rows, width = terms[0].shape[1:]
    shapes = [(high - low, rows, width) for low, high in spans]
    scratch = [pltpu.VMEM(shape, bf16) for shape in shapes for _ in range(2)]
    scratch += [pltpu.VMEM(array.shape, bf16) for array in came] + [pltpu.VMEM(shape, bf16) for shape in shapes]
    return pl.pallas_call(
        functools.partial(hop_kernel, spans, adds, len(after)),
        in_specs=[pl.BlockSpec(memory_space=pltpu.SMEM)]
        + [pl.BlockSpec(memory_space=pltpu.HBM)] * 2
        + [pl.BlockSpec(memory_space=pl.ANY)] * (len(came) + len(after)),
        out_specs=[pl.BlockSpec(memory_space=pltpu.HBM)] * len(spans),
        out_shape=[pltpu.HBM(shape, bf16) for shape in shapes],
        scratch_shapes=scratch + [pltpu.SemaphoreType.DMA((8,)), pltpu.SemaphoreType.DMA((2,))],
        compiler_params=pltpu.CompilerParams(vmem_limit_bytes=VMEM_ALL),
        cost_estimate=pl.CostEstimate(flops=0, bytes_accessed=8 * shapes[0][0] * rows * width * 2, transcendentals=0),
        name="hop",
    )(spots, *in_hbm(terms), *came, *after)


class Ring:
    def __init__(self, place, mine, other):
        self.place, self.size, self.left = place, mine.shape[0] // CHIPS, 4
        self.half = self.size // 2
        self.terms = (mine, swap_cores(other))

    def hop(self, after=()):
        n, half, size = self.left, self.half, self.size
        spots = jnp.stack([(self.place + n) % CHIPS, (self.place - n) % CHIPS]) * size
        if n == 4:
            spans, adds, came = [(0, half), (half, size)], [], []
        else:
            spans, came = [(0, size)] * 2, [self.ahead, self.behind]
            adds = [(0, 0, half, 0), (1, half, size, half)] if n == 3 else [(0, 0, size, 0), (1, 0, size, 0)]
        ahead, behind = hop_sums(spots.astype(jnp.int32), self.terms, spans, adds, came, after)
        self.sent = [ahead, behind]
        self.ahead, self.behind = along(ahead, 1), along(behind, -1)
        self.left -= 1

    def held(self, count=2):
        self.count = count
        return list(self.terms[:count])

    def later(self, made):
        self.terms = tuple(made[-self.count :]) + self.terms[self.count :]
        return made[: -self.count]

    def finish(self, after=()):
        spots = jnp.reshape(self.place * self.size, (1,)).astype(jnp.int32)
        adds = [(0, 0, self.size, 0)] * 2
        return hop_sums(spots, self.terms, [(0, self.size)], adds, [self.ahead, self.behind], after)[0]


def time_features(steps_in):
    half_width = D // 2
    freqs = jnp.exp(-math.log(10000.0) * jnp.arange(half_width, dtype=f32) / half_width)
    angles = steps_in.astype(f32)[:, None] * freqs[None, :]
    return jnp.concatenate([jnp.cos(angles), jnp.sin(angles)], axis=1)


def body(tokens, cotangent, loss_weight, timesteps, owners, master, first_moment, second_moment):
    section_index = lax.axis_index(SECTION)
    me = lax.axis_index(BATCH)
    owner_total = lax.axis_size(BATCH)
    slots, panel_rows = master.shape[1], master.shape[2]
    clips = timesteps.shape[0]
    length = tokens.shape[0] // clips
    low = master[0].astype(bf16)
    owner = owners[0] + (0.0 * low[0, 0, 0].astype(f32)).astype(jnp.int32)
    panels = owner.shape[0]
    moved = DOWN_END // panel_rows
    cap = min(slots, max(4, (slots * 25 + 30) // 31))
    section = jnp.reshape(section_index, (1,)).astype(jnp.int32)

    number = jnp.arange(panels, dtype=jnp.int32)
    same = (owner[:, None] == owner[None, :]) & (number[None, :] < number[:, None])
    rank = jnp.sum(same.astype(jnp.int32), axis=1)
    first_size = owner_total * cap
    place = jnp.where(
        rank < cap, owner * cap + rank, first_size + owner * (slots - cap) + rank - cap
    )[:moved]
    mine = (owner[None, :] == me) & (
        rank[None, :] == jnp.arange(slots, dtype=jnp.int32)[:, None]
    )
    slot_panel = jnp.sum(jnp.where(mine, number[None, :] + 1, 0), axis=1) - 1
    kind = jnp.where(slot_panel < 0, 0, jnp.where(slot_panel < moved, 1, 2)).astype(jnp.int32)
    grad_row = jnp.where(kind == 2, (slot_panel - moved) * panel_rows, 0).astype(jnp.int32)

    rings = owner_total == 2 * CHIPS
    code, index, slot_code, slot_index, sizes, beyond = routes(owner, rank, mine, me, owner_total, slots, moved)
    gathered = lax.all_gather(low[:cap], BATCH, axis=0, tiled=True)
    spot = jnp.arange(owner_total * clips, dtype=jnp.int32) // clips == me
    news = [jnp.where(spot, jnp.tile(timesteps.astype(f32), owner_total), 0.0)]
    past = jnp.max(jnp.where(number < moved, rank, 0)) >= cap
    news.append(jnp.stack([past, beyond]).astype(f32) + 0.0 * low[0, 0, 0].astype(f32))
    news = lax.pmax(jnp.concatenate(news), (SECTION, BATCH))
    all_steps = news[:-2]
    beyond = news[-1] > 0.5
    sources = [gathered]
    if cap < slots:
        rest_shape = (owner_total * (slots - cap), panel_rows, D)
        sources.append(
            lax.cond(
                news[-2] + 0.0 * gathered[0, 0, 0].astype(f32) > 0.5,
                lambda part: lax.all_gather(part, BATCH, axis=0, tiled=True),
                lambda part: jnp.zeros(rest_shape, bf16),
                low[cap:],
            )
        )
    sheet = assemble(place, sources, moved)

    cond = jax.nn.silu(time_features(all_steps)).astype(bf16)
    clip_total = cond.shape[0]
    share = jnp.einsum("cd,sd->cs", cond, low.reshape(slots * panel_rows, D), preferred_element_type=f32)
    share = lax.all_to_all(
        share.reshape(owner_total, clips, slots * panel_rows), BATCH, split_axis=0, concat_axis=0, tiled=True
    )
    share = share.reshape(owner_total, clips, slots, panel_rows).transpose(1, 0, 2, 3)
    share = share.reshape(clips, owner_total * slots, panel_rows)
    pick = (
        (owner * slots + rank)[moved:, None] == jnp.arange(owner_total * slots, dtype=jnp.int32)[None, :]
    ).astype(f32)
    mod = jnp.einsum("ps,csr->cpr", pick, share, precision=lax.Precision.HIGHEST)
    mod = mod.reshape(clips, 6, D)

    run = functools.partial
    base = dict(clips=clips, length=length, section=section, mod=mod, sheet=sheet)
    firsts, outs = [], None
    for c in range(clips):
        firsts.append(first_forward(c, x=tokens, outs=outs, **base))
        outs = firsts[c][N_OUTS]
    received = [lax.ppermute(f[N_SENT], SECTION, [(0, 1)]) for f in firsts]
    seconds, gin = [], None
    for c in range(clips):
        chain = {n: firsts[c][n] for n in (N_H1, N_O, N_H2, N_Z)} | {N_OUTS: outs, N_GIN: gin}
        seconds.append(second_both(c, loss_weight=loss_weight, x=received[c], g=cotangent, chain=chain, **base))
        outs, gin = seconds[c][N_OUTS], seconds[c][N_GIN]
    received = [lax.ppermute(f[N_SENT], SECTION, [(1, 0)]) for f in seconds]
    every = [dict(f) for f in seconds]

    all_jobs = ((N_Z, N_DB, UP_END), (N_DU, N_H2, PROJ_END), (N_DA, N_O, QKV_END), (N_DQKV, N_H1, 0))
    grads = run(weight_grads, code=code, index=index, length=length, panel_rows=panel_rows)
    partial, after = None, mod
    for c in range(clips):
        chain = {n: every[c][n] for n in BACK_MAKES} | {N_GIN: gin}
        every[c] |= first_back(c, x=tokens, g=received[c], kept=firsts[c], chain=chain, after=after, **base)
        gin, after = every[c][N_GIN], every[c][N_DMOD_ATT]
        if rings and c == clips - 2:
            (partial,) = grads(all_jobs, every=every[:-1], sizes=[moved], plain=True)
            after = partial

    dmod = [jnp.concatenate([e[N_DMOD_ATT], e[N_DMOD_FFN]]) for e in every]
    dmod = jnp.stack(dmod).reshape(1, clips, 6 * D).astype(bf16)
    dmod = lax.all_to_all(
        jnp.broadcast_to(dmod, (owner_total, clips, 6 * D)), BATCH, split_axis=0, concat_axis=0, tiled=True
    )
    slot_code = jnp.where(kind == 1, slot_code + 2, jnp.where(kind == 2, 1, 0)).astype(jnp.int32)
    update = run(
        adam, code=slot_code, index=slot_index, row=grad_row, master=master[0], first=first_moment[0],
        second=second_moment[0], dmod=dmod.reshape(clip_total, 6 * D).T, cond=cond,
    )
    if rings:
        place = me // 4 + (me // 2) % 2 * (CHIPS - 1 - 2 * (me // 4))
        wide = [sizes[1]] * 2 + [sizes[2]]
        first_jobs = ((N_DA, N_O, QKV_END), (N_DQKV, N_H1, 0), (N_DU, N_H2, PROJ_END))
        now = every[-1:] if partial is not None else every
        made = grads(first_jobs, every=now, sizes=[sizes[0]] * 2 + wide, partial=partial)
        first = Ring(place, *made[:2])
        made = grads(
            ((N_Z, N_DB, UP_END),), every=now, sizes=wide, thread=made[2:], through=first.held(1), partial=partial
        )
        made = first.later(made)
        second = Ring(place, *made[:2])
        rest = lax.cond(
            beyond,
            lambda part: lax.psum_scatter(part, BATCH, scatter_dimension=0, tiled=True),
            lambda part: jnp.zeros((slots, panel_rows, D), bf16),
            made[2],
        )
        first.hop()
        second.hop()
        first.hop(after=[rest, second.ahead, second.behind])
        second.hop()
        first.hop()
        second.hop()
        first.hop(after=[dmod])
        results = update(0, 2, sums=[], chain=[])
        second.hop(after=results[3:])
        half = first.finish()
        sums = [half, swap_cores(half)]
        results = update(2, 4, sums=sums, chain=results)
        half = second.finish(after=results[3:])
        sums += [half, swap_cores(half), rest]
        results = update(4, 7, sums=sums, chain=results)
    else:
        (made,) = grads(all_jobs, every=every, sizes=[sizes[0]])
        sums = [lax.psum_scatter(made, BATCH, scatter_dimension=0, tiled=True)]
        results = update(0, 3, sums=sums, chain=[])
    return (outs[None], gin[None], *(r[None] for r in results))


CAPS = (24, 24)


def count_before(flag, group):
    number = jnp.arange(group.shape[0], dtype=jnp.int32)
    before = (group[:, None] == group[None, :]) & (number[None, :] < number[:, None]) & flag[None, :]
    return jnp.sum(before.astype(jnp.int32), axis=1)


def routes(owner, rank, mine, me, owner_total, slots, moved):
    if owner_total != 2 * CHIPS:
        code = jnp.zeros((moved,), jnp.int32)
        return code, (owner * slots + rank)[:moved], jnp.zeros((slots,), jnp.int32), jnp.arange(slots, dtype=jnp.int32), [owner_total * slots], jnp.bool_(False)
    number = jnp.arange(moved, dtype=jnp.int32)
    held, core = owner[:moved], me % 2
    chip = held // 2
    spot = chip // 2 + chip % 2 * (CHIPS - 1 - 2 * (chip // 2))
    per_row = DOWN_END // moved
    down = number >= UP_END // per_row
    order = count_before(~down, chip)
    late = down | (order >= CAPS[0])
    order = jnp.where(late, count_before(late, chip), order)
    rest = late & (order >= CAPS[1])
    half = order % 2
    size = jnp.where(late, CAPS[1] // 2, CAPS[0] // 2)
    index = jnp.where(rest, held * slots + rank[:moved], spot * size + order // 2)
    away = (half != core).astype(jnp.int32)
    code = jnp.where(rest, 4, jnp.where(late, 2 + away, away))
    code = jnp.where(down, code - 2, code).astype(jnp.int32)
    taken = mine[:, :moved].astype(jnp.int32)
    found = jnp.where(rest, 4, 2 * late.astype(jnp.int32) + away)
    slot_code = jnp.sum(taken * found[None, :], axis=1)
    slot_index = jnp.sum(taken * jnp.where(rest, rank[:moved], order // 2)[None, :], axis=1)
    sizes = [CHIPS * cap // 2 for cap in CAPS] + [owner_total * slots]
    return code, index.astype(jnp.int32), slot_code.astype(jnp.int32), slot_index.astype(jnp.int32), sizes, jnp.any(rest)


def solution(mesh):
    placed = (
        P(BATCH, None),
        P(BATCH, None),
        P(BATCH),
        P(BATCH),
        P(SECTION, None),
        P(SECTION, BATCH, None, None),
        P(SECTION, BATCH, None, None),
        P(SECTION, BATCH, None, None),
    )
    return jax.shard_map(
        body,
        mesh=mesh,
        in_specs=placed,
        out_specs=(
            P(SECTION, BATCH, None),
            P(SECTION, BATCH, None),
            P(SECTION, BATCH, None, None),
            P(SECTION, BATCH, None, None),
            P(SECTION, BATCH, None, None),
            P(SECTION, BATCH, None, None),
        ),
        check_vma=False,
    )
```
